256 devices in a mesh: section: 2 (over core), seq: 32 (over y, z), mp: 4 (over x).
Axes of the slice: x: 4, y: 4, z: 8, core: 2. Of those that a mesh axis runs over, the one named last changes fastest.
Arguments:
- queries: bfloat16 [8192, 3072], P(('section', 'seq'), 'mp'), may hold values from -5 to 5
- keys: bfloat16 [8192, 3072], P(('section', 'seq'), 'mp'), may hold values from -5 to 5
- values: bfloat16 [8192, 3072], P(('section', 'seq'), 'mp'), may hold values from -6 to 6
- residual: bfloat16 [8192, 3072], P(('section', 'seq'), 'mp'), may hold values from -6 to 6
- segment_ids: int32 [2, 4096], P('section'), may hold values from 0 to 15, never falling along the last dimension, each value on 1 to 2048 neighbouring positions
- enc_counts: int32 [2, 32], P('section'), may hold values from 1 to 256, 4096 in all within a row
- enc_hidden: bfloat16 [16384, 4096], P(('section', 'seq'), 'mp'), may hold values from -6 to 6
- enc_down: bfloat16 [4096, 1536], P('mp'), may hold values from -0.09375 to 0.09375
- enc_resid: bfloat16 [16384, 1536], P(('section', 'seq'), 'mp'), may hold values from -6 to 6
- layer_scale: float32 [1536], replicated, may hold values from 0.2 to 2
- norm_gain: float32 [1536], replicated, may hold values from 0.25 to 1.75
- norm_bias: float32 [1536], replicated, may hold values from -3 to 3
- proj_in: bfloat16 [3072, 2048], P('mp'), may hold values from -0.109375 to 0.109375
- proj_out: bfloat16 [2048, 1536], P(None, 'mp'), may hold values from -0.125 to 0.125
- align_weight: float32 [8192], P(('section', 'seq')), may hold values from 2 to 20
Outputs:
- aligned: float32 [8192], P(('section', 'seq'))
- grad_in_t: float32 [2048, 3072], P(('section', 'seq'), 'mp')
- grad_out: float32 [2048, 1536], P(('section', 'seq'), 'mp')
The draws below stay inside these ranges and needn't reach their ends.
Inputs may be any that keep to these rules, and one draw needn't show every extreme that they name: `enc_counts`: in each micro-batch the counts sum to 4096; some device holds exactly 256 valid rows. Rows of an encoder device beyond its count are padding. `segment_ids`: each image covers consecutive positions, ids never fall along a micro-batch.
All inputs are finite; a program needn't handle non-finite values.
Results may differ from the reference program's by a relative error of at most 0.025.
Values may be sent and summed in bfloat16 or wider, within the bound.
A program may use at most 128 MiB of HBM per device.

```python
import math
import jax
import jax.numpy as jnp
import numpy as np
from jax import lax

D = 3072
HEADS = 24
HD = 128
ENC_D = 1536
ENC_FF = 4096
PROJ = 2048
T_DEV = 128
ENC_CAP = 256
SEQ_LEN = 4096
TOKENS = 8192
ENC_ROWS = 16384
IMAGES = 16
IMG_MOST = 2048
N_SECTION = 2
N_SEQ = 32


def draw_queries(key, part):
    own_key = jax.random.fold_in(key, 11)
    result = jnp.clip(jax.random.normal(own_key, (TOKENS, D)), -5.0, 5.0)
    return result.astype(jnp.bfloat16)


def draw_keys(key, part):
    own_key = jax.random.fold_in(key, 13)
    result = jnp.clip(jax.random.normal(own_key, (TOKENS, D)), -5.0, 5.0)
    return result.astype(jnp.bfloat16)


def block_levels(key, dims, pieces, least, high):
    loudness = 1.0
    for dim, blocks in pieces:
        steps = jax.random.uniform(jax.random.fold_in(jax.random.fold_in(key, 6), dim), (blocks,), jnp.float32, least / len(pieces), high / len(pieces))
        loudness = loudness * jnp.repeat(jnp.exp(steps), dims[dim] // blocks).reshape((-1,) + (1,) * (len(dims) - 1 - dim))
    return loudness


def length_profile(amount, total, bound, slope):
    portions = [(1 << 20) // math.isqrt(rank ** slope) + 1 for rank in range(2, amount + 1)]
    rest, holding = total - bound - (amount - 1), [1] * (amount - 1)
    while rest > 0:
        free = [i for i in range(amount - 1) if holding[i] < bound]
        whole, left = sum([portions[i] for i in free]), rest
        for i in free:
            extra = min(bound - holding[i], max(1, left * portions[i] // whole), rest)
            holding[i] = holding[i] + extra
            rest = rest - extra
    return np.array([bound] + holding)


def ragged_sizes(rng, count, total, bound, lean):
    if count == 2:
        one = jax.random.randint(rng, (), max(1, total - bound), min(bound, total - 1) + 1)
        return jnp.stack([one, total - one])
    tallies = jnp.asarray(length_profile(count, total, bound, lean), jnp.int32)
    couples = (count - 1) // 2
    source_of, receiver = tallies[1:1 + 2 * couples:2], tallies[2:2 + 2 * couples:2]
    slack = jnp.minimum(source_of - 1, bound - receiver)
    moved = jax.random.randint(jax.random.fold_in(rng, 1), (couples,), 0, 1 << 20) % (slack + 1)
    tallies = tallies.at[1:1 + 2 * couples:2].set(source_of - moved).at[2:2 + 2 * couples:2].set(receiver + moved)
    return tallies[jax.random.permutation(jax.random.fold_in(rng, 2), count)]


def gaussian(key, shape, scale, reach, shards=(), kind=jnp.bfloat16):
    gain = block_levels(key, shape, shards, -0.22, 0.18) if shards else 1.0
    array = jax.random.normal(key, shape, jnp.float32) * scale * gain
    return jnp.minimum(jnp.maximum(array, -reach), reach).astype(kind)


def setup_inputs(seed: int = 0) -> dict:
    key_of = jax.random.split(jax.random.key(seed), 16)
    return {
        "queries": draw_queries(jax.random.fold_in(key_of[15], 71), 0),
        "keys": draw_keys(jax.random.fold_in(key_of[15], 71), 0),
        "values": gaussian(key_of[2], (TOKENS, D), 1.0, 6.0, ((0, 64), (1, 4))),
        "residual": gaussian(key_of[3], (TOKENS, D), 1.0, 6.0, ((0, 64), (1, 4))),
        "segment_ids": jax.vmap(lambda own: jnp.searchsorted(jnp.cumsum(ragged_sizes(own, IMAGES, SEQ_LEN, IMG_MOST, 2)), jnp.arange(SEQ_LEN), side="right"))(jax.random.split(key_of[4], N_SECTION)).reshape((N_SECTION, SEQ_LEN)).astype(jnp.int32),
        "enc_counts": jax.vmap(lambda own: ragged_sizes(own, N_SEQ, SEQ_LEN, ENC_CAP, 2))(jax.random.split(key_of[5], N_SECTION)).reshape((N_SECTION, N_SEQ)).astype(jnp.int32),
        "enc_hidden": gaussian(key_of[6], (ENC_ROWS, ENC_FF), 1.0, 6.0, ((0, 64), (1, 4))),
        "enc_down": gaussian(key_of[7], (ENC_FF, ENC_D), ENC_FF ** -0.5, 0.09375, ((0, 4),)),
        "enc_resid": gaussian(key_of[8], (ENC_ROWS, ENC_D), 1.0, 6.0, ((0, 64), (1, 4))),
        "layer_scale": jnp.clip(jnp.exp(jax.random.uniform(key_of[9], (ENC_D,), jnp.float32, math.log(0.2), math.log(2.0))), 0.2, 2.0),
        "norm_gain": jnp.clip(1.0 + 0.15 * jax.random.normal(key_of[10], (ENC_D,), jnp.float32), 0.25, 1.75),
        "norm_bias": gaussian(key_of[11], (ENC_D,), 0.5, 3.0, (), jnp.float32),
        "proj_in": gaussian(key_of[12], (D, PROJ), D ** -0.5, 0.109375, ((0, 4),)),
        "proj_out": gaussian(key_of[13], (PROJ, ENC_D), PROJ ** -0.5, 0.125, ((1, 4),)),
        "align_weight": jnp.clip(jnp.exp(math.log(20.0) - 2.3025851 * jax.random.uniform(key_of[14], (TOKENS,), jnp.float32) ** block_levels(key_of[14], (TOKENS,), ((0, 64),), -0.2, 0.2)), 2.0, 20.0),
    }


def attention_block(q_rows, k_rows, v_rows, seg_rows):
    length = q_rows.shape[0]
    allowed = seg_rows[:, None] == seg_rows[None, :]
    q_heads = q_rows.reshape(length, HEADS, HD).transpose(1, 0, 2)
    k_heads = k_rows.reshape(length, HEADS, HD).transpose(1, 0, 2)
    v_heads = v_rows.reshape(length, HEADS, HD).transpose(1, 0, 2)

    def one_head(operands):
        q_head, k_head, v_head = operands
        scores = jnp.dot(q_head, k_head.T, preferred_element_type=jnp.float32) * HD ** (-0.5)
        scores = jnp.where(allowed, scores, -1e+30)
        best = lax.optimization_barrier(jnp.max(scores, axis=-1))
        weights = jnp.where(allowed, jnp.exp(scores - best[:, None]), 0.0)
        total = lax.optimization_barrier(jnp.sum(weights, axis=-1))
        mixed = jnp.dot(weights.astype(jnp.bfloat16), v_head, preferred_element_type=jnp.float32)
        return mixed / total[:, None]
    outputs = lax.map(one_head, (q_heads, k_heads, v_heads))
    return outputs.transpose(1, 0, 2).reshape(length, HEADS * HD).astype(jnp.bfloat16)

def reference(queries, keys, values, residual, segment_ids, enc_counts, enc_hidden, enc_down, enc_resid, layer_scale, norm_gain, norm_bias, proj_in, proj_out, align_weight):
    hidden_parts = []
    target_parts = []
    row_ids = jnp.arange(SEQ_LEN, dtype=jnp.int32)
    positions = row_ids % T_DEV * N_SEQ + row_ids // T_DEV
    for section_id in range(N_SECTION):
        low = section_id * SEQ_LEN
        seg_rows = segment_ids[section_id].reshape(T_DEV, N_SEQ).T.reshape(-1)
        attn = attention_block(queries[low:low + SEQ_LEN], keys[low:low + SEQ_LEN], values[low:low + SEQ_LEN], seg_rows)
        attn = lax.optimization_barrier(attn)
        hidden = (residual[low:low + SEQ_LEN].astype(jnp.float32) + attn.astype(jnp.float32)).astype(jnp.bfloat16)
        hidden_parts.append(hidden)
        enc_low = section_id * N_SEQ * ENC_CAP
        enc_block = enc_hidden[enc_low:enc_low + N_SEQ * ENC_CAP]
        enc = enc_resid[enc_low:enc_low + N_SEQ * ENC_CAP].astype(jnp.float32) + layer_scale[None, :] * jnp.dot(enc_block, enc_down, preferred_element_type=jnp.float32)
        mean = lax.optimization_barrier(jnp.mean(enc, axis=1))
        meansq = lax.optimization_barrier(jnp.mean(enc * enc, axis=1))
        variance = meansq - mean * mean
        feature = ((enc - mean[:, None]) * lax.rsqrt(variance + 1e-06)[:, None] * norm_gain[None, :] + norm_bias[None, :]).astype(jnp.bfloat16)
        counts = enc_counts[section_id].astype(jnp.int32)
        offsets = (jnp.cumsum(counts) - counts).astype(jnp.int32)
        source = (lax.optimization_barrier(jnp.sum((offsets[None, :] <= positions[:, None]).astype(jnp.int32), axis=1)) - 1).astype(jnp.int32)
        index = (source * ENC_CAP + positions - offsets[source]).astype(jnp.int32)
        target_parts.append(feature[index])
    hidden = jnp.concatenate(hidden_parts, axis=0)
    target = jnp.concatenate(target_parts, axis=0)
    first = jnp.dot(hidden, proj_in, preferred_element_type=jnp.float32)
    act = jax.nn.silu(first).astype(jnp.bfloat16)
    second = jnp.dot(act, proj_out, preferred_element_type=jnp.float32)
    target_f = target.astype(jnp.float32)
    inner = lax.optimization_barrier(jnp.sum(second * target_f, axis=1))
    norm_z = jnp.sqrt(lax.optimization_barrier(jnp.sum(second * second, axis=1)) + 1e-06)
    norm_f = jnp.sqrt(lax.optimization_barrier(jnp.sum(target_f * target_f, axis=1)) + 1e-06)
    aligned = inner / (norm_z * norm_f)
    back = (-align_weight[:, None] * (target_f / (norm_z * norm_f)[:, None] - (aligned / (norm_z * norm_z))[:, None] * second)).astype(jnp.bfloat16)
    grad_out = jnp.dot(act.T, back, preferred_element_type=jnp.float32)
    upstream = jnp.dot(back, proj_out.T, preferred_element_type=jnp.float32)
    sig = jax.nn.sigmoid(first)
    dfirst = (upstream * sig * (1.0 + first * (1.0 - sig))).astype(jnp.bfloat16)
    grad_in_t = jnp.dot(dfirst.T, hidden, preferred_element_type=jnp.float32)
    return (aligned, grad_in_t, grad_out)
```

```python
import math

import jax
import jax.numpy as jnp
from jax import lax
from jax.experimental import pallas as pl
from jax.experimental.pallas import tpu as pltpu
from jax.sharding import PartitionSpec as P

MESH = pl.DeviceIdType.MESH
F32, BF16, I32 = jnp.float32, jnp.bfloat16, jnp.int32
HD = 128
ENC_D = 1536
NX, NY, NZ = 4, 4, 8
NSEQ = NY * NZ
ROWS = 128
CAP = 256
WIDTH = 768
HEADS = 6
HALF = 384
CH = 384
FF = 1024
PROJ = 2048
PART = 512
SAME = 8192.0
EXP_SCALE = math.log2(math.e) * HD ** (-0.5)


def rcopy(src, dst, send, recv, dev):
    return pltpu.make_async_remote_copy(
        src_ref=src, dst_ref=dst, send_sem=send, recv_sem=recv, device_id=dev, device_id_type=MESH
    )


def iota(shape, dim):
    return lax.broadcasted_iota(I32, shape, dim)


def dot(a, b, ca=1, cb=0):
    return lax.dot_general(a, b, (((ca,), (cb,)), ((), ())), preferred_element_type=F32)


def kernel(
    q_hbm, k_hbm, v_hbm, res_hbm, seg_ref, cnt_ref, eh_hbm, ed_hbm, er_hbm, ls_ref, gain_ref, bias_ref,
    pin_hbm, pout_hbm, aw_ref,
    al_ref, gi_ref, go_ref,
    qbuf, kbuf, vbuf, vt, ko, resv, ehv, edv, erv, pin, pout,
    opart, stats, oin, sin,
    esend, erecv, share, estat, estat_in, packed, arecv, target,
    hidden, fsend, frecv, first, actbuf, second, sstat, sstat_in, back, dbuf, segrow,
    go_x, go_xr, go_h, go_yr, go_z, go_zr,
    gi_x, gi_xr, gi_h, gi_yr, gi_z, gi_zr,
    lsem, q_s, q_r, kv_s, kv_r, o_s, o_r, os_s, os_r, x_s, x_r, a_s, a_r,
    gx_s, gx_r, gy_s, gy_r, gz_s, gz_r,
):
    sec = lax.axis_index("section")
    seq = lax.axis_index("seq")
    x = lax.axis_index("mp")
    y = seq // NZ
    z = lax.rem(seq, NZ)
    zp = {"seq": y * NZ + lax.rem(z + 1, NZ)}
    zm = {"seq": y * NZ + lax.rem(z + NZ - 1, NZ)}
    yp = {"seq": lax.rem(y + 1, NY) * NZ + z}
    ym = {"seq": lax.rem(y + NY - 1, NY) * NZ + z}
    pending = []

    def go(copy):
        copy.start()
        pending.append(copy)
        return copy

    local = []
    for n, (src, dst) in enumerate((
        (q_hbm, qbuf.at[0]), (k_hbm, kbuf.at[0]), (v_hbm, vbuf.at[0]), (eh_hbm, ehv), (ed_hbm, edv),
        (er_hbm, erv), (res_hbm, resv), (pin_hbm, pin), (pout_hbm, pout),
    )):
        copy = pltpu.make_async_copy(src, dst, lsem.at[n])
        copy.start()
        local.append(copy)

    barrier = pltpu.get_barrier_semaphore()

    def greet(i, c):
        pl.semaphore_signal(barrier, inc=1, device_id={"seq": lax.rem(seq + i, NSEQ)}, device_id_type=MESH)
        return c

    lax.fori_loop(1, NSEQ, greet, 0)
    for r in range(1, NX):
        pl.semaphore_signal(barrier, inc=1, device_id={"mp": lax.rem(x + r, NX)}, device_id_type=MESH)
    pl.semaphore_signal(barrier, inc=1, device_id={"section": 1 - sec}, device_id_type=MESH)
    pl.semaphore_wait(barrier, NSEQ - 1 + NX - 1 + 1)

    def q_copy(d, t):
        slot = (8 - t) % 8 if d == 0 else t
        to = 7 - t if d == 0 else t + 1
        src, dst = qbuf.at[slot], qbuf.at[to]
        if t == 3:
            cols = pl.ds(d * HALF, HALF)
            src, dst = qbuf.at[slot, :, cols], qbuf.at[to, :, cols]
        return rcopy(src, dst, q_s.at[d, t], q_r.at[d, t], zp if d == 0 else zm)

    def kv_copy(n):
        src, dst, dev = (
            (kbuf.at[0], kbuf.at[3], yp), (kbuf.at[0], kbuf.at[1], ym),
            (vbuf.at[0], vbuf.at[3], yp), (vbuf.at[0], vbuf.at[1], ym),
            (kbuf.at[3], kbuf.at[2], yp), (vbuf.at[1], vbuf.at[2], ym),
        )[n]
        return rcopy(src, dst, kv_s.at[n], kv_r.at[n], dev)

    q_copies = [[q_copy(d, t) for t in range(4)] for d in range(2)]
    kv_copies = [kv_copy(n) for n in range(6)]
    local[0].wait()
    go(q_copies[0][0])
    go(q_copies[1][0])
    local[1].wait()
    go(kv_copies[0])
    go(kv_copies[1])
    local[2].wait()
    go(kv_copies[2])
    go(kv_copies[3])

    def x_copies(phase, src_of, dst_of):
        return {
            r: rcopy(src_of(r), dst_of(NX - r), x_s.at[phase, r - 1], x_r.at[phase, NX - r - 1],
                     {"mp": lax.rem(x + r, NX)})
            for r in (1, 2, 3)
        }

    local[3].wait()
    local[4].wait()
    enc_copies = x_copies(0, lambda r: esend.at[r], lambda r: erecv.at[r])
    for r in (2, 1, 3, 0):
        cols = pl.ds(pl.multiple_of(lax.rem(x + r, NX) * CH, CH), CH)
        esend[r] = dot(ehv[...], edv[:, cols]).astype(BF16)
        if r:
            go(enc_copies[r])

    ids = iota((16, NSEQ * ROWS), 0)
    seg = seg_ref[...]
    below = jnp.sum(jnp.where(seg < ids, 1.0, 0.0), axis=1, keepdims=True)
    upto = jnp.sum(jnp.where(seg <= ids, 1.0, 0.0), axis=1, keepdims=True)
    lane = iota((16, HD), 1)
    tail = jnp.full((HD - 16, HD), 1e9, F32)
    segrow[0] = jnp.concatenate([jnp.broadcast_to(below, lane.shape), tail], axis=0).T
    segrow[1] = jnp.concatenate([jnp.broadcast_to(upto, lane.shape), tail], axis=0).T

    def image_columns(device):
        place = (iota((ROWS, HD), 0) * NSEQ + device).astype(F32)
        return (place >= segrow[0]) & (place < segrow[1])

    for r in range(NY):
        device = lax.rem(y + r, NY) * NZ + z
        ko[r] = jnp.where(image_columns(device), SAME, 0.0).astype(BF16)

    def forward_q(t):
        for d in range(2):
            q_copies[d][t].wait_recv()
            if t < 3:
                go(q_copies[d][t + 1])

    forward_q(0)
    kv_copies[0].wait_recv()
    go(kv_copies[4])
    kv_copies[1].wait_recv()

    local[5].wait()
    own = pl.ds(pl.multiple_of(x * CH, CH), CH)
    for r in (1, 2, 3):
        enc_copies[NX - r].wait_recv()
    enc = esend[0].astype(F32)
    for r in (1, 2, 3):
        enc = enc + erecv[r].astype(F32)
    enc = erv[...].astype(F32) + ls_ref[:, own] * enc
    share[...] = enc
    lane = iota((CAP, HD), 1)
    total = jnp.sum(enc, axis=1, keepdims=True)
    square = jnp.sum(enc * enc, axis=1, keepdims=True)
    packed_stat = jnp.where(lane == 0, total, jnp.where(lane == 1, square, 0.0))
    for b in range(2):
        estat[:, b * HD:(b + 1) * HD] = packed_stat[b * HD:(b + 1) * HD].T[0:8]
    stat_copies = x_copies(1, lambda r: estat, lambda r: estat_in.at[r])
    for r in (2, 1, 3):
        go(stat_copies[r])

    kv_copies[2].wait_recv()
    kv_copies[3].wait_recv()
    go(kv_copies[5])
    forward_q(1)

    for r in (1, 2, 3):
        stat_copies[NX - r].wait_recv()
    both = estat[...]
    for r in (1, 2, 3):
        both = both + estat_in[r]
    mean = both[0:1] * (1.0 / ENC_D)
    scale = lax.rsqrt(both[1:2] * (1.0 / ENC_D) - mean * mean + 1e-6)
    pad = jnp.zeros((HD - 8, HD), F32)
    row8 = iota((8, HD), 0)
    gain = gain_ref[:, own]
    bias = bias_ref[:, own]
    parts = []
    for b in range(2):
        cut = slice(b * HD, (b + 1) * HD)
        rows = jnp.where(row8 == 0, mean[:, cut], jnp.where(row8 == 1, scale[:, cut], 0.0))
        cols = jnp.concatenate([rows, pad], axis=0).T
        parts.append((((share[cut] - cols[:, 0:1]) * cols[:, 1:2]) * gain + bias).astype(BF16))
    feature = jnp.concatenate(parts, axis=0)
    counts = cnt_ref[...].astype(F32)
    before = jnp.sum(jnp.where(iota((1, NSEQ), 1) < seq, counts, 0.0), axis=1, keepdims=True).astype(I32)
    row = iota((CAP, CAP), 0)
    wanted = (row & 7) * NSEQ + (((row >> 3) - before) & (NSEQ - 1))
    permutation = jnp.where(iota((CAP, CAP), 1) == wanted, 1.0, 0.0).astype(BF16)
    packed[...] = dot(permutation, feature).reshape(NSEQ, 8, CH)

    def row_copy(peer, mine):
        return rcopy(packed.at[peer], arecv.at[mine], a_s.at[peer], a_r.at[mine], {"seq": peer})

    def send_rows(i, c):
        row_copy(lax.rem(seq + i, NSEQ), seq).start()
        return c

    lax.fori_loop(1, NSEQ, send_rows, 0)
    arecv[pl.ds(seq, 1)] = packed[pl.ds(seq, 1)]

    for n in (4, 5):
        kv_copies[n].wait_recv()
    for r in range(NY):
        vt[:, r * ROWS:(r + 1) * ROWS] = vbuf[r].T
    keys_image = ko[...].reshape(NY * ROWS, HD)

    def attend(r):
        device = y * NZ + lax.rem(z + r, NZ)
        image = jnp.where(image_columns(device), 1.0, 0.0).astype(BF16)
        for h in range(HEADS):
            cols = slice(h * HD, (h + 1) * HD)
            keys = jnp.concatenate([kbuf[:, :, cols].reshape(NY * ROWS, HD), keys_image], axis=1)
            scores = dot(keys, jnp.concatenate([qbuf[r, :, cols], image], axis=1), 1, 1)
            best = jnp.max(scores, axis=0, keepdims=True)
            prob = jnp.exp2((scores - best) * EXP_SCALE)
            half, i = h // 3, h % 3
            stats[r, half, i:i + 1] = best * EXP_SCALE
            stats[r, half, 3 + i:4 + i] = jnp.sum(prob, axis=0, keepdims=True)
            opart[r, half, i * HD:(i + 1) * HD] = dot(vt[cols], prob.astype(BF16)).astype(BF16)

    def o_copy(d, t):
        r = 4 - t if d == 0 else 4 + t
        dev = zp if d == 0 else zm
        src, dst, ssrc, sdst = opart.at[r], oin.at[d, t], stats.at[r], sin.at[d, t]
        if t == 0:
            src, dst, ssrc, sdst = src.at[d], dst.at[d], ssrc.at[d], sdst.at[d]
        return (rcopy(src, dst, o_s.at[d, t], o_r.at[d, t], dev),
                rcopy(ssrc, sdst, os_s.at[d, t], os_r.at[d, t], dev))

    o_copies = [[o_copy(d, t) for t in range(4)] for d in range(2)]

    def attend_some(i, c):
        attend(4 + (2 - i // 2) * (1 - 2 * lax.rem(i, 2)))
        return c

    lax.fori_loop(0, 2, attend_some, 0)
    forward_q(2)
    lax.fori_loop(2, 4, attend_some, 0)
    forward_q(3)
    lax.fori_loop(4, 5, attend_some, 0)
    for d in range(2):
        for copy in o_copies[d][0]:
            go(copy)

    def merge(r, d, t, half):
        mine, other = stats[r, half], sin[d, t, half]
        for i in range(3):
            m0, m1 = mine[i:i + 1], other[i:i + 1]
            best = jnp.maximum(m0, m1)
            f0, f1 = jnp.exp2(m0 - best), jnp.exp2(m1 - best)
            rows = slice(i * HD, (i + 1) * HD)
            mixed = opart[r, half, rows].astype(F32) * f0 + oin[d, t, half, rows].astype(F32) * f1
            opart[r, half, rows] = mixed.astype(BF16)
            stats[r, half, i:i + 1] = best
            stats[r, half, 3 + i:4 + i] = mine[3 + i:4 + i] * f0 + other[3 + i:4 + i] * f1

    for t in (1, 2, 3):
        if t > 1:
            def attend_rest(i, c):
                attend(lax.rem(7 + 2 * i, 8) if t == 2 else 0 * i)
                return c
            lax.fori_loop(0, 2 if t == 2 else 1, attend_rest, 0)
        for d in range(2):
            for copy in o_copies[d][t - 1]:
                copy.wait_recv()
            for half in range(2):
                if t > 1 or half == d:
                    merge(4 - t if d == 0 else 4 + t, d, t - 1, half)
            for copy in o_copies[d][t]:
                go(copy)
    for d in range(2):
        for copy in o_copies[d][3]:
            copy.wait_recv()
        for half in range(2):
            merge(0, d, 3, half)
    local[6].wait()
    for h in range(HEADS):
        half, i = h // 3, h % 3
        cols = slice(h * HD, (h + 1) * HD)
        attn = opart[0, half, i * HD:(i + 1) * HD].astype(F32) / stats[0, half, 3 + i:4 + i]
        attn = attn.T.astype(BF16).astype(F32)
        hidden[:, cols] = (resv[:, cols].astype(F32) + attn).astype(BF16)

    local[7].wait()
    f_copies = x_copies(2, lambda r: fsend.at[0, r], lambda r: frecv.at[0, r])
    for r in (2, 1, 3, 0):
        cols = pl.ds(pl.multiple_of(lax.rem(x + r, NX) * PART, PART), PART)
        fsend[0, r] = dot(hidden[...], pin[:, cols]).astype(BF16)
        if r:
            go(f_copies[r])

    e_of = iota((NSEQ, CAP), 1) >> 3
    device = iota((NSEQ, CAP), 0)
    counts8 = jnp.broadcast_to(counts, (8, NSEQ)).astype(BF16)
    start = dot(counts8, jnp.where(device < e_of, 1.0, 0.0).astype(BF16))[0:1]
    count = dot(counts8, jnp.where(device == e_of, 1.0, 0.0).astype(BF16))[0:1]
    low = start + ((iota((1, CAP), 1) & 7) * NSEQ).astype(F32)
    high = jnp.minimum(low + float(NSEQ), start + count)
    place = (iota((ROWS, CAP), 0) * NSEQ + seq).astype(F32)
    chosen = jnp.where((place >= low) & (place < high), 1.0, 0.0).astype(BF16)

    def take_rows(i, c):
        peer = lax.rem(seq + i, NSEQ)
        row_copy(seq, peer).wait_recv()
        return c

    lax.fori_loop(1, NSEQ, take_rows, 0)
    target[...] = dot(chosen, arecv[...].reshape(CAP, CH).astype(BF16))
    tf = target[...]

    def x_sum(phase, copies):
        for r in (1, 2, 3):
            copies[NX - r].wait_recv()
        value = fsend[phase, 0].astype(F32)
        for r in (1, 2, 3):
            value = value + frecv[phase, r].astype(F32)
        return value

    value = x_sum(0, f_copies)
    first[...] = value
    actbuf[0] = (value * jax.nn.sigmoid(value)).astype(BF16)
    act_copies = x_copies(3, lambda r: actbuf.at[0], lambda r: actbuf.at[r])
    for r in (2, 1, 3):
        go(act_copies[r])
    local[8].wait()

    def out_rows(r):
        return pout[pl.ds(pl.multiple_of(lax.rem(x + r, NX) * PART, PART), PART), :]

    value = dot(actbuf[0], out_rows(0))
    for r in (1, 3, 2):
        act_copies[NX - r].wait_recv()
        value = value + dot(actbuf[r], out_rows(r))
    second[...] = value
    lane = iota((ROWS, HD), 1)
    inner = jnp.sum(value * tf, axis=1, keepdims=True)
    square_z = jnp.sum(value * value, axis=1, keepdims=True)
    square_f = jnp.sum(tf * tf, axis=1, keepdims=True)
    stat = jnp.where(lane == 0, inner, jnp.where(lane == 1, square_z, jnp.where(lane == 2, square_f, 0.0)))
    sstat[...] = stat.T[0:8]
    s_copies = x_copies(4, lambda r: sstat, lambda r: sstat_in.at[r])
    for r in (2, 1, 3):
        go(s_copies[r])
    for r in (1, 2, 3):
        s_copies[NX - r].wait_recv()
    stat = sstat[...]
    for r in (1, 2, 3):
        stat = stat + sstat_in[r]
    norm_z = jnp.sqrt(stat[1:2] + 1e-6)
    norm_f = jnp.sqrt(stat[2:3] + 1e-6)
    aligned = stat[0:1] / (norm_z * norm_f)
    al_ref[...] = aligned
    weight = aw_ref[...]
    rows = jnp.where(row8 == 0, -weight / (norm_z * norm_f),
                     jnp.where(row8 == 1, weight * aligned / (norm_z * norm_z), 0.0))
    cols = jnp.concatenate([rows, pad], axis=0).T
    back[...] = (cols[:, 0:1] * tf + cols[:, 1:2] * second[...]).astype(BF16)

    u_copies = x_copies(5, lambda r: fsend.at[1, r], lambda r: frecv.at[1, r])
    for r in (2, 1, 3, 0):
        fsend[1, r] = dot(back[...], out_rows(r), 1, 1).astype(BF16)
        if r:
            go(u_copies[r])

    def reduction(n, left, right, xs, xr, hs, yr, zs, zr, out):
        def across(jj):
            return rcopy(xs.at[jj], xr.at[jj], gx_s.at[n, jj], gx_r.at[n, jj], {"section": 1 - sec})

        def y_copy(r):
            peer = lax.rem(y + r, NY)
            return rcopy(hs.at[peer], yr.at[NY - r], gy_s.at[n, r - 1], gy_r.at[n, NY - r - 1],
                         {"seq": peer * NZ + z})

        def z_copy(r):
            peer = lax.rem(z + r, NZ)
            return rcopy(zs.at[peer], zr.at[NZ - r], gz_s.at[n, r - 1], gz_r.at[n, NZ - r - 1],
                         {"seq": y * NZ + peer})

        def product(j):
            return dot(left[lax.rem(j + NX - x, NX)], right[...], 0, 0).astype(BF16)

        def start():
            for jj in range(2):
                xs[jj] = product(2 * (1 - sec) + jj)
                go(across(jj))
            for jj in range(2):
                value = product(2 * sec + jj)
                for b in range(2):
                    hs[2 * jj + b] = value[b * 256:(b + 1) * 256]

        def middle():
            for jj in range(2):
                across(jj).wait_recv()
                for b in range(2):
                    hs[2 * jj + b] = (hs[2 * jj + b].astype(F32)
                                      + xr[jj, b * 256:(b + 1) * 256].astype(F32)).astype(BF16)
            for r in (2, 1, 3):
                go(y_copy(r))

        def late():
            for r in (1, 2, 3):
                y_copy(NY - r).wait_recv()
            value = hs[y].astype(F32)
            for r in (1, 2, 3):
                value = value + yr[r].astype(F32)
            zs[...] = value.astype(BF16).reshape(zs.shape)
            for r in (4, 3, 5, 2, 6, 1, 7):
                go(z_copy(r))

        def end():
            for r in range(1, NZ):
                z_copy(NZ - r).wait_recv()
            value = zs[z].astype(F32)
            for r in range(1, NZ):
                value = value + zr[r].astype(F32)
            out[...] = value

        return start, middle, late, end

    go_steps = reduction(0, actbuf, back, go_x, go_xr, go_h, go_yr, go_z, go_zr, go_ref)
    gi_steps = reduction(1, dbuf, hidden, gi_x, gi_xr, gi_h, gi_yr, gi_z, gi_zr, gi_ref)
    go_steps[0]()

    upstream = x_sum(1, u_copies)
    value = first[...]
    sig = jax.nn.sigmoid(value)
    dbuf[0] = (upstream * sig * (1.0 + value * (1.0 - sig))).astype(BF16)
    d_copies = x_copies(6, lambda r: dbuf.at[0], lambda r: dbuf.at[r])
    for r in (2, 1, 3):
        go(d_copies[r])
    go_steps[1]()
    for r in (1, 2, 3):
        d_copies[NX - r].wait_recv()
    gi_steps[0]()
    go_steps[2]()
    gi_steps[1]()
    go_steps[3]()
    gi_steps[2]()
    gi_steps[3]()

    for copy in pending:
        copy.wait_send()

    def sent_rows(i, c):
        row_copy(lax.rem(seq + i, NSEQ), seq).wait_send()
        return c

    lax.fori_loop(1, NSEQ, sent_rows, 0)


def body(
    queries, keys, values, residual, segment_ids, enc_counts, enc_hidden, enc_down, enc_resid,
    layer_scale, norm_gain, norm_bias, proj_in, proj_out, align_weight,
):
    anywhere = pl.BlockSpec(memory_space=pl.ANY)
    vmem = pl.BlockSpec(memory_space=pltpu.VMEM)
    V, D = pltpu.VMEM, pltpu.SemaphoreType.DMA
    scratch = [
        V((NZ, ROWS, WIDTH), BF16), V((NY, ROWS, WIDTH), BF16), V((NY, ROWS, WIDTH), BF16),
        V((WIDTH, NY * ROWS), BF16), V((NY, ROWS, HD), BF16), V((ROWS, WIDTH), BF16),
        V((CAP, FF), BF16), V((FF, ENC_D), BF16), V((CAP, CH), BF16),
        V((WIDTH, PROJ), BF16), V((PROJ, CH), BF16),
        V((NZ, 2, HALF, HD), BF16), V((NZ, 2, 8, HD), F32),
        V((2, 4, 2, HALF, HD), BF16), V((2, 4, 2, 8, HD), F32),
        V((NX, CAP, CH), BF16), V((NX, CAP, CH), BF16), V((CAP, CH), F32),
        V((8, CAP), F32), V((NX, 8, CAP), F32),
        V((NSEQ, 8, CH), F32), V((NSEQ, 8, CH), F32), V((ROWS, CH), F32),
        V((ROWS, WIDTH), BF16), V((2, NX, ROWS, PART), BF16), V((2, NX, ROWS, PART), BF16),
        V((ROWS, PART), F32), V((NX, ROWS, PART), BF16), V((ROWS, CH), F32),
        V((8, ROWS), F32), V((NX, 8, ROWS), F32), V((ROWS, CH), BF16), V((NX, ROWS, PART), BF16),
        V((2, HD, HD), F32),
    ]
    for width in (CH, WIDTH):
        scratch += [
            V((2, PART, width), BF16), V((2, PART, width), BF16), V((NY, 256, width), BF16),
            V((NY, 256, width), BF16), V((NZ, 32, width), BF16), V((NZ, 32, width), BF16),
        ]
    scratch += [
        D((9,)), D((2, 4)), D((2, 4)), D((6,)), D((6,)), D((2, 4)), D((2, 4)), D((2, 4)), D((2, 4)),
        D((7, 3)), D((7, 3)), D((NSEQ,)), D((NSEQ,)),
        D((2, 2)), D((2, 2)), D((2, 3)), D((2, 3)), D((2, 7)), D((2, 7)),
    ]
    aligned, grad_in_t, grad_out = pl.pallas_call(
        kernel,
        out_shape=(
            jax.ShapeDtypeStruct((1, ROWS), F32),
            jax.ShapeDtypeStruct((32, WIDTH), F32),
            jax.ShapeDtypeStruct((32, CH), F32),
        ),
        in_specs=[anywhere] * 4 + [vmem] * 2 + [anywhere] * 3 + [vmem] * 3 + [anywhere] * 2 + [vmem],
        out_specs=(vmem, vmem, vmem),
        scratch_shapes=scratch,
        compiler_params=pltpu.CompilerParams(
            collective_id=0, has_side_effects=True, vmem_limit_bytes=56 * 1024 * 1024
        ),
        name="align",
    )(
        queries, keys, values, residual, segment_ids, enc_counts, enc_hidden, enc_down, enc_resid,
        layer_scale.reshape(1, -1), norm_gain.reshape(1, -1), norm_bias.reshape(1, -1),
        proj_in, proj_out, align_weight.reshape(1, -1),
    )
    return aligned.reshape(-1), grad_in_t, grad_out


def solution(mesh):
    return jax.shard_map(
        body,
        mesh=mesh,
        in_specs=(
            P(("section", "seq"), "mp"),
            P(("section", "seq"), "mp"),
            P(("section", "seq"), "mp"),
            P(("section", "seq"), "mp"),
            P("section", None),
            P("section", None),
            P(("section", "seq"), "mp"),
            P("mp", None),
            P(("section", "seq"), "mp"),
            P(),
            P(),
            P(),
            P("mp", None),
            P(None, "mp"),
            P(("section", "seq")),
        ),
        out_specs=(P(("section", "seq")), P(("section", "seq"), "mp"), P(("section", "seq"), "mp")),
        check_vma=False,
    )
```

```python
import math

import jax
import jax.numpy as jnp
from jax import lax
from jax.experimental import pallas as pl
from jax.experimental.pallas import tpu as pltpu
from jax.sharding import PartitionSpec as P

MESH = pl.DeviceIdType.MESH
F32, BF16, I32 = jnp.float32, jnp.bfloat16, jnp.int32
HD = 128
ENC_D = 1536
NX, NY, NZ = 4, 4, 8
NSEQ = NY * NZ
ROWS = 128
CAP = 256
WIDTH = 768
HEADS = 6
HALF = 384
CH = 384
FF = 1024
PROJ = 2048
PART = 512
SAME = 8192.0
EXP_SCALE = math.log2(math.e) * HD ** (-0.5)


def rcopy(src, dst, send, recv, dev):
    return pltpu.make_async_remote_copy(
        src_ref=src, dst_ref=dst, send_sem=send, recv_sem=recv, device_id=dev, device_id_type=MESH
    )


def iota(shape, dim):
    return lax.broadcasted_iota(I32, shape, dim)


def dot(a, b, ca=1, cb=0):
    return lax.dot_general(a, b, (((ca,), (cb,)), ((), ())), preferred_element_type=F32)


def kernel(
    q_hbm, k_hbm, v_hbm, res_hbm, seg_ref, cnt_ref, eh_hbm, ed_hbm, er_hbm, ls_ref, gain_ref, bias_ref,
    pin_hbm, pout_hbm, aw_ref,
    al_ref, gi_ref, go_ref,
    qbuf, kbuf, vbuf, vt, ko, resv, ehv, edv, erv, pin, pout,
    opart, stats, oin, sin,
    esend, erecv, share, estat, estat_in, packed, arecv, aturn, alast, target,
    hidden, fsend, frecv, first, actbuf, second, sstat, sstat_in, back, dbuf, segrow,
    go_x, go_xr, go_h, go_yr, go_z, go_zr,
    gi_x, gi_xr, gi_h, a_y, a_yr, a_z, a_zr, b_z, b_in, b_y, b_yr,
    lsem, q_s, q_r, kv_s, kv_r, o_s, o_r, os_s, os_r, x_s, x_r, ay_s, ay_r, az_s, az_r,
    gx_s, gx_r, gy_s, gy_r, gz_s, gz_r, gb_s, gb_r,
):
    sec = lax.axis_index("section")
    seq = lax.axis_index("seq")
    x = lax.axis_index("mp")
    y = seq // NZ
    z = lax.rem(seq, NZ)
    zp = {"seq": y * NZ + lax.rem(z + 1, NZ)}
    zm = {"seq": y * NZ + lax.rem(z + NZ - 1, NZ)}
    yp = {"seq": lax.rem(y + 1, NY) * NZ + z}
    ym = {"seq": lax.rem(y + NY - 1, NY) * NZ + z}
    pending = []

    def go(copy):
        copy.start()
        pending.append(copy)
        return copy

    def take(copy):
        copy.wait_recv()

    local = []
    for n, (src, dst) in enumerate((
        (q_hbm, qbuf.at[0]), (k_hbm, kbuf.at[0]), (v_hbm, vbuf.at[0]), (eh_hbm, ehv), (ed_hbm, edv),
        (er_hbm, erv), (res_hbm, resv), (pin_hbm, pin), (pout_hbm, pout),
    )):
        copy = pltpu.make_async_copy(src, dst, lsem.at[n])
        copy.start()
        local.append(copy)

    barrier = pltpu.get_barrier_semaphore()

    greeted = [{"seq": y * NZ + lax.rem(z + r, NZ)} for r in range(1, NZ)]
    greeted += [{"seq": lax.rem(y + r, NY) * NZ + z} for r in range(1, NY)]
    greeted += [{"mp": lax.rem(x + r, NX)} for r in range(1, NX)]
    greeted += [{"section": 1 - sec}]
    for device in greeted:
        pl.semaphore_signal(barrier, inc=1, device_id=device, device_id_type=MESH)
    pl.semaphore_wait(barrier, len(greeted))

    def q_copy(d, t, half):
        cols = pl.ds(half * HALF, HALF)
        src = qbuf.at[(8 - t) % 8 if d == 0 else t, :, cols]
        dst = qbuf.at[7 - t if d == 0 else t + 1, :, cols]
        return rcopy(src, dst, q_s.at[d, t, half], q_r.at[d, t, half], zp if d == 0 else zm)

    def kv_copy(n):
        src, dst, dev = (
            (kbuf.at[0], kbuf.at[3], yp), (kbuf.at[0], kbuf.at[1], ym),
            (vbuf.at[0], vbuf.at[3], yp), (vbuf.at[0], vbuf.at[1], ym),
            (kbuf.at[3], kbuf.at[2], yp), (vbuf.at[1], vbuf.at[2], ym),
        )[n]
        return rcopy(src, dst, kv_s.at[n], kv_r.at[n], dev)

    q_copies = [[{h: q_copy(d, t, h) for h in ((0, 1) if t < 3 else (d,))} for t in range(4)] for d in range(2)]
    kv_copies = [kv_copy(n) for n in range(6)]
    local[0].wait()
    for half in range(2):
        for d in range(2):
            go(q_copies[d][0][half])
    local[1].wait()
    go(kv_copies[0])
    go(kv_copies[1])
    local[2].wait()
    go(kv_copies[2])
    go(kv_copies[3])

    def x_copies(phase, src_of, dst_of):
        return {
            r: rcopy(src_of(r), dst_of(NX - r), x_s.at[phase, r - 1], x_r.at[phase, NX - r - 1],
                     {"mp": lax.rem(x + r, NX)})
            for r in (1, 2, 3)
        }

    local[3].wait()
    local[4].wait()
    enc_copies = x_copies(0, lambda r: esend.at[r], lambda r: erecv.at[r])
    for r in (2, 1, 3, 0):
        cols = pl.ds(pl.multiple_of(lax.rem(x + r, NX) * CH, CH), CH)
        esend[r] = dot(ehv[...], edv[:, cols]).astype(BF16)
        if r:
            go(enc_copies[r])

    ids = iota((16, NSEQ * ROWS), 0)
    seg = seg_ref[...]
    below = jnp.sum(jnp.where(seg < ids, 1.0, 0.0), axis=1, keepdims=True)
    upto = jnp.sum(jnp.where(seg <= ids, 1.0, 0.0), axis=1, keepdims=True)
    lane = iota((16, HD), 1)
    tail = jnp.full((HD - 16, HD), 1e9, F32)
    segrow[0] = jnp.concatenate([jnp.broadcast_to(below, lane.shape), tail], axis=0).T
    segrow[1] = jnp.concatenate([jnp.broadcast_to(upto, lane.shape), tail], axis=0).T

    def image_columns(device):
        place = (iota((ROWS, HD), 0) * NSEQ + device).astype(F32)
        return (place >= segrow[0]) & (place < segrow[1])

    for r in range(NY):
        device = lax.rem(y + r, NY) * NZ + z
        ko[r] = jnp.where(image_columns(device), SAME, 0.0).astype(BF16)

    def forward_q(t, half):
        for d in range(2):
            if half in q_copies[d][t]:
                take(q_copies[d][t][half])
            if t < 3 and half in q_copies[d][t + 1]:
                go(q_copies[d][t + 1][half])

    forward_q(0, 0)
    forward_q(0, 1)
    take(kv_copies[0])
    go(kv_copies[4])
    take(kv_copies[1])

    local[5].wait()
    def own(ref):
        return jnp.concatenate([ref[pl.ds(3 * x + i, 1), :] for i in range(3)], axis=1)

    for r in (1, 2, 3):
        take(enc_copies[NX - r])
    enc = esend[0].astype(F32)
    for r in (1, 2, 3):
        enc = enc + erecv[r].astype(F32)
    enc = erv[...].astype(F32) + own(ls_ref) * enc
    share[...] = enc
    lane = iota((CAP, HD), 1)
    total = jnp.sum(enc, axis=1, keepdims=True)
    square = jnp.sum(enc * enc, axis=1, keepdims=True)
    packed_stat = jnp.where(lane == 0, total, jnp.where(lane == 1, square, 0.0))
    for b in range(2):
        estat[:, b * HD:(b + 1) * HD] = packed_stat[b * HD:(b + 1) * HD].T[0:8]
    stat_copies = x_copies(1, lambda r: estat, lambda r: estat_in.at[r])
    for r in (2, 1, 3):
        go(stat_copies[r])

    take(kv_copies[2])
    take(kv_copies[3])
    go(kv_copies[5])
    forward_q(1, 0)
    forward_q(1, 1)

    for r in (1, 2, 3):
        take(stat_copies[NX - r])
    both = estat[...]
    for r in (1, 2, 3):
        both = both + estat_in[r]
    mean = both[0:1] * (1.0 / ENC_D)
    scale = lax.rsqrt(both[1:2] * (1.0 / ENC_D) - mean * mean + 1e-6)
    pad = jnp.zeros((HD - 8, HD), F32)
    row8 = iota((8, HD), 0)
    gain = own(gain_ref)
    bias = own(bias_ref)
    parts = []
    for b in range(2):
        cut = slice(b * HD, (b + 1) * HD)
        rows = jnp.where(row8 == 0, mean[:, cut], jnp.where(row8 == 1, scale[:, cut], 0.0))
        cols = jnp.concatenate([rows, pad], axis=0).T
        parts.append((((share[cut] - cols[:, 0:1]) * cols[:, 1:2]) * gain + bias).astype(BF16))
    feature = jnp.concatenate(parts, axis=0)
    counts = cnt_ref[...].astype(F32)
    before = jnp.sum(jnp.where(iota((1, NSEQ), 1) < seq, counts, 0.0), axis=1, keepdims=True).astype(I32)
    row = iota((CAP, CAP), 0)
    wanted = (row & 7) * NSEQ + (((row >> 3) - before) & (NSEQ - 1))
    permutation = jnp.where(iota((CAP, CAP), 1) == wanted, 1.0, 0.0).astype(BF16)
    packed[...] = dot(permutation, feature).reshape(NY, NZ, 8, CH)

    def row_y(r):
        peer = lax.rem(y + r, NY)
        return rcopy(packed.at[peer], arecv.at[y], ay_s.at[r - 1], ay_r.at[NY - r - 1], {"seq": peer * NZ + z})

    def row_z(r):
        peer = lax.rem(z + r, NZ)
        return rcopy(aturn.at[peer], alast.at[z], az_s.at[r - 1], az_r.at[NZ - r - 1], {"seq": y * NZ + peer})

    row_ys = {r: row_y(r) for r in range(1, NY)}
    row_zs = {r: row_z(r) for r in range(1, NZ)}
    for r in (2, 1, 3):
        go(row_ys[r])
    arecv[pl.ds(y, 1)] = packed[pl.ds(y, 1)]
    for n in (4, 5):
        take(kv_copies[n])
    for r in range(NY):
        vt[:, r * ROWS:(r + 1) * ROWS] = vbuf[r].T
    keys_image = ko[...].reshape(NY * ROWS, HD)

    def attend(r):
        device = y * NZ + lax.rem(z + r, NZ)
        image = jnp.where(image_columns(device), 1.0, 0.0).astype(BF16)
        for h in range(HEADS):
            cols = slice(h * HD, (h + 1) * HD)
            keys = jnp.concatenate([kbuf[:, :, cols].reshape(NY * ROWS, HD), keys_image], axis=1)
            scores = dot(keys, jnp.concatenate([qbuf[r, :, cols], image], axis=1), 1, 1)
            best = jnp.max(scores, axis=0, keepdims=True)
            prob = jnp.exp2((scores - best) * EXP_SCALE)
            half, i = h // 3, h % 3
            stats[r, half, i:i + 1] = best * EXP_SCALE
            stats[r, half, 3 + i:4 + i] = jnp.sum(prob, axis=0, keepdims=True)
            opart[r, half, i * HD:(i + 1) * HD] = dot(vt[cols], prob.astype(BF16)).astype(BF16)

    def o_copy(d, t, half):
        r = 4 - t if d == 0 else 4 + t
        dev = zp if d == 0 else zm
        return (rcopy(opart.at[r, half], oin.at[d, t, half], o_s.at[d, t, half], o_r.at[d, t, half], dev),
                rcopy(stats.at[r, half], sin.at[d, t, half], os_s.at[d, t, half], os_r.at[d, t, half], dev))

    o_copies = [[{h: o_copy(d, t, h) for h in ((0, 1) if t else (d,))} for t in range(4)] for d in range(2)]

    def go_o(d, t, half):
        for copy in o_copies[d][t][half]:
            go(copy)

    def take_o(d, t, half):
        for copy in o_copies[d][t][half]:
            take(copy)

    def attend_some(i, c):
        attend(4 + (2 - i // 2) * (1 - 2 * lax.rem(i, 2)))
        return c

    lax.fori_loop(0, 2, attend_some, 0)
    forward_q(2, 0)
    forward_q(2, 1)
    lax.fori_loop(2, 4, attend_some, 0)
    forward_q(3, 0)
    forward_q(3, 1)
    lax.fori_loop(4, 5, attend_some, 0)
    for d in range(2):
        go_o(d, 0, d)
    for d in range(2):
        go_o(d, 1, 1 - d)
    def merge(r, d, t, half):
        mine, other = stats[r, half], sin[d, t, half]
        for i in range(3):
            m0, m1 = mine[i:i + 1], other[i:i + 1]
            best = jnp.maximum(m0, m1)
            f0, f1 = jnp.exp2(m0 - best), jnp.exp2(m1 - best)
            rows = slice(i * HD, (i + 1) * HD)
            mixed = opart[r, half, rows].astype(F32) * f0 + oin[d, t, half, rows].astype(F32) * f1
            opart[r, half, rows] = mixed.astype(BF16)
            stats[r, half, i:i + 1] = best
            stats[r, half, 3 + i:4 + i] = mine[3 + i:4 + i] * f0 + other[3 + i:4 + i] * f1

    for t in (1, 2, 3):
        if t < 3:
            def attend_rest(i, c):
                attend(lax.rem(7 + 2 * i, 8) if t == 1 else 0 * i)
                return c
            lax.fori_loop(0, 2 if t == 1 else 1, attend_rest, 0)
        for turn in range(2):
            for d in range(2):
                half = d if turn else 1 - d
                if t == 1 and not turn:
                    continue
                take_o(d, t - 1, half)
                merge(4 - t if d == 0 else 4 + t, d, t - 1, half)
                go_o(d, t, half)
    for r in (1, 2, 3):
        take(row_ys[NY - r])
    for n in range(NZ):
        aturn[n] = arecv[:, n].reshape(NY * 8, CH).astype(BF16)
    alast[pl.ds(z, 1)] = aturn[pl.ds(z, 1)]
    for half in range(2):
        for d in range(2):
            take_o(d, 3, half)
            merge(0, d, 3, half)
    for r in (4, 3, 5, 2, 6, 1, 7):
        go(row_zs[r])
    local[6].wait()
    for h in range(HEADS):
        half, i = h // 3, h % 3
        cols = slice(h * HD, (h + 1) * HD)
        attn = opart[0, half, i * HD:(i + 1) * HD].astype(F32) / stats[0, half, 3 + i:4 + i]
        attn = attn.T.astype(BF16).astype(F32)
        hidden[:, cols] = (resv[:, cols].astype(F32) + attn).astype(BF16)

    local[7].wait()
    f_copies = x_copies(2, lambda r: fsend.at[0, r], lambda r: frecv.at[0, r])
    for r in (2, 1, 3, 0):
        cols = pl.ds(pl.multiple_of(lax.rem(x + r, NX) * PART, PART), PART)
        fsend[0, r] = dot(hidden[...], pin[:, cols]).astype(BF16)
        if r:
            go(f_copies[r])

    def x_sum(phase, copies):
        for r in (1, 2, 3):
            take(copies[NX - r])
        value = fsend[phase, 0].astype(F32)
        for r in (1, 2, 3):
            value = value + frecv[phase, r].astype(F32)
        return value

    value = x_sum(0, f_copies)
    first[...] = value
    actbuf[0] = (value * jax.nn.sigmoid(value)).astype(BF16)
    act_copies = x_copies(3, lambda r: actbuf.at[0], lambda r: actbuf.at[r])
    for r in (2, 1, 3):
        go(act_copies[r])
    local[8].wait()

    column = iota((NSEQ, CAP), 1)
    e_of = ((column >> 3) & (NY - 1)) * NZ + (column >> 5)
    device = iota((NSEQ, CAP), 0)
    counts8 = jnp.broadcast_to(counts, (8, NSEQ)).astype(BF16)
    start = dot(counts8, jnp.where(device < e_of, 1.0, 0.0).astype(BF16))[0:1]
    count = dot(counts8, jnp.where(device == e_of, 1.0, 0.0).astype(BF16))[0:1]
    low = start + ((iota((1, CAP), 1) & 7) * NSEQ).astype(F32)
    high = jnp.minimum(low + float(NSEQ), start + count)
    place = (iota((ROWS, CAP), 0) * NSEQ + seq).astype(F32)
    chosen = jnp.where((place >= low) & (place < high), 1.0, 0.0).astype(BF16)

    for r in range(1, NZ):
        take(row_zs[NZ - r])
    target[...] = dot(chosen, alast[...].reshape(CAP, CH))
    tf = target[...]

    def out_rows(r):
        return pout[pl.ds(pl.multiple_of(lax.rem(x + r, NX) * PART, PART), PART), :]

    value = dot(actbuf[0], out_rows(0))
    for r in (1, 3, 2):
        take(act_copies[NX - r])
        value = value + dot(actbuf[r], out_rows(r))
    second[...] = value
    lane = iota((ROWS, HD), 1)
    inner = jnp.sum(value * tf, axis=1, keepdims=True)
    square_z = jnp.sum(value * value, axis=1, keepdims=True)
    square_f = jnp.sum(tf * tf, axis=1, keepdims=True)
    stat = jnp.where(lane == 0, inner, jnp.where(lane == 1, square_z, jnp.where(lane == 2, square_f, 0.0)))
    sstat[...] = stat.T[0:8]
    s_copies = x_copies(4, lambda r: sstat, lambda r: sstat_in.at[r])
    for r in (2, 1, 3):
        go(s_copies[r])
    for r in (1, 2, 3):
        take(s_copies[NX - r])
    stat = sstat[...]
    for r in (1, 2, 3):
        stat = stat + sstat_in[r]
    norm_z = jnp.sqrt(stat[1:2] + 1e-6)
    norm_f = jnp.sqrt(stat[2:3] + 1e-6)
    aligned = stat[0:1] / (norm_z * norm_f)
    al_ref[...] = aligned
    weight = aw_ref[...]
    rows = jnp.where(row8 == 0, -weight / (norm_z * norm_f),
                     jnp.where(row8 == 1, weight * aligned / (norm_z * norm_z), 0.0))
    cols = jnp.concatenate([rows, pad], axis=0).T
    back[...] = (cols[:, 0:1] * tf + cols[:, 1:2] * second[...]).astype(BF16)

    u_copies = x_copies(5, lambda r: fsend.at[1, r], lambda r: frecv.at[1, r])
    for r in (2, 1, 3, 0):
        fsend[1, r] = dot(back[...], out_rows(r), 1, 1).astype(BF16)
        if r:
            go(u_copies[r])

    def reduction(n, left, right, xs, xr, hs, yr, zs, zr, out):
        def across(jj):
            return rcopy(xs.at[jj], xr.at[jj], gx_s.at[n, jj], gx_r.at[n, jj], {"section": 1 - sec})

        def y_copy(r):
            peer = lax.rem(y + r, NY)
            return rcopy(hs.at[peer], yr.at[NY - r], gy_s.at[n, r - 1], gy_r.at[n, NY - r - 1],
                         {"seq": peer * NZ + z})

        def z_copy(r):
            peer = lax.rem(z + r, NZ)
            return rcopy(zs.at[peer], zr.at[NZ - r], gz_s.at[n, r - 1], gz_r.at[n, NZ - r - 1],
                         {"seq": y * NZ + peer})

        acrosses = [across(jj) for jj in range(2)]
        y_copies = {r: y_copy(r) for r in range(1, NY)}
        z_copies = {r: z_copy(r) for r in range(1, NZ)}

        def product(j):
            return dot(left[lax.rem(j + NX - x, NX)], right[...], 0, 0).astype(BF16)

        def start():
            for jj in range(2):
                xs[jj] = product(2 * (1 - sec) + jj)
                go(acrosses[jj])
            for jj in range(2):
                value = product(2 * sec + jj)
                for b in range(2):
                    hs[2 * jj + b] = value[b * 256:(b + 1) * 256]

        def middle():
            for jj in range(2):
                take(acrosses[jj])
                for b in range(2):
                    hs[2 * jj + b] = (hs[2 * jj + b].astype(F32)
                                      + xr[jj, b * 256:(b + 1) * 256].astype(F32)).astype(BF16)
            for r in (2, 1, 3):
                go(y_copies[r])

        def late():
            for r in (1, 2, 3):
                take(y_copies[NY - r])
            value = hs[y].astype(F32)
            for r in (1, 2, 3):
                value = value + yr[r].astype(F32)
            zs[...] = value.astype(BF16).reshape(zs.shape)
            for r in (4, 3, 5, 2, 6, 1, 7):
                go(z_copies[r])

        def end():
            for r in range(1, NZ):
                take(z_copies[NZ - r])
            value = zs[z].astype(F32)
            for r in range(1, NZ):
                value = value + zr[r].astype(F32)
            out[...] = value

        return start, middle, late, end

    go_steps = reduction(0, actbuf, back, go_x, go_xr, go_h, go_yr, go_z, go_zr, go_ref)
    go_steps[0]()

    upstream = x_sum(1, u_copies)
    value = first[...]
    sig = jax.nn.sigmoid(value)
    dbuf[0] = (upstream * sig * (1.0 + value * (1.0 - sig))).astype(BF16)
    d_copies = x_copies(6, lambda r: dbuf.at[0], lambda r: dbuf.at[r])
    for r in (2, 1, 3):
        go(d_copies[r])
    go_steps[1]()
    for r in (1, 2, 3):
        take(d_copies[NX - r])

    def across(jj):
        return rcopy(gi_x.at[jj], gi_xr.at[jj], gx_s.at[1, jj], gx_r.at[1, jj], {"section": 1 - sec})

    def product(j):
        return dot(dbuf[lax.rem(j + NX - x, NX)], hidden[...], 0, 0).astype(BF16)

    def ya_copy(r):
        peer = lax.rem(y + r, NY)
        return rcopy(a_y.at[peer], a_yr.at[NY - r], gy_s.at[1, r - 1], gy_r.at[1, NY - r - 1], {"seq": peer * NZ + z})

    def za_copy(r):
        peer = lax.rem(z + r, NZ)
        return rcopy(a_z.at[peer], a_zr.at[NZ - r], gz_s.at[1, r - 1], gz_r.at[1, NZ - r - 1], {"seq": y * NZ + peer})

    def yb_copy(r):
        peer = lax.rem(y + r, NY)
        return rcopy(b_y.at[peer], b_yr.at[NY - r], gy_s.at[2, r - 1], gy_r.at[2, NY - r - 1], {"seq": peer * NZ + z})

    def zb_copy(d, t, half):
        chunk = lax.rem(z + (4 - t if d == 0 else 4 + t), NZ)
        part = pl.ds(2 * half, 2)
        return rcopy(b_z.at[chunk, part], b_in.at[d, t, part], gb_s.at[d, t, half], gb_r.at[d, t, half],
                     zp if d == 0 else zm)

    acrosses = [across(jj) for jj in range(2)]
    ya_copies = {r: ya_copy(r) for r in range(1, NY)}
    za_copies = {r: za_copy(r) for r in range(1, NZ)}
    yb_copies = {r: yb_copy(r) for r in range(1, NY)}
    zb_copies = [[{h: zb_copy(d, t, h) for h in ((0, 1) if t else (d,))} for t in range(4)] for d in range(2)]
    for jj in range(2):
        gi_x[jj] = product(2 * (1 - sec) + jj)
        go(acrosses[jj])
    go_steps[2]()
    for jj in range(2):
        gi_h[jj] = product(2 * sec + jj)
    for jj in range(2):
        take(acrosses[jj])
        for b in range(2):
            rows = slice(b * 256, (b + 1) * 256)
            value = (gi_h[jj, rows].astype(F32) + gi_xr[jj, rows].astype(F32)).astype(BF16)
            a_y[2 * jj + b] = value[:, 0:HALF]
            for n in range(NZ):
                b_z[n, 2 * jj + b] = value[n * 32:(n + 1) * 32, HALF:WIDTH]

    def go_b(d, t, half):
        go(zb_copies[d][t][half])

    def merge_b(d, t, half):
        take(zb_copies[d][t][half])
        chunk = lax.rem(z + (3 - t if d == 0 else 5 + t), NZ)
        part = pl.ds(2 * half, 2)
        b_z[chunk, part] = (b_z[chunk, part].astype(F32) + b_in[d, t, part].astype(F32)).astype(BF16)

    for d in range(2):
        go_b(d, 0, d)
    for r in (2, 1, 3):
        go(ya_copies[r])
    for d in range(2):
        go_b(d, 1, 1 - d)
    for d in range(2):
        merge_b(d, 0, d)
        go_b(d, 1, d)
    for turn in range(2):
        for d in range(2):
            half = d if turn else 1 - d
            merge_b(d, 1, half)
            go_b(d, 2, half)
    for r in (1, 2, 3):
        take(ya_copies[NY - r])
    value = a_y[y].astype(F32)
    for r in (1, 2, 3):
        value = value + a_yr[r].astype(F32)
    a_z[...] = value.astype(BF16).reshape(NZ, 32, HALF)
    for r in (4, 3, 5, 2, 6, 1, 7):
        go(za_copies[r])
    for turn in range(2):
        for d in range(2):
            half = d if turn else 1 - d
            merge_b(d, 2, half)
            go_b(d, 3, half)
    for half in range(2):
        for d in range(2):
            merge_b(d, 3, half)
    b_y[...] = b_z[z]
    for r in (2, 1, 3):
        go(yb_copies[r])
    go_steps[3]()
    for r in range(1, NZ):
        take(za_copies[NZ - r])
    value = a_z[z].astype(F32)
    for r in range(1, NZ):
        value = value + a_zr[r].astype(F32)
    gi_ref[:, 0:HALF] = value
    for r in (1, 2, 3):
        take(yb_copies[NY - r])
    value = b_y[y].astype(F32)
    for r in (1, 2, 3):
        value = value + b_yr[r].astype(F32)
    gi_ref[:, HALF:WIDTH] = value

    for copy in pending:
        copy.wait_send()


def body(
    queries, keys, values, residual, segment_ids, enc_counts, enc_hidden, enc_down, enc_resid,
    layer_scale, norm_gain, norm_bias, proj_in, proj_out, align_weight,
):
    anywhere = pl.BlockSpec(memory_space=pl.ANY)
    vmem = pl.BlockSpec(memory_space=pltpu.VMEM)
    V, D = pltpu.VMEM, pltpu.SemaphoreType.DMA
    scratch = [
        V((NZ, ROWS, WIDTH), BF16), V((NY, ROWS, WIDTH), BF16), V((NY, ROWS, WIDTH), BF16),
        V((WIDTH, NY * ROWS), BF16), V((NY, ROWS, HD), BF16), V((ROWS, WIDTH), BF16),
        V((CAP, FF), BF16), V((FF, ENC_D), BF16), V((CAP, CH), BF16),
        V((WIDTH, PROJ), BF16), V((PROJ, CH), BF16),
        V((NZ, 2, HALF, HD), BF16), V((NZ, 2, 8, HD), F32),
        V((2, 4, 2, HALF, HD), BF16), V((2, 4, 2, 8, HD), F32),
        V((NX, CAP, CH), BF16), V((NX, CAP, CH), BF16), V((CAP, CH), F32),
        V((8, CAP), F32), V((NX, 8, CAP), F32),
        V((NY, NZ, 8, CH), F32), V((NY, NZ, 8, CH), F32), V((NZ, 32, CH), BF16), V((NZ, 32, CH), BF16),
        V((ROWS, CH), F32),
        V((ROWS, WIDTH), BF16), V((2, NX, ROWS, PART), BF16), V((2, NX, ROWS, PART), BF16),
        V((ROWS, PART), F32), V((NX, ROWS, PART), BF16), V((ROWS, CH), F32),
        V((8, ROWS), F32), V((NX, 8, ROWS), F32), V((ROWS, CH), BF16), V((NX, ROWS, PART), BF16),
        V((2, HD, HD), F32),
    ]
    scratch += [
        V((2, PART, CH), BF16), V((2, PART, CH), BF16), V((NY, 256, CH), BF16),
        V((NY, 256, CH), BF16), V((NZ, 32, CH), BF16), V((NZ, 32, CH), BF16),
        V((2, PART, WIDTH), BF16), V((2, PART, WIDTH), BF16), V((2, PART, WIDTH), BF16),
        V((NY, 256, HALF), BF16), V((NY, 256, HALF), BF16), V((NZ, 32, HALF), BF16), V((NZ, 32, HALF), BF16),
        V((NZ, NY, 32, HALF), BF16), V((2, 4, NY, 32, HALF), BF16), V((NY, 32, HALF), BF16), V((NY, 32, HALF), BF16),
    ]
    scratch += [
        D((9,)), D((2, 4, 2)), D((2, 4, 2)), D((6,)), D((6,)),
        D((2, 4, 2)), D((2, 4, 2)), D((2, 4, 2)), D((2, 4, 2)),
        D((7, 3)), D((7, 3)), D((3,)), D((3,)), D((7,)), D((7,)),
        D((2, 2)), D((2, 2)), D((3, 3)), D((3, 3)), D((2, 7)), D((2, 7)), D((2, 4, 2)), D((2, 4, 2)),
    ]
    aligned, grad_in_t, grad_out = pl.pallas_call(
        kernel,
        out_shape=(
            jax.ShapeDtypeStruct((1, ROWS), F32),
            jax.ShapeDtypeStruct((32, WIDTH), F32),
            jax.ShapeDtypeStruct((32, CH), F32),
        ),
        in_specs=[anywhere] * 4 + [vmem] * 2 + [anywhere] * 3 + [vmem] * 3 + [anywhere] * 2 + [vmem],
        out_specs=(vmem, vmem, vmem),
        scratch_shapes=scratch,
        compiler_params=pltpu.CompilerParams(
            collective_id=0, has_side_effects=True, vmem_limit_bytes=56 * 1024 * 1024
        ),
        name="align",
    )(
        queries, keys, values, residual, segment_ids, enc_counts, enc_hidden, enc_down, enc_resid,
        layer_scale.reshape(-1, HD), norm_gain.reshape(-1, HD), norm_bias.reshape(-1, HD),
        proj_in, proj_out, align_weight.reshape(1, -1),
    )

    def hand_on(a, b, c, a_out, b_out, c_out):
        a_out[...] = a[...]
        b_out[...] = b[...]
        c_out[...] = c[...]

    aligned, grad_in_t, grad_out = pl.pallas_call(
        hand_on,
        out_shape=tuple(jax.ShapeDtypeStruct(v.shape, F32) for v in (aligned, grad_in_t, grad_out)),
        in_specs=[vmem] * 3,
        out_specs=(vmem, vmem, vmem),
        name="hand_on",
    )(aligned, grad_in_t, grad_out)
    return aligned.reshape(-1), grad_in_t, grad_out


def solution(mesh):
    return jax.shard_map(
        body,
        mesh=mesh,
        in_specs=(
            P(("section", "seq"), "mp"),
            P(("section", "seq"), "mp"),
            P(("section", "seq"), "mp"),
            P(("section", "seq"), "mp"),
            P("section", None),
            P("section", None),
            P(("section", "seq"), "mp"),
            P("mp", None),
            P(("section", "seq"), "mp"),
            P(),
            P(),
            P(),
            P("mp", None),
            P(None, "mp"),
            P(("section", "seq")),
        ),
        out_specs=(P(("section", "seq")), P(("section", "seq"), "mp"), P(("section", "seq"), "mp")),
        check_vma=False,
    )
```

```python
import math

import jax
import jax.numpy as jnp
from jax import lax
from jax.experimental import pallas as pl
from jax.experimental.pallas import tpu as pltpu
from jax.sharding import PartitionSpec as P

MESH = pl.DeviceIdType.MESH
F32, BF16, I32 = jnp.float32, jnp.bfloat16, jnp.int32
HD = 128
ENC_D = 1536
NX, NY, NZ = 4, 4, 8
NSEQ = NY * NZ
ROWS = 128
CAP = 256
WIDTH = 768
HEADS = 6
HALF = 384
CH = 384
FF = 1024
PROJ = 2048
PART = 512
SAME = 8192.0
EXP_SCALE = math.log2(math.e) * HD ** (-0.5)


def rcopy(src, dst, send, recv, dev):
    return pltpu.make_async_remote_copy(
        src_ref=src, dst_ref=dst, send_sem=send, recv_sem=recv, device_id=dev, device_id_type=MESH
    )


def iota(shape, dim):
    return lax.broadcasted_iota(I32, shape, dim)


def dot(a, b, ca=1, cb=0):
    return lax.dot_general(a, b, (((ca,), (cb,)), ((), ())), preferred_element_type=F32)


def kernel(
    q_hbm, k_hbm, v_hbm, res_hbm, seg_ref, cnt_ref, eh_hbm, ed_hbm, er_hbm, ls_ref, gain_ref, bias_ref,
    pin_hbm, pout_hbm, aw_ref,
    al_ref, gi_ref, go_ref,
    qbuf, kbuf, vbuf, vt, ko, resv, ehv, edv, erv, pin, pfull,
    opart, stats, oin, sin,
    esend, erecv, share, estat, estat_in, packed, arecv, aturn, alast, tsend, tgt,
    hidden, fpart, frecv, first, actall, second, bsend, backall, alall, dall, column_weight, segrow,
    go_x, go_xr, go_h, go_yr, go_z, go_zr,
    gi_x, gi_xr, gi_h, a_y, a_yr, a_z, a_zr, b_z, b_in, b_y, b_yr,
    lsem, q_s, q_r, kv_s, kv_r, o_s, o_r, os_s, os_r, x_s, x_r, pc_s, pc_r, ay_s, ay_r, az_s, az_r,
    gx_s, gx_r, gy_s, gy_r, gz_s, gz_r, gb_s, gb_r,
):
    sec = lax.axis_index("section")
    seq = lax.axis_index("seq")
    x = lax.axis_index("mp")
    y = seq // NZ
    z = lax.rem(seq, NZ)
    zp = {"seq": y * NZ + lax.rem(z + 1, NZ)}
    zm = {"seq": y * NZ + lax.rem(z + NZ - 1, NZ)}
    yp = {"seq": lax.rem(y + 1, NY) * NZ + z}
    ym = {"seq": lax.rem(y + NY - 1, NY) * NZ + z}
    pending = []

    def go(copy):
        copy.start()
        pending.append(copy)
        return copy

    def take(copy):
        copy.wait_recv()

    local = []
    for n, (src, dst) in enumerate((
        (q_hbm, qbuf.at[0]), (k_hbm, kbuf.at[0]), (v_hbm, vbuf.at[0]), (eh_hbm, ehv), (ed_hbm, edv),
        (er_hbm, erv), (res_hbm, resv), (pin_hbm, pin), (pout_hbm, pfull.at[0]),
    )):
        copy = pltpu.make_async_copy(src, dst, lsem.at[n])
        copy.start()
        local.append(copy)

    barrier = pltpu.get_barrier_semaphore()

    greeted = [{"seq": y * NZ + lax.rem(z + r, NZ)} for r in range(1, NZ)]
    greeted += [{"seq": lax.rem(y + r, NY) * NZ + z} for r in range(1, NY)]
    greeted += [{"mp": lax.rem(x + r, NX)} for r in range(1, NX)]
    greeted += [{"section": 1 - sec}]
    for device in greeted:
        pl.semaphore_signal(barrier, inc=1, device_id=device, device_id_type=MESH)
    pl.semaphore_wait(barrier, len(greeted))

    def q_copy(d, t, half):
        cols = pl.ds(half * HALF, HALF)
        src = qbuf.at[(8 - t) % 8 if d == 0 else t, :, cols]
        dst = qbuf.at[7 - t if d == 0 else t + 1, :, cols]
        return rcopy(src, dst, q_s.at[d, t, half], q_r.at[d, t, half], zp if d == 0 else zm)

    def kv_copy(n):
        src, dst, dev = (
            (kbuf.at[0], kbuf.at[3], yp), (kbuf.at[0], kbuf.at[1], ym),
            (vbuf.at[0], vbuf.at[3], yp), (vbuf.at[0], vbuf.at[1], ym),
            (kbuf.at[3], kbuf.at[2], yp), (vbuf.at[1], vbuf.at[2], ym),
        )[n]
        return rcopy(src, dst, kv_s.at[n], kv_r.at[n], dev)

    q_copies = [[{h: q_copy(d, t, h) for h in ((0, 1) if t < 3 else (d,))} for t in range(4)] for d in range(2)]
    kv_copies = [kv_copy(n) for n in range(6)]
    local[0].wait()
    for half in range(2):
        for d in range(2):
            go(q_copies[d][0][half])
    local[1].wait()
    go(kv_copies[0])
    go(kv_copies[1])
    local[2].wait()
    go(kv_copies[2])
    go(kv_copies[3])

    def x_copies(phase, src_of, dst_of):
        return {
            r: rcopy(src_of(r), dst_of(NX - r), x_s.at[phase, r - 1], x_r.at[phase, NX - r - 1],
                     {"mp": lax.rem(x + r, NX)})
            for r in (1, 2, 3)
        }

    local[3].wait()
    local[4].wait()
    enc_copies = x_copies(0, lambda r: esend.at[r], lambda r: erecv.at[r])
    for r in (2, 1, 3, 0):
        cols = pl.ds(pl.multiple_of(lax.rem(x + r, NX) * CH, CH), CH)
        esend[r] = dot(ehv[...], edv[:, cols]).astype(BF16)
        if r:
            go(enc_copies[r])

    local[8].wait()
    core_rows = pl.ds(pl.multiple_of(sec * (PROJ // 2), PROJ // 2), PROJ // 2)
    p_copies = x_copies(9, lambda r: pfull.at[0, core_rows], lambda r: pfull.at[r, core_rows])
    pc_copies = {r: rcopy(pfull.at[r, core_rows], pfull.at[r, core_rows], pc_s.at[r - 1], pc_r.at[r - 1],
                          {"section": 1 - sec}) for r in (1, 2, 3)}
    for r in (1, 3, 2):
        go(p_copies[r])
    ids = iota((16, NSEQ * ROWS), 0)
    seg = seg_ref[...]
    below = jnp.sum(jnp.where(seg < ids, 1.0, 0.0), axis=1, keepdims=True)
    upto = jnp.sum(jnp.where(seg <= ids, 1.0, 0.0), axis=1, keepdims=True)
    lane = iota((16, HD), 1)
    tail = jnp.full((HD - 16, HD), 1e9, F32)
    segrow[0] = jnp.concatenate([jnp.broadcast_to(below, lane.shape), tail], axis=0).T
    segrow[1] = jnp.concatenate([jnp.broadcast_to(upto, lane.shape), tail], axis=0).T

    def image_columns(device):
        place = (iota((ROWS, HD), 0) * NSEQ + device).astype(F32)
        return (place >= segrow[0]) & (place < segrow[1])

    for r in range(NY):
        device = lax.rem(y + r, NY) * NZ + z
        ko[r] = jnp.where(image_columns(device), SAME, 0.0).astype(BF16)

    def forward_q(t, half):
        for d in range(2):
            if half in q_copies[d][t]:
                take(q_copies[d][t][half])
            if t < 3 and half in q_copies[d][t + 1]:
                go(q_copies[d][t + 1][half])

    def own(ref):
        return jnp.concatenate([ref[pl.ds(3 * x + i, 1), :] for i in range(3)], axis=1)

    stat_copies = x_copies(1, lambda r: estat, lambda r: estat_in.at[r])
    pad = jnp.zeros((HD - 8, HD), F32)
    row8 = iota((8, HD), 0)
    counts = cnt_ref[...].astype(F32)

    def row_y(r):
        peer = lax.rem(y + r, NY)
        return rcopy(packed.at[peer], arecv.at[y], ay_s.at[r - 1], ay_r.at[NY - r - 1], {"seq": peer * NZ + z})

    def row_z(r):
        peer = lax.rem(z + r, NZ)
        return rcopy(aturn.at[peer], alast.at[z], az_s.at[r - 1], az_r.at[NZ - r - 1], {"seq": y * NZ + peer})

    row_ys = {r: row_y(r) for r in range(1, NY)}
    row_zs = {r: row_z(r) for r in range(1, NZ)}
    def sum_encoder():
        local[5].wait()
        for r in (1, 2, 3):
            take(enc_copies[NX - r])
        enc = esend[0].astype(F32)
        for r in (1, 2, 3):
            enc = enc + erecv[r].astype(F32)
        enc = erv[...].astype(F32) + own(ls_ref) * enc
        share[...] = enc
        lane = iota((CAP, HD), 1)
        total = jnp.sum(enc, axis=1, keepdims=True)
        square = jnp.sum(enc * enc, axis=1, keepdims=True)
        packed_stat = jnp.where(lane == 0, total, jnp.where(lane == 1, square, 0.0))
        for b in range(2):
            estat[:, b * HD:(b + 1) * HD] = packed_stat[b * HD:(b + 1) * HD].T[0:8]
        for r in (2, 1, 3):
            go(stat_copies[r])


    def send_rows():
        for r in (1, 2, 3):
            take(stat_copies[NX - r])
        both = estat[...]
        for r in (1, 2, 3):
            both = both + estat_in[r]
        mean = both[0:1] * (1.0 / ENC_D)
        scale = lax.rsqrt(both[1:2] * (1.0 / ENC_D) - mean * mean + 1e-6)
        gain = own(gain_ref)
        bias = own(bias_ref)
        parts = []
        for b in range(2):
            cut = slice(b * HD, (b + 1) * HD)
            rows = jnp.where(row8 == 0, mean[:, cut], jnp.where(row8 == 1, scale[:, cut], 0.0))
            cols = jnp.concatenate([rows, pad], axis=0).T
            parts.append((((share[cut] - cols[:, 0:1]) * cols[:, 1:2]) * gain + bias).astype(BF16))
        feature = jnp.concatenate(parts, axis=0)
        before = jnp.sum(jnp.where(iota((1, NSEQ), 1) < seq, counts, 0.0), axis=1, keepdims=True).astype(I32)
        row = iota((CAP, CAP), 0)
        wanted = (row & 7) * NSEQ + (((row >> 3) - before) & (NSEQ - 1))
        permutation = jnp.where(iota((CAP, CAP), 1) == wanted, 1.0, 0.0).astype(BF16)
        packed[...] = dot(permutation, feature).reshape(NY, NZ, 8, CH)

        for r in (2, 1, 3):
            go(row_ys[r])
        arecv[pl.ds(y, 1)] = packed[pl.ds(y, 1)]

    def attend(r):
        device = y * NZ + lax.rem(z + r, NZ)
        image = jnp.where(image_columns(device), 1.0, 0.0).astype(BF16)
        keys_image = ko[...].reshape(NY * ROWS, HD)
        for h in range(HEADS):
            cols = slice(h * HD, (h + 1) * HD)
            keys = jnp.concatenate([kbuf[:, :, cols].reshape(NY * ROWS, HD), keys_image], axis=1)
            scores = dot(keys, jnp.concatenate([qbuf[r, :, cols], image], axis=1), 1, 1)
            best = jnp.max(scores, axis=0, keepdims=True)
            prob = jnp.exp2((scores - best) * EXP_SCALE)
            half, i = h // 3, h % 3
            stats[r, half, i:i + 1] = best * EXP_SCALE
            stats[r, half, 3 + i:4 + i] = jnp.sum(prob, axis=0, keepdims=True)
            opart[r, half, i * HD:(i + 1) * HD] = dot(vt[cols], prob.astype(BF16)).astype(BF16)

    def attend_two(k):
        def one(i, c):
            attend(4 + k * (1 - 2 * i))
            return c

        lax.fori_loop(0, 2, one, 0)

    def attend_one(r):
        lax.fori_loop(r, r + 1, lambda i, c: (attend(i), c)[1], 0)

    def turn_values(r):
        vt[:, r * ROWS:(r + 1) * ROWS] = vbuf[r].T

    def o_copy(d, t, half):
        r = 4 - t if d == 0 else 4 + t
        dev = zp if d == 0 else zm
        return (rcopy(opart.at[r, half], oin.at[d, t, half], o_s.at[d, t, half], o_r.at[d, t, half], dev),
                rcopy(stats.at[r, half], sin.at[d, t, half], os_s.at[d, t, half], os_r.at[d, t, half], dev))

    o_copies = [[{h: o_copy(d, t, h) for h in ((0, 1) if t else (d,))} for t in range(4)] for d in range(2)]

    def go_o(d, t, half):
        for copy in o_copies[d][t][half]:
            go(copy)

    def take_o(d, t, half):
        for copy in o_copies[d][t][half]:
            take(copy)

    forward_q(0, 0)
    forward_q(0, 1)
    take(kv_copies[0])
    go(kv_copies[4])
    take(kv_copies[1])
    forward_q(1, 0)
    take(kv_copies[2])
    take(kv_copies[3])
    go(kv_copies[5])
    forward_q(1, 1)
    for r in (0, 1, 3):
        turn_values(r)
    forward_q(2, 0)
    sum_encoder()
    forward_q(2, 1)
    for n in (4, 5):
        take(kv_copies[n])
    turn_values(2)
    attend_two(1)
    forward_q(3, 0)
    forward_q(3, 1)
    attend_one(4)
    for d in range(2):
        go_o(d, 0, d)
    for d in range(2):
        go_o(d, 1, 1 - d)
    send_rows()
    for r in (1, 3, 2):
        take(p_copies[NX - r])
        go(pc_copies[r])
    attend_two(2)

    def merge(r, d, t, half):
        mine, other = stats[r, half], sin[d, t, half]
        for i in range(3):
            m0, m1 = mine[i:i + 1], other[i:i + 1]
            best = jnp.maximum(m0, m1)
            f0, f1 = jnp.exp2(m0 - best), jnp.exp2(m1 - best)
            rows = slice(i * HD, (i + 1) * HD)
            mixed = opart[r, half, rows].astype(F32) * f0 + oin[d, t, half, rows].astype(F32) * f1
            opart[r, half, rows] = mixed.astype(BF16)
            stats[r, half, i:i + 1] = best
            stats[r, half, 3 + i:4 + i] = mine[3 + i:4 + i] * f0 + other[3 + i:4 + i] * f1

    for t in (1, 2, 3):
        if t == 2:
            attend_two(3)
        if t == 3:
            attend_one(0)
        for turn in range(2):
            for d in range(2):
                half = d if turn else 1 - d
                if t == 1 and not turn:
                    continue
                take_o(d, t - 1, half)
                merge(4 - t if d == 0 else 4 + t, d, t - 1, half)
                go_o(d, t, half)
    for r in (1, 2, 3):
        take(row_ys[NY - r])
    for n in range(NZ):
        aturn[n] = arecv[:, n].reshape(NY * 8, CH).astype(BF16)
    alast[pl.ds(z, 1)] = aturn[pl.ds(z, 1)]
    for half in range(2):
        for d in range(2):
            take_o(d, 3, half)
            merge(0, d, 3, half)
    for r in (4, 3, 5, 2, 6, 1, 7):
        go(row_zs[r])
    local[6].wait()
    for h in range(HEADS):
        half, i = h // 3, h % 3
        cols = slice(h * HD, (h + 1) * HD)
        attn = opart[0, half, i * HD:(i + 1) * HD].astype(F32) / stats[0, half, 3 + i:4 + i]
        attn = attn.T.astype(BF16).astype(F32)
        hidden[:, cols] = (resv[:, cols].astype(F32) + attn).astype(BF16)

    local[7].wait()
    f_copies = []
    for c in range(2):
        cols = slice(c * 1024, (c + 1) * 1024)
        fpart[:, :, cols] = dot(hidden[...], pin[:, cols]).astype(BF16).reshape(NX, 32, 1024)
        f_copies.append(x_copies(
            2 + c, lambda r: fpart.at[lax.rem(x + r, NX), :, cols], lambda r: frecv.at[r, :, cols]))
        for r in (2, 1, 3):
            go(f_copies[c][r])
    column = iota((NSEQ, CAP), 1)
    e_of = ((column >> 3) & (NY - 1)) * NZ + (column >> 5)
    device = iota((NSEQ, CAP), 0)
    counts8 = jnp.broadcast_to(counts, (8, NSEQ)).astype(BF16)
    start = dot(counts8, jnp.where(device < e_of, 1.0, 0.0).astype(BF16))[0:1]
    count = dot(counts8, jnp.where(device == e_of, 1.0, 0.0).astype(BF16))[0:1]
    low = start + ((iota((1, CAP), 1) & 7) * NSEQ).astype(F32)
    high = jnp.minimum(low + float(NSEQ), start + count)
    place = (iota((ROWS, CAP), 0) * NSEQ + seq).astype(F32)
    chosen = jnp.where((place >= low) & (place < high), 1.0, 0.0).astype(BF16)

    for r in range(1, NZ):
        take(row_zs[NZ - r])
    tsend[...] = dot(chosen, alast[...].reshape(CAP, CH)).astype(BF16).reshape(NX, 32, CH)
    t_copies = x_copies(5, lambda r: tsend.at[lax.rem(x + r, NX)], lambda r: tgt.at[r])
    for r in (2, 1, 3):
        go(t_copies[r])
    tgt[0] = tsend[x]
    column_weight[...] = jnp.broadcast_to(aw_ref[...], (ROWS, ROWS)).T
    for c in range(2):
        cols = slice(c * 1024, (c + 1) * 1024)
        for r in (1, 2, 3):
            take(f_copies[c][NX - r])
        value = fpart[x, :, cols].astype(F32)
        for r in (1, 2, 3):
            value = value + frecv[r, :, cols].astype(F32)
        first[:, cols] = value
        actall[x, :, cols] = (value * jax.nn.sigmoid(value)).astype(BF16)
    act_copies = x_copies(4, lambda r: actall.at[x], lambda r: actall.at[x])
    for r in (2, 1, 3):
        go(act_copies[r])
    act = actall[x]
    for r in range(NX):
        if r:
            take(pc_copies[r])
        second[r] = dot(act, pfull[r])
    for r in (1, 2, 3):
        take(t_copies[NX - r])
    inner = square_z = square_f = 0.0
    for r in range(NX):
        tf = tgt[r].astype(F32)
        inner = inner + jnp.sum(second[r] * tf, axis=1, keepdims=True)
        square_z = square_z + jnp.sum(second[r] * second[r], axis=1, keepdims=True)
        square_f = square_f + jnp.sum(tf * tf, axis=1, keepdims=True)
    norm_z = jnp.sqrt(square_z + 1e-6)
    norm_f = jnp.sqrt(square_f + 1e-6)
    aligned = inner / (norm_z * norm_f)
    weight = column_weight[pl.ds(pl.multiple_of(x * 32, 32), 32), 0:1]
    by_target = -weight / (norm_z * norm_f)
    by_second = weight * aligned / (norm_z * norm_z)
    b_copies = x_copies(6, lambda r: bsend.at[r], lambda r: backall.at[x])
    for r in (2, 1, 3, 0):
        bsend[r] = (by_target * tgt[r].astype(F32) + by_second * second[r]).astype(BF16)
        if r:
            go(b_copies[r])
    backall[x] = bsend[0]
    alall[x] = jnp.broadcast_to(aligned, (32, HD))
    l_copies = x_copies(7, lambda r: alall.at[x], lambda r: alall.at[x])
    for r in (2, 1, 3):
        go(l_copies[r])
    upstream = dot(bsend[0], pfull[0], 1, 1)
    for r in (1, 2, 3):
        upstream = upstream + dot(bsend[r], pfull[r], 1, 1)
    value = first[...]
    sig = jax.nn.sigmoid(value)
    dall[x] = (upstream * sig * (1.0 + value * (1.0 - sig))).astype(BF16)
    d_copies = x_copies(8, lambda r: dall.at[x], lambda r: dall.at[x])
    for r in (2, 1, 3):
        go(d_copies[r])
    for r in (1, 2, 3):
        take(act_copies[NX - r])
        take(b_copies[NX - r])
        take(l_copies[NX - r])
    al_ref[...] = alall[...].reshape(ROWS, HD).T[0:1]

    def reduction(n, left, right, xs, xr, hs, yr, zs, zr, out):
        def across(jj):
            return rcopy(xs.at[jj], xr.at[jj], gx_s.at[n, jj], gx_r.at[n, jj], {"section": 1 - sec})

        def y_copy(r):
            peer = lax.rem(y + r, NY)
            return rcopy(hs.at[peer], yr.at[NY - r], gy_s.at[n, r - 1], gy_r.at[n, NY - r - 1],
                         {"seq": peer * NZ + z})

        def z_copy(r):
            peer = lax.rem(z + r, NZ)
            return rcopy(zs.at[peer], zr.at[NZ - r], gz_s.at[n, r - 1], gz_r.at[n, NZ - r - 1],
                         {"seq": y * NZ + peer})

        acrosses = [across(jj) for jj in range(2)]
        y_copies = {r: y_copy(r) for r in range(1, NY)}
        z_copies = {r: z_copy(r) for r in range(1, NZ)}

        def product(j):
            cols = pl.ds(pl.multiple_of(j * PART, PART), PART)
            return dot(left[:, :, cols].reshape(ROWS, PART), right[...].reshape(ROWS, -1), 0, 0).astype(BF16)

        def start():
            for jj in range(2):
                xs[jj] = product(2 * (1 - sec) + jj)
                go(acrosses[jj])
            for jj in range(2):
                value = product(2 * sec + jj)
                for b in range(2):
                    hs[2 * jj + b] = value[b * 256:(b + 1) * 256]

        def middle():
            for jj in range(2):
                take(acrosses[jj])
                for b in range(2):
                    hs[2 * jj + b] = (hs[2 * jj + b].astype(F32)
                                      + xr[jj, b * 256:(b + 1) * 256].astype(F32)).astype(BF16)
            for r in (2, 1, 3):
                go(y_copies[r])

        def late():
            for r in (1, 2, 3):
                take(y_copies[NY - r])
            value = hs[y].astype(F32)
            for r in (1, 2, 3):
                value = value + yr[r].astype(F32)
            zs[...] = value.astype(BF16).reshape(zs.shape)
            for r in (4, 3, 5, 2, 6, 1, 7):
                go(z_copies[r])

        def end():
            for r in range(1, NZ):
                take(z_copies[NZ - r])
            value = zs[z].astype(F32)
            for r in range(1, NZ):
                value = value + zr[r].astype(F32)
            out[...] = value

        return start, middle, late, end

    go_steps = reduction(0, actall, backall, go_x, go_xr, go_h, go_yr, go_z, go_zr, go_ref)
    go_steps[0]()

    go_steps[1]()
    for r in (1, 2, 3):
        take(d_copies[NX - r])

    def across(jj):
        return rcopy(gi_x.at[jj], gi_xr.at[jj], gx_s.at[1, jj], gx_r.at[1, jj], {"section": 1 - sec})

    def product(j):
        cols = pl.ds(pl.multiple_of(j * PART, PART), PART)
        return dot(dall[:, :, cols].reshape(ROWS, PART), hidden[...], 0, 0).astype(BF16)

    def ya_copy(r):
        peer = lax.rem(y + r, NY)
        return rcopy(a_y.at[peer], a_yr.at[NY - r], gy_s.at[1, r - 1], gy_r.at[1, NY - r - 1], {"seq": peer * NZ + z})

    def za_copy(r):
        peer = lax.rem(z + r, NZ)
        return rcopy(a_z.at[peer], a_zr.at[NZ - r], gz_s.at[1, r - 1], gz_r.at[1, NZ - r - 1], {"seq": y * NZ + peer})

    def yb_copy(r):
        peer = lax.rem(y + r, NY)
        return rcopy(b_y.at[peer], b_yr.at[NY - r], gy_s.at[2, r - 1], gy_r.at[2, NY - r - 1], {"seq": peer * NZ + z})

    def zb_copy(d, t, half):
        chunk = lax.rem(z + (4 - t if d == 0 else 4 + t), NZ)
        part = pl.ds(2 * half, 2)
        return rcopy(b_z.at[chunk, part], b_in.at[d, t, part], gb_s.at[d, t, half], gb_r.at[d, t, half],
                     zp if d == 0 else zm)

    acrosses = [across(jj) for jj in range(2)]
    ya_copies = {r: ya_copy(r) for r in range(1, NY)}
    za_copies = {r: za_copy(r) for r in range(1, NZ)}
    yb_copies = {r: yb_copy(r) for r in range(1, NY)}
    zb_copies = [[{h: zb_copy(d, t, h) for h in ((0, 1) if t else (d,))} for t in range(4)] for d in range(2)]
    for jj in range(2):
        gi_x[jj] = product(2 * (1 - sec) + jj)
        go(acrosses[jj])
    for jj in range(2):
        gi_h[jj] = product(2 * sec + jj)
    for jj in range(2):
        take(acrosses[jj])
        for b in range(2):
            rows = slice(b * 256, (b + 1) * 256)
            value = (gi_h[jj, rows].astype(F32) + gi_xr[jj, rows].astype(F32)).astype(BF16)
            a_y[2 * jj + b] = value[:, 0:HALF]
            for n in range(NZ):
                b_z[n, 2 * jj + b] = value[n * 32:(n + 1) * 32, HALF:WIDTH]

    def go_b(d, t, half):
        go(zb_copies[d][t][half])

    def merge_b(d, t, half):
        take(zb_copies[d][t][half])
        chunk = lax.rem(z + (3 - t if d == 0 else 5 + t), NZ)
        part = pl.ds(2 * half, 2)
        b_z[chunk, part] = (b_z[chunk, part].astype(F32) + b_in[d, t, part].astype(F32)).astype(BF16)

    for d in range(2):
        go_b(d, 0, d)
    for r in (2, 1, 3):
        go(ya_copies[r])
    for d in range(2):
        go_b(d, 1, 1 - d)
    for d in range(2):
        merge_b(d, 0, d)
        go_b(d, 1, d)
    go_steps[2]()
    for turn in range(2):
        for d in range(2):
            half = d if turn else 1 - d
            merge_b(d, 1, half)
            go_b(d, 2, half)
    for r in (1, 2, 3):
        take(ya_copies[NY - r])
    value = a_y[y].astype(F32)
    for r in (1, 2, 3):
        value = value + a_yr[r].astype(F32)
    a_z[...] = value.astype(BF16).reshape(NZ, 32, HALF)
    for r in (4, 3, 5, 2, 6, 1, 7):
        go(za_copies[r])
    for turn in range(2):
        for d in range(2):
            half = d if turn else 1 - d
            merge_b(d, 2, half)
            go_b(d, 3, half)
    for half in range(2):
        for d in range(2):
            merge_b(d, 3, half)
    b_y[...] = b_z[z]
    for r in (2, 1, 3):
        go(yb_copies[r])
    go_steps[3]()
    for r in range(1, NZ):
        take(za_copies[NZ - r])
    value = a_z[z].astype(F32)
    for r in range(1, NZ):
        value = value + a_zr[r].astype(F32)
    gi_ref[:, 0:HALF] = value
    for r in (1, 2, 3):
        take(yb_copies[NY - r])
    value = b_y[y].astype(F32)
    for r in (1, 2, 3):
        value = value + b_yr[r].astype(F32)
    gi_ref[:, HALF:WIDTH] = value

    for copy in pending:
        copy.wait_send()


def body(
    queries, keys, values, residual, segment_ids, enc_counts, enc_hidden, enc_down, enc_resid,
    layer_scale, norm_gain, norm_bias, proj_in, proj_out, align_weight,
):
    anywhere = pl.BlockSpec(memory_space=pl.ANY)
    vmem = pl.BlockSpec(memory_space=pltpu.VMEM)
    V, D = pltpu.VMEM, pltpu.SemaphoreType.DMA
    scratch = [
        V((NZ, ROWS, WIDTH), BF16), V((NY, ROWS, WIDTH), BF16), V((NY, ROWS, WIDTH), BF16),
        V((WIDTH, NY * ROWS), BF16), V((NY, ROWS, HD), BF16), V((ROWS, WIDTH), BF16),
        V((CAP, FF), BF16), V((FF, ENC_D), BF16), V((CAP, CH), BF16),
        V((WIDTH, PROJ), BF16), V((NX, PROJ, CH), BF16),
        V((NZ, 2, HALF, HD), BF16), V((NZ, 2, 8, HD), F32),
        V((2, 4, 2, HALF, HD), BF16), V((2, 4, 2, 8, HD), F32),
        V((NX, CAP, CH), BF16), V((NX, CAP, CH), BF16), V((CAP, CH), F32),
        V((8, CAP), F32), V((NX, 8, CAP), F32),
        V((NY, NZ, 8, CH), F32), V((NY, NZ, 8, CH), F32), V((NZ, 32, CH), BF16), V((NZ, 32, CH), BF16),
        V((NX, 32, CH), BF16), V((NX, 32, CH), BF16),
        V((ROWS, WIDTH), BF16), V((NX, 32, PROJ), BF16), V((NX, 32, PROJ), BF16), V((32, PROJ), F32),
        V((NX, 32, PROJ), BF16), V((NX, 32, CH), F32), V((NX, 32, CH), BF16), V((NX, 32, CH), BF16),
        V((NX, 32, HD), F32), V((NX, 32, PROJ), BF16), V((ROWS, ROWS), F32),
        V((2, HD, HD), F32),
    ]
    scratch += [
        V((2, PART, CH), BF16), V((2, PART, CH), BF16), V((NY, 256, CH), BF16),
        V((NY, 256, CH), BF16), V((NZ, 32, CH), BF16), V((NZ, 32, CH), BF16),
        V((2, PART, WIDTH), BF16), V((2, PART, WIDTH), BF16), V((2, PART, WIDTH), BF16),
        V((NY, 256, HALF), BF16), V((NY, 256, HALF), BF16), V((NZ, 32, HALF), BF16), V((NZ, 32, HALF), BF16),
        V((NZ, NY, 32, HALF), BF16), V((2, 4, NY, 32, HALF), BF16), V((NY, 32, HALF), BF16), V((NY, 32, HALF), BF16),
    ]
    scratch += [
        D((9,)), D((2, 4, 2)), D((2, 4, 2)), D((6,)), D((6,)),
        D((2, 4, 2)), D((2, 4, 2)), D((2, 4, 2)), D((2, 4, 2)),
        D((10, 3)), D((10, 3)), D((3,)), D((3,)), D((3,)), D((3,)), D((7,)), D((7,)),
        D((2, 2)), D((2, 2)), D((3, 3)), D((3, 3)), D((2, 7)), D((2, 7)), D((2, 4, 2)), D((2, 4, 2)),
    ]
    aligned, grad_in_t, grad_out = pl.pallas_call(
        kernel,
        out_shape=(
            jax.ShapeDtypeStruct((1, ROWS), F32),
            jax.ShapeDtypeStruct((32, WIDTH), F32),
            jax.ShapeDtypeStruct((32, CH), F32),
        ),
        in_specs=[anywhere] * 4 + [vmem] * 2 + [anywhere] * 3 + [vmem] * 3 + [anywhere] * 2 + [vmem],
        out_specs=(vmem, vmem, vmem),
        scratch_shapes=scratch,
        compiler_params=pltpu.CompilerParams(
            collective_id=0, has_side_effects=True, vmem_limit_bytes=56 * 1024 * 1024
        ),
        name="align",
    )(
        queries, keys, values, residual, segment_ids, enc_counts, enc_hidden, enc_down, enc_resid,
        layer_scale.reshape(-1, HD), norm_gain.reshape(-1, HD), norm_bias.reshape(-1, HD),
        proj_in, proj_out, align_weight.reshape(1, -1),
    )

    def hand_on(a, b, c, a_out, b_out, c_out):
        a_out[...] = a[...]
        b_out[...] = b[...]
        c_out[...] = c[...]

    aligned, grad_in_t, grad_out = pl.pallas_call(
        hand_on,
        out_shape=tuple(jax.ShapeDtypeStruct(v.shape, F32) for v in (aligned, grad_in_t, grad_out)),
        in_specs=[vmem] * 3,
        out_specs=(vmem, vmem, vmem),
        name="hand_on",
    )(aligned, grad_in_t, grad_out)
    return aligned.reshape(-1), grad_in_t, grad_out


def solution(mesh):
    return jax.shard_map(
        body,
        mesh=mesh,
        in_specs=(
            P(("section", "seq"), "mp"),
            P(("section", "seq"), "mp"),
            P(("section", "seq"), "mp"),
            P(("section", "seq"), "mp"),
            P("section", None),
            P("section", None),
            P(("section", "seq"), "mp"),
            P("mp", None),
            P(("section", "seq"), "mp"),
            P(),
            P(),
            P(),
            P("mp", None),
            P(None, "mp"),
            P(("section", "seq")),
        ),
        out_specs=(P(("section", "seq")), P(("section", "seq"), "mp"), P(("section", "seq"), "mp")),
        check_vma=False,
    )
```

```python
import math

import jax
import jax.numpy as jnp
from jax import lax
from jax.experimental import pallas as pl
from jax.experimental.pallas import tpu as pltpu
from jax.sharding import PartitionSpec as P

MESH = pl.DeviceIdType.MESH
F32, BF16, I32 = jnp.float32, jnp.bfloat16, jnp.int32
HD = 128
ENC_D = 1536
NX, NY, NZ = 4, 4, 8
NSEQ = NY * NZ
ROWS = 128
CAP = 256
WIDTH = 768
HEADS = 6
HALF = 384
CH = 384
FF = 1024
PROJ = 2048
PART = 512
SAME = 8192.0
EXP_SCALE = math.log2(math.e) * HD ** (-0.5)


def rcopy(src, dst, send, recv, dev):
    return pltpu.make_async_remote_copy(
        src_ref=src, dst_ref=dst, send_sem=send, recv_sem=recv, device_id=dev, device_id_type=MESH
    )


def iota(shape, dim):
    return lax.broadcasted_iota(I32, shape, dim)


def dot(a, b, ca=1, cb=0):
    return lax.dot_general(a, b, (((ca,), (cb,)), ((), ())), preferred_element_type=F32)


def kernel(
    q_hbm, k_hbm, v_hbm, res_hbm, seg_ref, cnt_ref, eh_hbm, ed_hbm, er_hbm, ls_ref, gain_ref, bias_ref,
    pin_hbm, pout_hbm, aw_ref,
    al_ref, gi_ref, go_ref,
    qbuf, kbuf, vbuf, vt, ko, resv, ehv, edv, erv, pin, pfull,
    opart, stats, oin, sin,
    esend, erecv, share, estat, estat_in, packed, arecv, aturn, alast, tsend, tgt,
    hgrp, fpart, frecv, first, act_rows, second, bsend, bgrp, alall, column_weight,
    apiece, agrp, dpiece, dgrp, gz, gz_in, segrow,
    lsem, q_s, q_r, kv_s, kv_r, o_s, o_r, os_s, os_r, x_s, x_r, pc_s, pc_r, ay_s, ay_r, az_s, az_r,
    gx_s, gx_r, gy_s, gy_r, gz_s, gz_r, gg_s, gg_r,
):
    sec = lax.axis_index("section")
    seq = lax.axis_index("seq")
    x = lax.axis_index("mp")
    y = seq // NZ
    z = lax.rem(seq, NZ)
    zp = {"seq": y * NZ + lax.rem(z + 1, NZ)}
    zm = {"seq": y * NZ + lax.rem(z + NZ - 1, NZ)}
    yp = {"seq": lax.rem(y + 1, NY) * NZ + z}
    ym = {"seq": lax.rem(y + NY - 1, NY) * NZ + z}
    pending = []

    def go(copy):
        copy.start()
        pending.append(copy)
        return copy

    def take(copy):
        copy.wait_recv()

    local = []
    for n, (src, dst) in enumerate((
        (q_hbm, qbuf.at[0]), (k_hbm, kbuf.at[0]), (v_hbm, vbuf.at[0]), (eh_hbm, ehv), (ed_hbm, edv),
        (er_hbm, erv), (res_hbm, resv), (pin_hbm, pin), (pout_hbm, pfull.at[0]),
    )):
        copy = pltpu.make_async_copy(src, dst, lsem.at[n])
        copy.start()
        local.append(copy)

    barrier = pltpu.get_barrier_semaphore()

    greeted = [{"seq": y * NZ + lax.rem(z + r, NZ)} for r in range(1, NZ)]
    greeted += [{"seq": lax.rem(y + r, NY) * NZ + z} for r in range(1, NY)]
    greeted += [{"mp": lax.rem(x + r, NX)} for r in range(1, NX)]
    greeted += [{"section": 1 - sec, "seq": lax.rem(y + r, NY) * NZ + z} for r in range(NY)]
    for device in greeted:
        pl.semaphore_signal(barrier, inc=1, device_id=device, device_id_type=MESH)
    pl.semaphore_wait(barrier, len(greeted))

    def q_copy(d, t, half):
        cols = pl.ds(half * HALF, HALF)
        src = qbuf.at[(8 - t) % 8 if d == 0 else t, :, cols]
        dst = qbuf.at[7 - t if d == 0 else t + 1, :, cols]
        return rcopy(src, dst, q_s.at[d, t, half], q_r.at[d, t, half], zp if d == 0 else zm)

    def kv_copy(n):
        src, dst, dev = (
            (kbuf.at[0], kbuf.at[3], yp), (kbuf.at[0], kbuf.at[1], ym),
            (vbuf.at[0], vbuf.at[3], yp), (vbuf.at[0], vbuf.at[1], ym),
            (kbuf.at[3], kbuf.at[2], yp), (vbuf.at[1], vbuf.at[2], ym),
        )[n]
        return rcopy(src, dst, kv_s.at[n], kv_r.at[n], dev)

    q_copies = [[{h: q_copy(d, t, h) for h in ((0, 1) if t < 3 else (d,))} for t in range(4)] for d in range(2)]
    kv_copies = [kv_copy(n) for n in range(6)]
    local[0].wait()
    for half in range(2):
        for d in range(2):
            go(q_copies[d][0][half])
    local[1].wait()
    go(kv_copies[0])
    go(kv_copies[1])
    local[2].wait()
    go(kv_copies[2])
    go(kv_copies[3])

    def x_copies(phase, src_of, dst_of):
        return {
            r: rcopy(src_of(r), dst_of(NX - r), x_s.at[phase, r - 1], x_r.at[phase, NX - r - 1],
                     {"mp": lax.rem(x + r, NX)})
            for r in (1, 2, 3)
        }

    def y_copies(n, ref_of):
        return {
            r: rcopy(ref_of(), ref_of(), gy_s.at[n, r - 1], gy_r.at[n, NY - r - 1],
                     {"seq": lax.rem(y + r, NY) * NZ + z})
            for r in (1, 2, 3)
        }

    def core_copy(n, ref):
        return rcopy(ref, ref, gx_s.at[n], gx_r.at[n], {"section": 1 - sec})

    def group_copies(n, pieces, group):
        copies = []
        for ds in range(2):
            for r in range(NY):
                if ds or r:
                    to_sec, to_y = lax.rem(sec + ds, 2), lax.rem(y + r, NY)
                    copies.append(rcopy(
                        pieces.at[to_sec, to_y], group.at[x, sec, y],
                        gg_s.at[n, ds * NY + r], gg_r.at[n, ds * NY + (NY - r) % NY],
                        {"section": to_sec, "seq": to_y * NZ + z}))
        return copies

    def send_pieces(copies, rows, pieces, group):
        for a in range(2):
            for b in range(NY):
                pieces[a, b] = rows[:, (a * NY + b) * 256:(a * NY + b + 1) * 256]
        for copy in copies:
            go(copy)
        group[x, sec, y] = pieces[sec, y]

    local[3].wait()
    local[4].wait()
    enc_copies = x_copies(0, lambda r: esend.at[r], lambda r: erecv.at[r])
    for r in (2, 1, 3, 0):
        cols = pl.ds(pl.multiple_of(lax.rem(x + r, NX) * CH, CH), CH)
        esend[r] = dot(ehv[...], edv[:, cols]).astype(BF16)
        if r:
            go(enc_copies[r])

    local[8].wait()
    core_rows = pl.ds(pl.multiple_of(sec * (PROJ // 2), PROJ // 2), PROJ // 2)
    p_copies = x_copies(9, lambda r: pfull.at[0, core_rows], lambda r: pfull.at[r, core_rows])
    pc_copies = {r: rcopy(pfull.at[r, core_rows], pfull.at[r, core_rows], pc_s.at[r - 1], pc_r.at[r - 1],
                          {"section": 1 - sec}) for r in (1, 2, 3)}
    for r in (1, 3, 2):
        go(p_copies[r])
    ids = iota((16, NSEQ * ROWS), 0)
    seg = seg_ref[...]
    below = jnp.sum(jnp.where(seg < ids, 1.0, 0.0), axis=1, keepdims=True)
    upto = jnp.sum(jnp.where(seg <= ids, 1.0, 0.0), axis=1, keepdims=True)
    lane = iota((16, HD), 1)
    tail = jnp.full((HD - 16, HD), 1e9, F32)
    segrow[0] = jnp.concatenate([jnp.broadcast_to(below, lane.shape), tail], axis=0).T
    segrow[1] = jnp.concatenate([jnp.broadcast_to(upto, lane.shape), tail], axis=0).T

    def image_columns(device):
        place = (iota((ROWS, HD), 0) * NSEQ + device).astype(F32)
        return (place >= segrow[0]) & (place < segrow[1])

    for r in range(NY):
        device = lax.rem(y + r, NY) * NZ + z
        ko[r] = jnp.where(image_columns(device), SAME, 0.0).astype(BF16)

    def forward_q(t, half):
        for d in range(2):
            if half in q_copies[d][t]:
                take(q_copies[d][t][half])
            if t < 3 and half in q_copies[d][t + 1]:
                go(q_copies[d][t + 1][half])

    def own(ref):
        return jnp.concatenate([ref[pl.ds(3 * x + i, 1), :] for i in range(3)], axis=1)

    stat_copies = x_copies(1, lambda r: estat, lambda r: estat_in.at[r])
    pad = jnp.zeros((HD - 8, HD), F32)
    row8 = iota((8, HD), 0)
    counts = cnt_ref[...].astype(F32)

    def row_y(r):
        peer = lax.rem(y + r, NY)
        return rcopy(packed.at[peer], arecv.at[y], ay_s.at[r - 1], ay_r.at[NY - r - 1], {"seq": peer * NZ + z})

    def row_z(r):
        peer = lax.rem(z + r, NZ)
        return rcopy(aturn.at[peer], alast.at[z], az_s.at[r - 1], az_r.at[NZ - r - 1], {"seq": y * NZ + peer})

    row_ys = {r: row_y(r) for r in range(1, NY)}
    row_zs = {r: row_z(r) for r in range(1, NZ)}
    def sum_encoder():
        local[5].wait()
        for r in (1, 2, 3):
            take(enc_copies[NX - r])
        enc = esend[0].astype(F32)
        for r in (1, 2, 3):
            enc = enc + erecv[r].astype(F32)
        enc = erv[...].astype(F32) + own(ls_ref) * enc
        share[...] = enc
        lane = iota((CAP, HD), 1)
        total = jnp.sum(enc, axis=1, keepdims=True)
        square = jnp.sum(enc * enc, axis=1, keepdims=True)
        packed_stat = jnp.where(lane == 0, total, jnp.where(lane == 1, square, 0.0))
        for b in range(2):
            estat[:, b * HD:(b + 1) * HD] = packed_stat[b * HD:(b + 1) * HD].T[0:8]
        for r in (2, 1, 3):
            go(stat_copies[r])


    def send_rows():
        for r in (1, 2, 3):
            take(stat_copies[NX - r])
        both = estat[...]
        for r in (1, 2, 3):
            both = both + estat_in[r]
        mean = both[0:1] * (1.0 / ENC_D)
        scale = lax.rsqrt(both[1:2] * (1.0 / ENC_D) - mean * mean + 1e-6)
        gain = own(gain_ref)
        bias = own(bias_ref)
        parts = []
        for b in range(2):
            cut = slice(b * HD, (b + 1) * HD)
            rows = jnp.where(row8 == 0, mean[:, cut], jnp.where(row8 == 1, scale[:, cut], 0.0))
            cols = jnp.concatenate([rows, pad], axis=0).T
            parts.append((((share[cut] - cols[:, 0:1]) * cols[:, 1:2]) * gain + bias).astype(BF16))
        feature = jnp.concatenate(parts, axis=0)
        before = jnp.sum(jnp.where(iota((1, NSEQ), 1) < seq, counts, 0.0), axis=1, keepdims=True).astype(I32)
        row = iota((CAP, CAP), 0)
        wanted = (row & 7) * NSEQ + (((row >> 3) - before) & (NSEQ - 1))
        permutation = jnp.where(iota((CAP, CAP), 1) == wanted, 1.0, 0.0).astype(BF16)
        packed[...] = dot(permutation, feature).reshape(NY, NZ, 8, CH)

        for r in (2, 1, 3):
            go(row_ys[r])
        arecv[pl.ds(y, 1)] = packed[pl.ds(y, 1)]

    def attend(r):
        device = y * NZ + lax.rem(z + r, NZ)
        image = jnp.where(image_columns(device), 1.0, 0.0).astype(BF16)
        keys_image = ko[...].reshape(NY * ROWS, HD)
        for h in range(HEADS):
            cols = slice(h * HD, (h + 1) * HD)
            keys = jnp.concatenate([kbuf[:, :, cols].reshape(NY * ROWS, HD), keys_image], axis=1)
            scores = dot(keys, jnp.concatenate([qbuf[r, :, cols], image], axis=1), 1, 1)
            best = jnp.max(scores, axis=0, keepdims=True)
            prob = jnp.exp2((scores - best) * EXP_SCALE)
            half, i = h // 3, h % 3
            stats[r, half, i:i + 1] = best * EXP_SCALE
            stats[r, half, 3 + i:4 + i] = jnp.sum(prob, axis=0, keepdims=True)
            opart[r, half, i * HD:(i + 1) * HD] = dot(vt[cols], prob.astype(BF16)).astype(BF16)

    def attend_two(k):
        def one(i, c):
            attend(4 + k * (1 - 2 * i))
            return c

        lax.fori_loop(0, 2, one, 0)

    def attend_one(r):
        lax.fori_loop(r, r + 1, lambda i, c: (attend(i), c)[1], 0)

    def turn_values(r):
        vt[:, r * ROWS:(r + 1) * ROWS] = vbuf[r].T

    def o_copy(d, t, half):
        r = 4 - t if d == 0 else 4 + t
        dev = zp if d == 0 else zm
        return (rcopy(opart.at[r, half], oin.at[d, t, half], o_s.at[d, t, half], o_r.at[d, t, half], dev),
                rcopy(stats.at[r, half], sin.at[d, t, half], os_s.at[d, t, half], os_r.at[d, t, half], dev))

    o_copies = [[{h: o_copy(d, t, h) for h in ((0, 1) if t else (d,))} for t in range(4)] for d in range(2)]

    def go_o(d, t, half):
        for copy in o_copies[d][t][half]:
            go(copy)

    def take_o(d, t, half):
        for copy in o_copies[d][t][half]:
            take(copy)

    forward_q(0, 0)
    forward_q(0, 1)
    take(kv_copies[0])
    go(kv_copies[4])
    take(kv_copies[1])
    forward_q(1, 0)
    take(kv_copies[2])
    take(kv_copies[3])
    go(kv_copies[5])
    forward_q(1, 1)
    for r in (0, 1, 3):
        turn_values(r)
    forward_q(2, 0)
    sum_encoder()
    forward_q(2, 1)
    for n in (4, 5):
        take(kv_copies[n])
    turn_values(2)
    attend_two(1)
    forward_q(3, 0)
    forward_q(3, 1)
    attend_one(4)
    for d in range(2):
        go_o(d, 0, d)
    for d in range(2):
        go_o(d, 1, 1 - d)
    send_rows()
    attend_two(2)

    def merge(r, d, t, half):
        mine, other = stats[r, half], sin[d, t, half]
        for i in range(3):
            m0, m1 = mine[i:i + 1], other[i:i + 1]
            best = jnp.maximum(m0, m1)
            f0, f1 = jnp.exp2(m0 - best), jnp.exp2(m1 - best)
            rows = slice(i * HD, (i + 1) * HD)
            mixed = opart[r, half, rows].astype(F32) * f0 + oin[d, t, half, rows].astype(F32) * f1
            opart[r, half, rows] = mixed.astype(BF16)
            stats[r, half, i:i + 1] = best
            stats[r, half, 3 + i:4 + i] = mine[3 + i:4 + i] * f0 + other[3 + i:4 + i] * f1

    for t in (1, 2, 3):
        if t == 2:
            attend_two(3)
        if t == 3:
            attend_one(0)
        for turn in range(2):
            for d in range(2):
                half = d if turn else 1 - d
                if t == 1 and not turn:
                    continue
                take_o(d, t - 1, half)
                merge(4 - t if d == 0 else 4 + t, d, t - 1, half)
                go_o(d, t, half)
    for r in (1, 2, 3):
        take(row_ys[NY - r])
    for n in range(NZ):
        aturn[n] = arecv[:, n].reshape(NY * 8, CH).astype(BF16)
    alast[pl.ds(z, 1)] = aturn[pl.ds(z, 1)]
    for half in range(2):
        for d in range(2):
            take_o(d, 3, half)
            merge(0, d, 3, half)
    for r in (4, 3, 5, 2, 6, 1, 7):
        go(row_zs[r])
    for r in (1, 3, 2):
        take(p_copies[NX - r])
        go(pc_copies[r])
    local[6].wait()
    for h in range(HEADS):
        half, i = h // 3, h % 3
        cols = slice(h * HD, (h + 1) * HD)
        attn = opart[0, half, i * HD:(i + 1) * HD].astype(F32) / stats[0, half, 3 + i:4 + i]
        attn = attn.T.astype(BF16).astype(F32)
        hgrp[sec, y, :, cols] = (resv[:, cols].astype(F32) + attn).astype(BF16)

    h_copies = y_copies(0, lambda: hgrp.at[sec, y])
    for r in (2, 1, 3):
        go(h_copies[r])
    local[7].wait()
    hidden = hgrp[sec, y]
    f_copies = []
    for c in range(2):
        cols = slice(c * 1024, (c + 1) * 1024)
        fpart[:, :, cols] = dot(hidden, pin[:, cols]).astype(BF16).reshape(NX, 32, 1024)
        f_copies.append(x_copies(
            2 + c, lambda r: fpart.at[lax.rem(x + r, NX), :, cols], lambda r: frecv.at[r, :, cols]))
        for r in (2, 1, 3):
            go(f_copies[c][r])
    column = iota((NSEQ, CAP), 1)
    e_of = ((column >> 3) & (NY - 1)) * NZ + (column >> 5)
    device = iota((NSEQ, CAP), 0)
    counts8 = jnp.broadcast_to(counts, (8, NSEQ)).astype(BF16)
    start = dot(counts8, jnp.where(device < e_of, 1.0, 0.0).astype(BF16))[0:1]
    count = dot(counts8, jnp.where(device == e_of, 1.0, 0.0).astype(BF16))[0:1]
    low = start + ((iota((1, CAP), 1) & 7) * NSEQ).astype(F32)
    high = jnp.minimum(low + float(NSEQ), start + count)
    place = (iota((ROWS, CAP), 0) * NSEQ + seq).astype(F32)
    chosen = jnp.where((place >= low) & (place < high), 1.0, 0.0).astype(BF16)

    for r in range(1, NZ):
        take(row_zs[NZ - r])
    tsend[...] = dot(chosen, alast[...].reshape(CAP, CH)).astype(BF16).reshape(NX, 32, CH)
    t_copies = x_copies(5, lambda r: tsend.at[lax.rem(x + r, NX)], lambda r: tgt.at[r])
    for r in (2, 1, 3):
        go(t_copies[r])
    tgt[0] = tsend[x]
    column_weight[...] = jnp.broadcast_to(aw_ref[...], (ROWS, ROWS)).T
    for c in range(2):
        cols = slice(c * 1024, (c + 1) * 1024)
        for r in (1, 2, 3):
            take(f_copies[c][NX - r])
        value = fpart[x, :, cols].astype(F32)
        for r in (1, 2, 3):
            value = value + frecv[r, :, cols].astype(F32)
        first[:, cols] = value
        act_rows[:, cols] = (value * jax.nn.sigmoid(value)).astype(BF16)
    act = act_rows[...]
    act_pieces = group_copies(0, apiece, agrp)
    send_pieces(act_pieces, act, apiece, agrp)
    for r in range(NX):
        if r:
            take(pc_copies[r])
        second[r] = dot(act, pfull[r])
    for r in (1, 2, 3):
        take(t_copies[NX - r])
    inner = square_z = square_f = 0.0
    for r in range(NX):
        tf = tgt[r].astype(F32)
        inner = inner + jnp.sum(second[r] * tf, axis=1, keepdims=True)
        square_z = square_z + jnp.sum(second[r] * second[r], axis=1, keepdims=True)
        square_f = square_f + jnp.sum(tf * tf, axis=1, keepdims=True)
    norm_z = jnp.sqrt(square_z + 1e-6)
    norm_f = jnp.sqrt(square_f + 1e-6)
    aligned = inner / (norm_z * norm_f)
    weight = column_weight[pl.ds(pl.multiple_of(x * 32, 32), 32), 0:1]
    by_target = -weight / (norm_z * norm_f)
    by_second = weight * aligned / (norm_z * norm_z)
    b_copies = x_copies(6, lambda r: bsend.at[r], lambda r: bgrp.at[sec, y, x])
    for r in (2, 1, 3, 0):
        bsend[r] = (by_target * tgt[r].astype(F32) + by_second * second[r]).astype(BF16)
        if r:
            go(b_copies[r])
    bgrp[sec, y, x] = bsend[0]
    alall[x] = jnp.broadcast_to(aligned, (32, HD))
    l_copies = x_copies(7, lambda r: alall.at[x], lambda r: alall.at[x])
    for r in (2, 1, 3):
        go(l_copies[r])
    for copy in act_pieces:
        take(copy)
    act_copies = x_copies(4, lambda r: agrp.at[x], lambda r: agrp.at[x])
    for r in (2, 1, 3):
        go(act_copies[r])
    upstream = dot(bsend[0], pfull[0], 1, 1)
    for r in (1, 2, 3):
        upstream = upstream + dot(bsend[r], pfull[r], 1, 1)
    value = first[...]
    sig = jax.nn.sigmoid(value)
    dfirst = (upstream * sig * (1.0 + value * (1.0 - sig))).astype(BF16)
    d_pieces = group_copies(1, dpiece, dgrp)
    send_pieces(d_pieces, dfirst, dpiece, dgrp)
    for r in (1, 2, 3):
        take(b_copies[NX - r])
    back_copies = y_copies(1, lambda: bgrp.at[sec, y])
    for r in (2, 1, 3):
        go(back_copies[r])
    for r in (1, 2, 3):
        take(h_copies[NY - r])
    hidden_core = core_copy(0, hgrp.at[sec])
    go(hidden_core)
    for copy in d_pieces:
        take(copy)
    d_copies = x_copies(8, lambda r: dgrp.at[x], lambda r: dgrp.at[x])
    for r in (2, 1, 3):
        go(d_copies[r])
    for r in (1, 2, 3):
        take(l_copies[NX - r])
    al_ref[...] = alall[...].reshape(ROWS, HD).T[0:1]
    for r in (1, 2, 3):
        take(back_copies[NY - r])
    back_core = core_copy(1, bgrp.at[sec])
    go(back_core)
    for r in (1, 2, 3):
        take(act_copies[NX - r])
    take(back_core)

    def z_copies(n):
        copies = {}
        for r in range(1, NZ):
            peer = lax.rem(z + r, NZ)
            copies[r] = rcopy(gz.at[n, peer], gz_in.at[n, NZ - r], gz_s.at[n, r - 1], gz_r.at[n, NZ - r - 1],
                              {"seq": y * NZ + peer})
        return copies

    z_all = [z_copies(n) for n in range(3)]

    def product(n, left, right_of):
        value = 0.0
        for b in range(NX):
            rows = left[b].reshape(CAP, CAP)
            value = value + dot(rows, right_of(b).reshape(CAP, CH), 0, 0)
        gz[n] = value.astype(BF16).reshape(NZ, 32, CH)
        for r in (4, 3, 5, 2, 6, 1, 7):
            go(z_all[n][r])

    def finish(n):
        for r in range(1, NZ):
            take(z_all[n][NZ - r])
        value = gz[n, z].astype(F32)
        for r in range(1, NZ):
            value = value + gz_in[n, r].astype(F32)
        return value

    product(0, agrp, lambda b: bgrp[:, :, b])
    take(hidden_core)
    for r in (1, 2, 3):
        take(d_copies[NX - r])
    for n in range(2):
        product(1 + n, dgrp, lambda b: hgrp[:, :, b * 32:(b + 1) * 32, n * CH:(n + 1) * CH])
    go_ref[...] = finish(0)
    for n in range(2):
        gi_ref[:, n * CH:(n + 1) * CH] = finish(1 + n)

    for copy in pending:
        copy.wait_send()


def body(
    queries, keys, values, residual, segment_ids, enc_counts, enc_hidden, enc_down, enc_resid,
    layer_scale, norm_gain, norm_bias, proj_in, proj_out, align_weight,
):
    anywhere = pl.BlockSpec(memory_space=pl.ANY)
    vmem = pl.BlockSpec(memory_space=pltpu.VMEM)
    V, D = pltpu.VMEM, pltpu.SemaphoreType.DMA
    scratch = [
        V((NZ, ROWS, WIDTH), BF16), V((NY, ROWS, WIDTH), BF16), V((NY, ROWS, WIDTH), BF16),
        V((WIDTH, NY * ROWS), BF16), V((NY, ROWS, HD), BF16), V((ROWS, WIDTH), BF16),
        V((CAP, FF), BF16), V((FF, ENC_D), BF16), V((CAP, CH), BF16),
        V((WIDTH, PROJ), BF16), V((NX, PROJ, CH), BF16),
        V((NZ, 2, HALF, HD), BF16), V((NZ, 2, 8, HD), F32),
        V((2, 4, 2, HALF, HD), BF16), V((2, 4, 2, 8, HD), F32),
        V((NX, CAP, CH), BF16), V((NX, CAP, CH), BF16), V((CAP, CH), F32),
        V((8, CAP), F32), V((NX, 8, CAP), F32),
        V((NY, NZ, 8, CH), F32), V((NY, NZ, 8, CH), F32), V((NZ, 32, CH), BF16), V((NZ, 32, CH), BF16),
        V((NX, 32, CH), BF16), V((NX, 32, CH), BF16),
        V((2, NY, ROWS, WIDTH), BF16), V((NX, 32, PROJ), BF16), V((NX, 32, PROJ), BF16), V((32, PROJ), F32),
        V((32, PROJ), BF16), V((NX, 32, CH), F32), V((NX, 32, CH), BF16), V((2, NY, NX, 32, CH), BF16),
        V((NX, 32, HD), F32), V((ROWS, ROWS), F32),
        V((2, NY, 32, 256), BF16), V((NX, 2, NY, 32, 256), BF16),
        V((2, NY, 32, 256), BF16), V((NX, 2, NY, 32, 256), BF16),
        V((3, NZ, 32, CH), BF16), V((3, NZ, 32, CH), BF16),
        V((2, HD, HD), F32),
    ]
    scratch += [
        D((9,)), D((2, 4, 2)), D((2, 4, 2)), D((6,)), D((6,)),
        D((2, 4, 2)), D((2, 4, 2)), D((2, 4, 2)), D((2, 4, 2)),
        D((10, 3)), D((10, 3)), D((3,)), D((3,)), D((3,)), D((3,)), D((7,)), D((7,)),
        D((2,)), D((2,)), D((2, 3)), D((2, 3)), D((3, 7)), D((3, 7)), D((2, 8)), D((2, 8)),
    ]
    aligned, grad_in_t, grad_out = pl.pallas_call(
        kernel,
        out_shape=(
            jax.ShapeDtypeStruct((1, ROWS), F32),
            jax.ShapeDtypeStruct((32, WIDTH), F32),
            jax.ShapeDtypeStruct((32, CH), F32),
        ),
        in_specs=[anywhere] * 4 + [vmem] * 2 + [anywhere] * 3 + [vmem] * 3 + [anywhere] * 2 + [vmem],
        out_specs=(vmem, vmem, vmem),
        scratch_shapes=scratch,
        compiler_params=pltpu.CompilerParams(
            collective_id=0, has_side_effects=True, vmem_limit_bytes=56 * 1024 * 1024
        ),
        name="align",
    )(
        queries, keys, values, residual, segment_ids, enc_counts, enc_hidden, enc_down, enc_resid,
        layer_scale.reshape(-1, HD), norm_gain.reshape(-1, HD), norm_bias.reshape(-1, HD),
        proj_in, proj_out, align_weight.reshape(1, -1),
    )

    def hand_on(a, b, c, a_out, b_out, c_out):
        a_out[...] = a[...]
        b_out[...] = b[...]
        c_out[...] = c[...]

    aligned, grad_in_t, grad_out = pl.pallas_call(
        hand_on,
        out_shape=tuple(jax.ShapeDtypeStruct(v.shape, F32) for v in (aligned, grad_in_t, grad_out)),
        in_specs=[vmem] * 3,
        out_specs=(vmem, vmem, vmem),
        name="hand_on",
    )(aligned, grad_in_t, grad_out)
    return aligned.reshape(-1), grad_in_t, grad_out


def solution(mesh):
    return jax.shard_map(
        body,
        mesh=mesh,
        in_specs=(
            P(("section", "seq"), "mp"),
            P(("section", "seq"), "mp"),
            P(("section", "seq"), "mp"),
            P(("section", "seq"), "mp"),
            P("section", None),
            P("section", None),
            P(("section", "seq"), "mp"),
            P("mp", None),
            P(("section", "seq"), "mp"),
            P(),
            P(),
            P(),
            P("mp", None),
            P(None, "mp"),
            P(("section", "seq")),
        ),
        out_specs=(P(("section", "seq")), P(("section", "seq"), "mp"), P(("section", "seq"), "mp")),
        check_vma=False,
    )
```

```python
import math

import jax
import jax.numpy as jnp
from jax import lax
from jax.experimental import pallas as pl
from jax.experimental.pallas import tpu as pltpu
from jax.sharding import PartitionSpec as P

MESH = pl.DeviceIdType.MESH
F32, BF16, I32 = jnp.float32, jnp.bfloat16, jnp.int32
HD = 128
ENC_D = 1536
NX, NY, NZ = 4, 4, 8
NSEQ = NY * NZ
ROWS = 128
CAP = 256
WIDTH = 768
HEADS = 6
HALF = 384
CH = 384
FF = 1024
PROJ = 2048
PART = 512
SAME = 8192.0
EXP_SCALE = math.log2(math.e) * HD ** (-0.5)


def rcopy(src, dst, send, recv, dev):
    return pltpu.make_async_remote_copy(
        src_ref=src, dst_ref=dst, send_sem=send, recv_sem=recv, device_id=dev, device_id_type=MESH
    )


def iota(shape, dim):
    return lax.broadcasted_iota(I32, shape, dim)


def dot(a, b, ca=1, cb=0):
    return lax.dot_general(a, b, (((ca,), (cb,)), ((), ())), preferred_element_type=F32)


def kernel(
    q_hbm, k_hbm, v_hbm, res_hbm, seg_ref, cnt_ref, eh_hbm, ed_hbm, er_hbm, ls_ref, gain_ref, bias_ref,
    pin_hbm, pout_hbm, aw_ref,
    al_ref, gi_ref, go_ref,
    qbuf, kbuf, vbuf, vt, ko, resv, ehv, edv, erv, pin, pfull,
    opart, stats, oin, sin,
    esend, erecv, share, estat, estat_in, packed, arecv, aturn, alast, tsend, tgt,
    hgrp, fpart, frecv, first, act_rows, second, bsend, bgrp, alall, column_weight,
    apiece, agrp, dpiece, dgrp, gz, gz_in, segrow,
    lsem, q_s, q_r, kv_s, kv_r, o_s, o_r, os_s, os_r, x_s, x_r, pc_s, pc_r, pr_s, pr_r, ay_s, ay_r, az_s, az_r,
    gx_s, gx_r, gy_s, gy_r, gz_s, gz_r, gg_s, gg_r,
):
    sec = lax.axis_index("section")
    seq = lax.axis_index("seq")
    x = lax.axis_index("mp")
    y = seq // NZ
    z = lax.rem(seq, NZ)
    zp = {"seq": y * NZ + lax.rem(z + 1, NZ)}
    zm = {"seq": y * NZ + lax.rem(z + NZ - 1, NZ)}
    yp = {"seq": lax.rem(y + 1, NY) * NZ + z}
    ym = {"seq": lax.rem(y + NY - 1, NY) * NZ + z}
    pending = []

    def go(copy):
        copy.start()
        pending.append(copy)
        return copy

    def take(copy):
        copy.wait_recv()

    local = []
    for n, (src, dst) in enumerate((
        (q_hbm, qbuf.at[0]), (k_hbm, kbuf.at[0]), (v_hbm, vbuf.at[0]), (eh_hbm, ehv), (ed_hbm, edv),
        (er_hbm, erv), (res_hbm, resv), (pin_hbm, pin), (pout_hbm, pfull.at[0]),
    )):
        copy = pltpu.make_async_copy(src, dst, lsem.at[n])
        local.append(copy)

    def fetch(first, last):
        for n in range(first, last):
            local[n].start()

    fetch(0, 3)

    barrier = pltpu.get_barrier_semaphore()

    greeted = [{"seq": y * NZ + lax.rem(z + r, NZ)} for r in range(1, NZ)]
    greeted += [{"seq": lax.rem(y + r, NY) * NZ + z} for r in range(1, NY)]
    greeted += [{"mp": lax.rem(x + r, NX)} for r in range(1, NX)]
    greeted += [{"section": 1 - sec, "seq": lax.rem(y + r, NY) * NZ + z} for r in range(NY)]
    for device in greeted:
        pl.semaphore_signal(barrier, inc=1, device_id=device, device_id_type=MESH)
    pl.semaphore_wait(barrier, len(greeted))

    def q_copy(d, t, half):
        cols = pl.ds(half * HALF, HALF)
        src = qbuf.at[(8 - t) % 8 if d == 0 else t, :, cols]
        dst = qbuf.at[7 - t if d == 0 else t + 1, :, cols]
        return rcopy(src, dst, q_s.at[d, t, half], q_r.at[d, t, half], zp if d == 0 else zm)

    def kv_copy(n):
        src, dst, dev = (
            (kbuf.at[0], kbuf.at[3], yp), (kbuf.at[0], kbuf.at[1], ym),
            (vbuf.at[0], vbuf.at[3], yp), (vbuf.at[0], vbuf.at[1], ym),
            (kbuf.at[3], kbuf.at[2], yp), (vbuf.at[1], vbuf.at[2], ym),
        )[n]
        return rcopy(src, dst, kv_s.at[n], kv_r.at[n], dev)

    q_copies = [[{h: q_copy(d, t, h) for h in ((0, 1) if t < 3 else (d,))} for t in range(4)] for d in range(2)]
    kv_copies = [kv_copy(n) for n in range(6)]
    for n in range(3):
        local[n].wait()
    fetch(3, 9)
    for half in range(2):
        for d in range(2):
            go(q_copies[d][0][half])
    go(kv_copies[0])
    go(kv_copies[1])
    go(kv_copies[2])
    go(kv_copies[3])

    def x_copies(phase, src_of, dst_of, which=(1, 2, 3)):
        return {
            r: rcopy(src_of(r), dst_of(NX - r), x_s.at[phase, r - 1], x_r.at[phase, NX - r - 1],
                     {"mp": lax.rem(x + r, NX)})
            for r in which
        }

    def y_copies(n, ref_of):
        return {
            r: rcopy(ref_of(), ref_of(), gy_s.at[n, r - 1], gy_r.at[n, NY - r - 1],
                     {"seq": lax.rem(y + r, NY) * NZ + z})
            for r in (1, 2, 3)
        }

    def core_copy(n, ref):
        return rcopy(ref, ref, gx_s.at[n], gx_r.at[n], {"section": 1 - sec})

    def group_copies(n, pieces, group):
        copies = []
        for ds in range(2):
            for r in range(NY):
                if ds or r:
                    to_sec, to_y = lax.rem(sec + ds, 2), lax.rem(y + r, NY)
                    copies.append(rcopy(
                        pieces.at[to_sec, to_y], group.at[x, sec, y],
                        gg_s.at[n, ds * NY + r], gg_r.at[n, ds * NY + (NY - r) % NY],
                        {"section": to_sec, "seq": to_y * NZ + z}))
        return copies

    def send_pieces(copies, rows, pieces, group):
        for a in range(2):
            for b in range(NY):
                pieces[a, b] = rows[:, (a * NY + b) * 256:(a * NY + b + 1) * 256]
        for copy in copies:
            go(copy)
        group[x, sec, y] = pieces[sec, y]

    local[3].wait()
    local[4].wait()
    enc_copies = x_copies(0, lambda r: esend.at[r], lambda r: erecv.at[r])
    for r in (2, 1, 3, 0):
        cols = pl.ds(pl.multiple_of(lax.rem(x + r, NX) * CH, CH), CH)
        esend[r] = dot(ehv[...], edv[:, cols]).astype(BF16)
        if r:
            go(enc_copies[r])

    core_rows = pl.ds(pl.multiple_of(sec * (PROJ // 2), PROJ // 2), PROJ // 2)
    p_copies = x_copies(9, lambda r: pfull.at[0, core_rows], lambda r: pfull.at[r, core_rows], (1, 3))

    def relay(n):
        part = pl.ds(pl.multiple_of(sec * (PROJ // 2) + n * PART, PART), PART)
        return rcopy(pfull.at[(3, 1)[n], part], pfull.at[2, part], pr_s.at[n], pr_r.at[n],
                     {"mp": lax.rem(x + (1, 3)[n], NX)})

    relays = [relay(0), relay(1)]
    pc_copies = {r: rcopy(pfull.at[r, core_rows], pfull.at[r, core_rows], pc_s.at[r - 1], pc_r.at[r - 1],
                          {"section": 1 - sec}) for r in (1, 2, 3)}
    ids = iota((16, NSEQ * ROWS), 0)
    seg = seg_ref[...]
    below = jnp.sum(jnp.where(seg < ids, 1.0, 0.0), axis=1, keepdims=True)
    upto = jnp.sum(jnp.where(seg <= ids, 1.0, 0.0), axis=1, keepdims=True)
    lane = iota((16, HD), 1)
    tail = jnp.full((HD - 16, HD), 1e9, F32)
    segrow[0] = jnp.concatenate([jnp.broadcast_to(below, lane.shape), tail], axis=0).T
    segrow[1] = jnp.concatenate([jnp.broadcast_to(upto, lane.shape), tail], axis=0).T

    def image_columns(device):
        place = (iota((ROWS, HD), 0) * NSEQ + device).astype(F32)
        return (place >= segrow[0]) & (place < segrow[1])

    for r in range(NY):
        device = lax.rem(y + r, NY) * NZ + z
        ko[r] = jnp.where(image_columns(device), SAME, 0.0).astype(BF16)

    def forward_q(t, half):
        for d in range(2):
            if half in q_copies[d][t]:
                take(q_copies[d][t][half])
            if t < 3 and half in q_copies[d][t + 1]:
                go(q_copies[d][t + 1][half])

    def own(ref):
        return jnp.concatenate([ref[pl.ds(3 * x + i, 1), :] for i in range(3)], axis=1)

    stat_copies = x_copies(1, lambda r: estat, lambda r: estat_in.at[r])
    pad = jnp.zeros((HD - 8, HD), F32)
    row8 = iota((8, HD), 0)
    counts = cnt_ref[...].astype(F32)

    def row_y(r):
        peer = lax.rem(y + r, NY)
        return rcopy(packed.at[peer], arecv.at[y], ay_s.at[r - 1], ay_r.at[NY - r - 1], {"seq": peer * NZ + z})

    def row_z(r):
        peer = lax.rem(z + r, NZ)
        return rcopy(aturn.at[peer], alast.at[z], az_s.at[r - 1], az_r.at[NZ - r - 1], {"seq": y * NZ + peer})

    row_ys = {r: row_y(r) for r in range(1, NY)}
    row_zs = {r: row_z(r) for r in range(1, NZ)}
    def sum_encoder():
        local[5].wait()
        for r in (1, 2, 3):
            take(enc_copies[NX - r])
        enc = esend[0].astype(F32)
        for r in (1, 2, 3):
            enc = enc + erecv[r].astype(F32)
        enc = erv[...].astype(F32) + own(ls_ref) * enc
        share[...] = enc
        lane = iota((CAP, HD), 1)
        total = jnp.sum(enc, axis=1, keepdims=True)
        square = jnp.sum(enc * enc, axis=1, keepdims=True)
        packed_stat = jnp.where(lane == 0, total, jnp.where(lane == 1, square, 0.0))
        for b in range(2):
            estat[:, b * HD:(b + 1) * HD] = packed_stat[b * HD:(b + 1) * HD].T[0:8]
        for r in (2, 1, 3):
            go(stat_copies[r])

    def gather_out():
        local[8].wait()
        for r in (1, 3):
            go(p_copies[r])

    def relay_out():
        for n in range(2):
            take(p_copies[(1, 3)[n]])
            go(relays[n])


    def send_rows():
        for r in (1, 2, 3):
            take(stat_copies[NX - r])
        both = estat[...]
        for r in (1, 2, 3):
            both = both + estat_in[r]
        mean = both[0:1] * (1.0 / ENC_D)
        scale = lax.rsqrt(both[1:2] * (1.0 / ENC_D) - mean * mean + 1e-6)
        gain = own(gain_ref)
        bias = own(bias_ref)
        parts = []
        for b in range(2):
            cut = slice(b * HD, (b + 1) * HD)
            rows = jnp.where(row8 == 0, mean[:, cut], jnp.where(row8 == 1, scale[:, cut], 0.0))
            cols = jnp.concatenate([rows, pad], axis=0).T
            parts.append((((share[cut] - cols[:, 0:1]) * cols[:, 1:2]) * gain + bias).astype(BF16))
        feature = jnp.concatenate(parts, axis=0)
        before = jnp.sum(jnp.where(iota((1, NSEQ), 1) < seq, counts, 0.0), axis=1, keepdims=True).astype(I32)
        row = iota((CAP, CAP), 0)
        wanted = (row & 7) * NSEQ + (((row >> 3) - before) & (NSEQ - 1))
        permutation = jnp.where(iota((CAP, CAP), 1) == wanted, 1.0, 0.0).astype(BF16)
        packed[...] = dot(permutation, feature).reshape(NY, NZ, 8, CH)

        for r in (2, 1, 3):
            go(row_ys[r])
        arecv[pl.ds(y, 1)] = packed[pl.ds(y, 1)]

    def attend(pair):
        keys_image = ko[...].reshape(NY * ROWS, HD)
        image = jnp.concatenate(
            [jnp.where(image_columns(y * NZ + lax.rem(z + r, NZ)), 1.0, 0.0).astype(BF16) for r in pair], axis=0)
        scores, probs = {}, {}
        for step in range(HEADS + 2):
            if step < HEADS:
                cols = slice(step * HD, (step + 1) * HD)
                keys = jnp.concatenate([kbuf[:, :, cols].reshape(NY * ROWS, HD), keys_image], axis=1)
                rows = jnp.concatenate([qbuf[r, :, cols] for r in pair], axis=0)
                scores[step] = dot(keys, jnp.concatenate([rows, image], axis=1), 1, 1)
            if 1 <= step <= HEADS:
                h = step - 1
                score = scores.pop(h)
                best = jnp.max(score, axis=0, keepdims=True)
                prob = jnp.exp2((score - best) * EXP_SCALE)
                total = jnp.sum(prob, axis=0, keepdims=True)
                half, i = h // 3, h % 3
                for n, r in enumerate(pair):
                    cut = slice(n * ROWS, (n + 1) * ROWS)
                    stats[r, half, i:i + 1] = best[:, cut] * EXP_SCALE
                    stats[r, half, 3 + i:4 + i] = total[:, cut]
                probs[h] = prob.astype(BF16)
            if step >= 2:
                h = step - 2
                half, i = h // 3, h % 3
                mixed = dot(vt[h * HD:(h + 1) * HD], probs.pop(h)).astype(BF16)
                for n, r in enumerate(pair):
                    opart[r, half, i * HD:(i + 1) * HD] = mixed[:, n * ROWS:(n + 1) * ROWS]

    def turn_values(r):
        vt[:, r * ROWS:(r + 1) * ROWS] = vbuf[r].T

    def o_copy(d, t, half):
        r = 4 - t if d == 0 else 4 + t
        dev = zp if d == 0 else zm
        return (rcopy(opart.at[r, half], oin.at[d, t, half], o_s.at[d, t, half], o_r.at[d, t, half], dev),
                rcopy(stats.at[r, half], sin.at[d, t, half], os_s.at[d, t, half], os_r.at[d, t, half], dev))

    o_copies = [[{h: o_copy(d, t, h) for h in ((0, 1) if t else (d,))} for t in range(4)] for d in range(2)]

    def go_o(d, t, half):
        for copy in o_copies[d][t][half]:
            go(copy)

    def take_o(d, t, half):
        for copy in o_copies[d][t][half]:
            take(copy)

    forward_q(0, 0)
    forward_q(0, 1)
    forward_q(1, 0)
    take(kv_copies[0])
    go(kv_copies[4])
    forward_q(1, 1)
    take(kv_copies[3])
    go(kv_copies[5])
    take(kv_copies[1])
    take(kv_copies[2])
    for r in (0, 1, 3):
        turn_values(r)
    forward_q(2, 0)
    sum_encoder()
    gather_out()
    forward_q(2, 1)
    for n in (4, 5):
        take(kv_copies[n])
    turn_values(2)
    attend((5, 3))
    forward_q(3, 0)
    forward_q(3, 1)
    attend((4, 0))
    for d in range(2):
        go_o(d, 0, d)
    for d in range(2):
        go_o(d, 1, 1 - d)
    send_rows()
    attend((6, 2))

    def merge(r, d, t, half):
        mine, other = stats[r, half], sin[d, t, half]
        for i in range(3):
            m0, m1 = mine[i:i + 1], other[i:i + 1]
            best = jnp.maximum(m0, m1)
            f0, f1 = jnp.exp2(m0 - best), jnp.exp2(m1 - best)
            rows = slice(i * HD, (i + 1) * HD)
            mixed = opart[r, half, rows].astype(F32) * f0 + oin[d, t, half, rows].astype(F32) * f1
            opart[r, half, rows] = mixed.astype(BF16)
            stats[r, half, i:i + 1] = best
            stats[r, half, 3 + i:4 + i] = mine[3 + i:4 + i] * f0 + other[3 + i:4 + i] * f1

    for t in (1, 2, 3):
        if t == 2:
            attend((7, 1))
        for turn in range(2):
            for d in range(2):
                half = d if turn else 1 - d
                if t == 1 and not turn:
                    continue
                take_o(d, t - 1, half)
                merge(4 - t if d == 0 else 4 + t, d, t - 1, half)
                go_o(d, t, half)
    relay_out()
    for r in (1, 2, 3):
        take(row_ys[NY - r])
    for n in range(NZ):
        aturn[n] = arecv[:, n].reshape(NY * 8, CH).astype(BF16)
    alast[pl.ds(z, 1)] = aturn[pl.ds(z, 1)]
    for r in (4, 3, 5, 2, 6, 1, 7):
        go(row_zs[r])
    for half in range(2):
        for d in range(2):
            take_o(d, 3, half)
            merge(0, d, 3, half)
    for r in (1, 3):
        go(pc_copies[r])
    for n in range(2):
        take(relays[n])
    go(pc_copies[2])
    local[6].wait()
    for h in range(HEADS):
        half, i = h // 3, h % 3
        cols = slice(h * HD, (h + 1) * HD)
        attn = opart[0, half, i * HD:(i + 1) * HD].astype(F32) / stats[0, half, 3 + i:4 + i]
        attn = attn.T.astype(BF16).astype(F32)
        hgrp[sec, y, :, cols] = (resv[:, cols].astype(F32) + attn).astype(BF16)

    h_copies = y_copies(0, lambda: hgrp.at[sec, y])
    for r in (2, 1, 3):
        go(h_copies[r])
    local[7].wait()
    hidden = hgrp[sec, y]
    f_copies = []
    for c in range(2):
        cols = slice(c * 1024, (c + 1) * 1024)
        fpart[:, :, cols] = dot(hidden, pin[:, cols]).astype(BF16).reshape(NX, 32, 1024)
        f_copies.append(x_copies(
            2 + c, lambda r: fpart.at[lax.rem(x + r, NX), :, cols], lambda r: frecv.at[r, :, cols]))
        for r in (2, 1, 3):
            go(f_copies[c][r])
    column = iota((NSEQ, CAP), 1)
    e_of = ((column >> 3) & (NY - 1)) * NZ + (column >> 5)
    device = iota((NSEQ, CAP), 0)
    counts8 = jnp.broadcast_to(counts, (8, NSEQ)).astype(BF16)
    start = dot(counts8, jnp.where(device < e_of, 1.0, 0.0).astype(BF16))[0:1]
    count = dot(counts8, jnp.where(device == e_of, 1.0, 0.0).astype(BF16))[0:1]
    low = start + ((iota((1, CAP), 1) & 7) * NSEQ).astype(F32)
    high = jnp.minimum(low + float(NSEQ), start + count)
    place = (iota((ROWS, CAP), 0) * NSEQ + seq).astype(F32)
    chosen = jnp.where((place >= low) & (place < high), 1.0, 0.0).astype(BF16)

    for c in range(2):
        cols = slice(c * 1024, (c + 1) * 1024)
        for r in (1, 2, 3):
            take(f_copies[c][NX - r])
        value = fpart[x, :, cols].astype(F32)
        for r in (1, 2, 3):
            value = value + frecv[r, :, cols].astype(F32)
        first[:, cols] = value
        act_rows[:, cols] = (value * jax.nn.sigmoid(value)).astype(BF16)
    act = act_rows[...]
    act_pieces = group_copies(0, apiece, agrp)
    send_pieces(act_pieces, act, apiece, agrp)
    for r in range(NX):
        if r:
            take(pc_copies[r])
        if r == 2:
            for copy in act_pieces:
                take(copy)
            act_copies = x_copies(4, lambda r: agrp.at[x], lambda r: agrp.at[x])
            for r2 in (2, 1, 3):
                go(act_copies[r2])
        second[r] = dot(act, pfull[r])
    for r in range(1, NZ):
        take(row_zs[NZ - r])
    tsend[...] = dot(chosen, alast[...].reshape(CAP, CH)).astype(BF16).reshape(NX, 32, CH)
    t_copies = x_copies(5, lambda r: tsend.at[lax.rem(x + r, NX)], lambda r: tgt.at[r])
    for r in (2, 1, 3):
        go(t_copies[r])
    tgt[0] = tsend[x]
    column_weight[...] = jnp.broadcast_to(aw_ref[...], (ROWS, ROWS)).T
    for r in (1, 2, 3):
        take(t_copies[NX - r])
    inner = square_z = square_f = 0.0
    for r in range(NX):
        tf = tgt[r].astype(F32)
        inner = inner + jnp.sum(second[r] * tf, axis=1, keepdims=True)
        square_z = square_z + jnp.sum(second[r] * second[r], axis=1, keepdims=True)
        square_f = square_f + jnp.sum(tf * tf, axis=1, keepdims=True)
    norm_z = jnp.sqrt(square_z + 1e-6)
    norm_f = jnp.sqrt(square_f + 1e-6)
    aligned = inner / (norm_z * norm_f)
    weight = column_weight[pl.ds(pl.multiple_of(x * 32, 32), 32), 0:1]
    by_target = -weight / (norm_z * norm_f)
    by_second = weight * aligned / (norm_z * norm_z)
    b_copies = x_copies(6, lambda r: bsend.at[r], lambda r: bgrp.at[sec, y, x])
    for r in (2, 1, 3, 0):
        bsend[r] = (by_target * tgt[r].astype(F32) + by_second * second[r]).astype(BF16)
        if r:
            go(b_copies[r])
    bgrp[sec, y, x] = bsend[0]
    alall[x] = jnp.broadcast_to(aligned, (32, HD))
    l_copies = x_copies(7, lambda r: alall.at[x], lambda r: alall.at[x])
    for r in (2, 1, 3):
        go(l_copies[r])
    upstream = dot(bsend[0], pfull[0], 1, 1)
    for r in (1, 2, 3):
        upstream = upstream + dot(bsend[r], pfull[r], 1, 1)
    value = first[...]
    sig = jax.nn.sigmoid(value)
    dfirst = (upstream * sig * (1.0 + value * (1.0 - sig))).astype(BF16)
    d_pieces = group_copies(1, dpiece, dgrp)
    send_pieces(d_pieces, dfirst, dpiece, dgrp)
    for r in (1, 2, 3):
        take(b_copies[NX - r])
    back_copies = y_copies(1, lambda: bgrp.at[sec, y])
    for r in (2, 1, 3):
        go(back_copies[r])
    for r in (1, 2, 3):
        take(h_copies[NY - r])
    hidden_core = core_copy(0, hgrp.at[sec])
    go(hidden_core)
    for copy in d_pieces:
        take(copy)
    d_copies = x_copies(8, lambda r: dgrp.at[x], lambda r: dgrp.at[x])
    for r in (2, 1, 3):
        go(d_copies[r])
    for r in (1, 2, 3):
        take(l_copies[NX - r])
    al_ref[...] = alall[...].reshape(ROWS, HD).T[0:1]
    for r in (1, 2, 3):
        take(back_copies[NY - r])
    back_core = core_copy(1, bgrp.at[sec])
    go(back_core)
    for r in (1, 2, 3):
        take(act_copies[NX - r])
    take(back_core)

    def z_copies(n):
        copies = {}
        for r in range(1, NZ):
            peer = lax.rem(z + r, NZ)
            copies[r] = rcopy(gz.at[n, peer], gz_in.at[n, NZ - r], gz_s.at[n, r - 1], gz_r.at[n, NZ - r - 1],
                              {"seq": y * NZ + peer})
        return copies

    z_all = [z_copies(n) for n in range(3)]

    def product(n, left, right_of):
        value = 0.0
        for b in range(NX):
            rows = left[b].reshape(CAP, CAP)
            value = value + dot(rows, right_of(b).reshape(CAP, CH), 0, 0)
        gz[n] = value.astype(BF16).reshape(NZ, 32, CH)
        for r in (4, 3, 5, 2, 6, 1, 7):
            go(z_all[n][r])

    def finish(n):
        for r in range(1, NZ):
            take(z_all[n][NZ - r])
        value = gz[n, z].astype(F32)
        for r in range(1, NZ):
            value = value + gz_in[n, r].astype(F32)
        return value

    product(0, agrp, lambda b: bgrp[:, :, b])
    take(hidden_core)
    for r in (1, 2, 3):
        take(d_copies[NX - r])
    for n in range(2):
        product(1 + n, dgrp, lambda b: hgrp[:, :, b * 32:(b + 1) * 32, n * CH:(n + 1) * CH])
    go_ref[...] = finish(0)
    for n in range(2):
        gi_ref[:, n * CH:(n + 1) * CH] = finish(1 + n)

    for copy in pending:
        copy.wait_send()


def body(
    queries, keys, values, residual, segment_ids, enc_counts, enc_hidden, enc_down, enc_resid,
    layer_scale, norm_gain, norm_bias, proj_in, proj_out, align_weight,
):
    anywhere = pl.BlockSpec(memory_space=pl.ANY)
    vmem = pl.BlockSpec(memory_space=pltpu.VMEM)
    V, D = pltpu.VMEM, pltpu.SemaphoreType.DMA
    scratch = [
        V((NZ, ROWS, WIDTH), BF16), V((NY, ROWS, WIDTH), BF16), V((NY, ROWS, WIDTH), BF16),
        V((WIDTH, NY * ROWS), BF16), V((NY, ROWS, HD), BF16), V((ROWS, WIDTH), BF16),
        V((CAP, FF), BF16), V((FF, ENC_D), BF16), V((CAP, CH), BF16),
        V((WIDTH, PROJ), BF16), V((NX, PROJ, CH), BF16),
        V((NZ, 2, HALF, HD), BF16), V((NZ, 2, 8, HD), F32),
        V((2, 4, 2, HALF, HD), BF16), V((2, 4, 2, 8, HD), F32),
        V((NX, CAP, CH), BF16), V((NX, CAP, CH), BF16), V((CAP, CH), F32),
        V((8, CAP), F32), V((NX, 8, CAP), F32),
        V((NY, NZ, 8, CH), F32), V((NY, NZ, 8, CH), F32), V((NZ, 32, CH), BF16), V((NZ, 32, CH), BF16),
        V((NX, 32, CH), BF16), V((NX, 32, CH), BF16),
        V((2, NY, ROWS, WIDTH), BF16), V((NX, 32, PROJ), BF16), V((NX, 32, PROJ), BF16), V((32, PROJ), F32),
        V((32, PROJ), BF16), V((NX, 32, CH), F32), V((NX, 32, CH), BF16), V((2, NY, NX, 32, CH), BF16),
        V((NX, 32, HD), F32), V((ROWS, ROWS), F32),
        V((2, NY, 32, 256), BF16), V((NX, 2, NY, 32, 256), BF16),
        V((2, NY, 32, 256), BF16), V((NX, 2, NY, 32, 256), BF16),
        V((3, NZ, 32, CH), BF16), V((3, NZ, 32, CH), BF16),
        V((2, HD, HD), F32),
    ]
    scratch += [
        D((9,)), D((2, 4, 2)), D((2, 4, 2)), D((6,)), D((6,)),
        D((2, 4, 2)), D((2, 4, 2)), D((2, 4, 2)), D((2, 4, 2)),
        D((10, 3)), D((10, 3)), D((3,)), D((3,)), D((2,)), D((2,)), D((3,)), D((3,)), D((7,)), D((7,)),
        D((2,)), D((2,)), D((2, 3)), D((2, 3)), D((3, 7)), D((3, 7)), D((2, 8)), D((2, 8)),
    ]
    aligned, grad_in_t, grad_out = pl.pallas_call(
        kernel,
        out_shape=(
            jax.ShapeDtypeStruct((1, ROWS), F32),
            jax.ShapeDtypeStruct((32, WIDTH), F32),
            jax.ShapeDtypeStruct((32, CH), F32),
        ),
        in_specs=[anywhere] * 4 + [vmem] * 2 + [anywhere] * 3 + [vmem] * 3 + [anywhere] * 2 + [vmem],
        out_specs=(vmem, vmem, vmem),
        scratch_shapes=scratch,
        compiler_params=pltpu.CompilerParams(
            collective_id=0, has_side_effects=True, vmem_limit_bytes=56 * 1024 * 1024
        ),
        name="align",
    )(
        queries, keys, values, residual, segment_ids, enc_counts, enc_hidden, enc_down, enc_resid,
        layer_scale.reshape(-1, HD), norm_gain.reshape(-1, HD), norm_bias.reshape(-1, HD),
        proj_in, proj_out, align_weight.reshape(1, -1),
    )

    def hand_on(a, b, c, a_out, b_out, c_out):
        a_out[...] = a[...]
        b_out[...] = b[...]
        c_out[...] = c[...]

    aligned, grad_in_t, grad_out = pl.pallas_call(
        hand_on,
        out_shape=tuple(jax.ShapeDtypeStruct(v.shape, F32) for v in (aligned, grad_in_t, grad_out)),
        in_specs=[vmem] * 3,
        out_specs=(vmem, vmem, vmem),
        name="hand_on",
    )(aligned, grad_in_t, grad_out)
    return aligned.reshape(-1), grad_in_t, grad_out


def solution(mesh):
    return jax.shard_map(
        body,
        mesh=mesh,
        in_specs=(
            P(("section", "seq"), "mp"),
            P(("section", "seq"), "mp"),
            P(("section", "seq"), "mp"),
            P(("section", "seq"), "mp"),
            P("section", None),
            P("section", None),
            P(("section", "seq"), "mp"),
            P("mp", None),
            P(("section", "seq"), "mp"),
            P(),
            P(),
            P(),
            P("mp", None),
            P(None, "mp"),
            P(("section", "seq")),
        ),
        out_specs=(P(("section", "seq")), P(("section", "seq"), "mp"), P(("section", "seq"), "mp")),
        check_vma=False,
    )
```

```python
import math

import jax
import jax.numpy as jnp
from jax import lax
from jax.experimental import pallas as pl
from jax.experimental.pallas import tpu as pltpu
from jax.sharding import PartitionSpec as P

MESH = pl.DeviceIdType.MESH
F32, BF16, I32 = jnp.float32, jnp.bfloat16, jnp.int32
HD = 128
ENC_D = 1536
NX, NY, NZ = 4, 4, 8
NSEQ = NY * NZ
ROWS = 128
CAP = 256
WIDTH = 768
HEADS = 6
HALF = 384
CH = 384
FF = 1024
PROJ = 2048
PART = 512
SAME = 8192.0
EXP_SCALE = math.log2(math.e) * HD ** (-0.5)


def rcopy(src, dst, send, recv, dev):
    return pltpu.make_async_remote_copy(
        src_ref=src, dst_ref=dst, send_sem=send, recv_sem=recv, device_id=dev, device_id_type=MESH
    )


def iota(shape, dim):
    return lax.broadcasted_iota(I32, shape, dim)


def dot(a, b, ca=1, cb=0):
    return lax.dot_general(a, b, (((ca,), (cb,)), ((), ())), preferred_element_type=F32)


def kernel(
    q_hbm, k_hbm, v_hbm, res_hbm, seg_ref, cnt_ref, eh_hbm, ed_hbm, er_hbm, ls_ref, gain_ref, bias_ref,
    pin_hbm, pout_hbm, aw_ref,
    al_ref, gi_ref, go_ref,
    qbuf, kbuf, vbuf, vt, ko, resv, ehv, edv, erv, pin, pfull,
    opart, stats, oin, sin,
    esend, erecv, share, estat, estat_in, packed, arecv, aturn, alast, tsend, tgt,
    hgrp, fpart, frecv, first, act_rows, second, bsend, bgrp, alall, column_weight,
    apiece, agrp, dpiece, dgrp, gz, gz_in, segrow,
    lsem, q_s, q_r, kv_s, kv_r, o_s, o_r, os_s, os_r, x_s, x_r, pc_s, pc_r, pr_s, pr_r, ay_s, ay_r, az_s, az_r,
    gx_s, gx_r, gy_s, gy_r, gz_s, gz_r, gg_s, gg_r,
):
    sec = lax.axis_index("section")
    seq = lax.axis_index("seq")
    x = lax.axis_index("mp")
    y = seq // NZ
    z = lax.rem(seq, NZ)
    zp = {"seq": y * NZ + lax.rem(z + 1, NZ)}
    zm = {"seq": y * NZ + lax.rem(z + NZ - 1, NZ)}
    yp = {"seq": lax.rem(y + 1, NY) * NZ + z}
    ym = {"seq": lax.rem(y + NY - 1, NY) * NZ + z}
    pending = []

    def go(copy):
        copy.start()
        pending.append(copy)
        return copy

    def take(copy):
        copy.wait_recv()

    local = []
    for n, (src, dst) in enumerate((
        (q_hbm, qbuf.at[0]), (k_hbm, kbuf.at[0]), (v_hbm, vbuf.at[0]), (eh_hbm, ehv), (ed_hbm, edv),
        (er_hbm, erv), (res_hbm, resv), (pin_hbm, pin), (pout_hbm, pfull.at[0]),
    )):
        copy = pltpu.make_async_copy(src, dst, lsem.at[n])
        local.append(copy)

    def fetch(first, last):
        for n in range(first, last):
            local[n].start()

    fetch(0, 3)

    barrier = pltpu.get_barrier_semaphore()

    greeted = [{"seq": y * NZ + lax.rem(z + r, NZ)} for r in range(1, NZ)]
    greeted += [{"seq": lax.rem(y + r, NY) * NZ + z} for r in range(1, NY)]
    greeted += [{"mp": lax.rem(x + r, NX)} for r in range(1, NX)]
    greeted += [{"section": 1 - sec, "seq": lax.rem(y + r, NY) * NZ + z} for r in range(NY)]
    for device in greeted:
        pl.semaphore_signal(barrier, inc=1, device_id=device, device_id_type=MESH)
    pl.semaphore_wait(barrier, len(greeted))

    def q_copy(d, t, half):
        cols = pl.ds(half * HALF, HALF)
        src = qbuf.at[(8 - t) % 8 if d == 0 else t, :, cols]
        dst = qbuf.at[7 - t if d == 0 else t + 1, :, cols]
        return rcopy(src, dst, q_s.at[d, t, half], q_r.at[d, t, half], zp if d == 0 else zm)

    def kv_copy(n):
        src, dst, dev = (
            (kbuf.at[0], kbuf.at[3], yp), (kbuf.at[0], kbuf.at[1], ym),
            (vbuf.at[0], vbuf.at[3], yp), (vbuf.at[0], vbuf.at[1], ym),
            (kbuf.at[3], kbuf.at[2], yp), (vbuf.at[1], vbuf.at[2], ym),
        )[n]
        return rcopy(src, dst, kv_s.at[n], kv_r.at[n], dev)

    q_copies = [[{h: q_copy(d, t, h) for h in ((0, 1) if t < 3 else (d,))} for t in range(4)] for d in range(2)]
    kv_copies = [kv_copy(n) for n in range(6)]
    for n in range(3):
        local[n].wait()
    fetch(3, 9)
    for half in range(2):
        for d in range(2):
            go(q_copies[d][0][half])
    go(kv_copies[0])
    go(kv_copies[1])
    go(kv_copies[2])
    go(kv_copies[3])

    def x_copies(phase, src_of, dst_of, which=(1, 2, 3)):
        return {
            r: rcopy(src_of(r), dst_of(NX - r), x_s.at[phase, r - 1], x_r.at[phase, NX - r - 1],
                     {"mp": lax.rem(x + r, NX)})
            for r in which
        }

    def y_copies(n, ref_of):
        return {
            r: rcopy(ref_of(), ref_of(), gy_s.at[n, r - 1], gy_r.at[n, NY - r - 1],
                     {"seq": lax.rem(y + r, NY) * NZ + z})
            for r in (1, 2, 3)
        }

    def core_copy(n, ref):
        return rcopy(ref, ref, gx_s.at[n], gx_r.at[n], {"section": 1 - sec})

    def group_copies(n, pieces, group):
        copies = []
        for ds in range(2):
            for r in range(NY):
                if ds or r:
                    to_sec, to_y = lax.rem(sec + ds, 2), lax.rem(y + r, NY)
                    copies.append(rcopy(
                        pieces.at[to_sec, to_y], group.at[x, sec, y],
                        gg_s.at[n, ds * NY + r], gg_r.at[n, ds * NY + (NY - r) % NY],
                        {"section": to_sec, "seq": to_y * NZ + z}))
        return copies

    def send_pieces(copies, rows, pieces, group):
        for a in range(2):
            for b in range(NY):
                pieces[a, b] = rows[:, (a * NY + b) * 256:(a * NY + b + 1) * 256]
        for copy in copies:
            go(copy)
        group[x, sec, y] = pieces[sec, y]

    local[3].wait()
    local[4].wait()
    enc_copies = x_copies(0, lambda r: esend.at[r], lambda r: erecv.at[r])
    for r in (2, 1, 3, 0):
        cols = pl.ds(pl.multiple_of(lax.rem(x + r, NX) * CH, CH), CH)
        esend[r] = dot(ehv[...], edv[:, cols]).astype(BF16)
        if r:
            go(enc_copies[r])

    core_rows = pl.ds(pl.multiple_of(sec * (PROJ // 2), PROJ // 2), PROJ // 2)
    p_copies = x_copies(9, lambda r: pfull.at[0, core_rows], lambda r: pfull.at[r, core_rows], (1, 3))

    def relay(n):
        part = pl.ds(pl.multiple_of(sec * (PROJ // 2) + n * PART, PART), PART)
        return rcopy(pfull.at[(3, 1)[n], part], pfull.at[2, part], pr_s.at[n], pr_r.at[n],
                     {"mp": lax.rem(x + (1, 3)[n], NX)})

    relays = [relay(0), relay(1)]
    pc_copies = {r: rcopy(pfull.at[r, core_rows], pfull.at[r, core_rows], pc_s.at[r - 1], pc_r.at[r - 1],
                          {"section": 1 - sec}) for r in (1, 2, 3)}
    ids = iota((16, NSEQ * ROWS), 0)
    seg = seg_ref[...]
    below = jnp.sum(jnp.where(seg < ids, 1.0, 0.0), axis=1, keepdims=True)
    upto = jnp.sum(jnp.where(seg <= ids, 1.0, 0.0), axis=1, keepdims=True)
    lane = iota((16, HD), 1)
    tail = jnp.full((HD - 16, HD), 1e9, F32)
    segrow[0] = jnp.concatenate([jnp.broadcast_to(below, lane.shape), tail], axis=0).T
    segrow[1] = jnp.concatenate([jnp.broadcast_to(upto, lane.shape), tail], axis=0).T

    def image_columns(device):
        place = (iota((ROWS, HD), 0) * NSEQ + device).astype(F32)
        return (place >= segrow[0]) & (place < segrow[1])

    for r in range(NY):
        device = lax.rem(y + r, NY) * NZ + z
        ko[r] = jnp.where(image_columns(device), SAME, 0.0).astype(BF16)

    def forward_q(t, half):
        for d in range(2):
            if half in q_copies[d][t]:
                take(q_copies[d][t][half])
            if t < 3 and half in q_copies[d][t + 1]:
                go(q_copies[d][t + 1][half])

    def own(ref):
        return jnp.concatenate([ref[pl.ds(3 * x + i, 1), :] for i in range(3)], axis=1)

    stat_copies = x_copies(1, lambda r: estat, lambda r: estat_in.at[r])
    pad = jnp.zeros((HD - 8, HD), F32)
    row8 = iota((8, HD), 0)
    counts = cnt_ref[...].astype(F32)

    def row_y(r):
        peer = lax.rem(y + r, NY)
        return rcopy(packed.at[peer], arecv.at[y], ay_s.at[r - 1], ay_r.at[NY - r - 1], {"seq": peer * NZ + z})

    def row_z(r):
        peer = lax.rem(z + r, NZ)
        return rcopy(aturn.at[peer], alast.at[z], az_s.at[r - 1], az_r.at[NZ - r - 1], {"seq": y * NZ + peer})

    row_ys = {r: row_y(r) for r in range(1, NY)}
    row_zs = {r: row_z(r) for r in range(1, NZ)}
    def sum_encoder():
        local[5].wait()
        for r in (1, 2, 3):
            take(enc_copies[NX - r])
        enc = esend[0].astype(F32)
        for r in (1, 2, 3):
            enc = enc + erecv[r].astype(F32)
        enc = erv[...].astype(F32) + own(ls_ref) * enc
        share[...] = enc
        lane = iota((CAP, HD), 1)
        total = jnp.sum(enc, axis=1, keepdims=True)
        square = jnp.sum(enc * enc, axis=1, keepdims=True)
        packed_stat = jnp.where(lane == 0, total, jnp.where(lane == 1, square, 0.0))
        for b in range(2):
            estat[:, b * HD:(b + 1) * HD] = packed_stat[b * HD:(b + 1) * HD].T[0:8]
        for r in (2, 1, 3):
            go(stat_copies[r])

    def gather_out():
        local[8].wait()
        for r in (1, 3):
            go(p_copies[r])

    def relay_out():
        for n in range(2):
            take(p_copies[(1, 3)[n]])
            go(relays[n])
            go(pc_copies[(3, 1)[n]])


    def send_rows():
        for r in (1, 2, 3):
            take(stat_copies[NX - r])
        both = estat[...]
        for r in (1, 2, 3):
            both = both + estat_in[r]
        mean = both[0:1] * (1.0 / ENC_D)
        scale = lax.rsqrt(both[1:2] * (1.0 / ENC_D) - mean * mean + 1e-6)
        gain = own(gain_ref)
        bias = own(bias_ref)
        parts = []
        for b in range(2):
            cut = slice(b * HD, (b + 1) * HD)
            rows = jnp.where(row8 == 0, mean[:, cut], jnp.where(row8 == 1, scale[:, cut], 0.0))
            cols = jnp.concatenate([rows, pad], axis=0).T
            parts.append((((share[cut] - cols[:, 0:1]) * cols[:, 1:2]) * gain + bias).astype(BF16))
        feature = jnp.concatenate(parts, axis=0)
        before = jnp.sum(jnp.where(iota((1, NSEQ), 1) < seq, counts, 0.0), axis=1, keepdims=True).astype(I32)
        row = iota((CAP, CAP), 0)
        wanted = (row & 7) * NSEQ + (((row >> 3) - before) & (NSEQ - 1))
        permutation = jnp.where(iota((CAP, CAP), 1) == wanted, 1.0, 0.0).astype(BF16)
        packed[...] = dot(permutation, feature).reshape(NY, NZ, 8, CH)

        for r in (2, 1, 3):
            go(row_ys[r])
        arecv[pl.ds(y, 1)] = packed[pl.ds(y, 1)]

    def attend(pair):
        keys_image = ko[...].reshape(NY * ROWS, HD)
        image = jnp.concatenate(
            [jnp.where(image_columns(y * NZ + lax.rem(z + r, NZ)), 1.0, 0.0).astype(BF16) for r in pair], axis=0)
        scores, probs = {}, {}
        for step in range(HEADS + 2):
            if step < HEADS:
                cols = slice(step * HD, (step + 1) * HD)
                keys = jnp.concatenate([kbuf[:, :, cols].reshape(NY * ROWS, HD), keys_image], axis=1)
                rows = jnp.concatenate([qbuf[r, :, cols] for r in pair], axis=0)
                scores[step] = dot(keys, jnp.concatenate([rows, image], axis=1), 1, 1)
            if 1 <= step <= HEADS:
                h = step - 1
                score = scores.pop(h)
                best = jnp.max(score, axis=0, keepdims=True)
                prob = jnp.exp2((score - best) * EXP_SCALE)
                total = jnp.sum(prob, axis=0, keepdims=True)
                half, i = h // 3, h % 3
                for n, r in enumerate(pair):
                    cut = slice(n * ROWS, (n + 1) * ROWS)
                    stats[r, half, i:i + 1] = best[:, cut] * EXP_SCALE
                    stats[r, half, 3 + i:4 + i] = total[:, cut]
                probs[h] = prob.astype(BF16)
            if step >= 2:
                h = step - 2
                half, i = h // 3, h % 3
                mixed = dot(vt[h * HD:(h + 1) * HD], probs.pop(h)).astype(BF16)
                for n, r in enumerate(pair):
                    opart[r, half, i * HD:(i + 1) * HD] = mixed[:, n * ROWS:(n + 1) * ROWS]

    def turn_values(r):
        vt[:, r * ROWS:(r + 1) * ROWS] = vbuf[r].T

    def o_copy(d, t, half):
        r = 4 - t if d == 0 else 4 + t
        dev = zp if d == 0 else zm
        return (rcopy(opart.at[r, half], oin.at[d, t, half], o_s.at[d, t, half], o_r.at[d, t, half], dev),
                rcopy(stats.at[r, half], sin.at[d, t, half], os_s.at[d, t, half], os_r.at[d, t, half], dev))

    o_copies = [[{h: o_copy(d, t, h) for h in ((0, 1) if t else (d,))} for t in range(4)] for d in range(2)]

    def go_o(d, t, half):
        for copy in o_copies[d][t][half]:
            go(copy)

    def take_o(d, t, half):
        for copy in o_copies[d][t][half]:
            take(copy)

    forward_q(0, 0)
    forward_q(0, 1)
    forward_q(1, 0)
    take(kv_copies[0])
    go(kv_copies[4])
    forward_q(1, 1)
    take(kv_copies[3])
    go(kv_copies[5])
    take(kv_copies[1])
    take(kv_copies[2])
    for r in (0, 1, 3):
        turn_values(r)
    forward_q(2, 0)
    sum_encoder()
    gather_out()
    forward_q(2, 1)
    for n in (4, 5):
        take(kv_copies[n])
    turn_values(2)
    attend((5, 3))
    forward_q(3, 0)
    forward_q(3, 1)
    attend((4, 0))
    for d in range(2):
        go_o(d, 0, d)
    for d in range(2):
        go_o(d, 1, 1 - d)
    send_rows()
    attend((6, 2))

    def merge(r, d, t, half):
        mine, other = stats[r, half], sin[d, t, half]
        for i in range(3):
            m0, m1 = mine[i:i + 1], other[i:i + 1]
            best = jnp.maximum(m0, m1)
            f0, f1 = jnp.exp2(m0 - best), jnp.exp2(m1 - best)
            rows = slice(i * HD, (i + 1) * HD)
            mixed = opart[r, half, rows].astype(F32) * f0 + oin[d, t, half, rows].astype(F32) * f1
            opart[r, half, rows] = mixed.astype(BF16)
            stats[r, half, i:i + 1] = best
            stats[r, half, 3 + i:4 + i] = mine[3 + i:4 + i] * f0 + other[3 + i:4 + i] * f1

    for t in (1, 2, 3):
        if t == 2:
            attend((7, 1))
        for turn in range(2):
            for d in range(2):
                half = d if turn else 1 - d
                if t == 1 and not turn:
                    continue
                take_o(d, t - 1, half)
                merge(4 - t if d == 0 else 4 + t, d, t - 1, half)
                go_o(d, t, half)
        if t == 2:
            relay_out()
    for r in (1, 2, 3):
        take(row_ys[NY - r])
    for n in range(NZ):
        aturn[n] = arecv[:, n].reshape(NY * 8, CH).astype(BF16)
    alast[pl.ds(z, 1)] = aturn[pl.ds(z, 1)]
    for r in (4, 3, 5, 2, 6, 1, 7):
        go(row_zs[r])
    for half in range(2):
        for d in range(2):
            take_o(d, 3, half)
            merge(0, d, 3, half)
    for n in range(2):
        take(relays[n])
    go(pc_copies[2])
    local[6].wait()
    for h in range(HEADS):
        half, i = h // 3, h % 3
        cols = slice(h * HD, (h + 1) * HD)
        attn = opart[0, half, i * HD:(i + 1) * HD].astype(F32) / stats[0, half, 3 + i:4 + i]
        attn = attn.T.astype(BF16).astype(F32)
        hgrp[sec, y, :, cols] = (resv[:, cols].astype(F32) + attn).astype(BF16)

    h_copies = y_copies(0, lambda: hgrp.at[sec, y])
    for r in (2, 1, 3):
        go(h_copies[r])
    local[7].wait()
    hidden = hgrp[sec, y]
    f_copies = []
    for c in range(2):
        cols = slice(c * 1024, (c + 1) * 1024)
        fpart[:, :, cols] = dot(hidden, pin[:, cols]).astype(BF16).reshape(NX, 32, 1024)
        f_copies.append(x_copies(
            2 + c, lambda r: fpart.at[lax.rem(x + r, NX), :, cols], lambda r: frecv.at[r, :, cols]))
        for r in (2, 1, 3):
            go(f_copies[c][r])
    column = iota((NSEQ, CAP), 1)
    e_of = ((column >> 3) & (NY - 1)) * NZ + (column >> 5)
    device = iota((NSEQ, CAP), 0)
    counts8 = jnp.broadcast_to(counts, (8, NSEQ)).astype(BF16)
    start = dot(counts8, jnp.where(device < e_of, 1.0, 0.0).astype(BF16))[0:1]
    count = dot(counts8, jnp.where(device == e_of, 1.0, 0.0).astype(BF16))[0:1]
    low = start + ((iota((1, CAP), 1) & 7) * NSEQ).astype(F32)
    high = jnp.minimum(low + float(NSEQ), start + count)
    place = (iota((ROWS, CAP), 0) * NSEQ + seq).astype(F32)
    chosen = jnp.where((place >= low) & (place < high), 1.0, 0.0).astype(BF16)

    for c in range(2):
        cols = slice(c * 1024, (c + 1) * 1024)
        for r in (1, 2, 3):
            take(f_copies[c][NX - r])
        value = fpart[x, :, cols].astype(F32)
        for r in (1, 2, 3):
            value = value + frecv[r, :, cols].astype(F32)
        first[:, cols] = value
        act_rows[:, cols] = (value * jax.nn.sigmoid(value)).astype(BF16)
    act = act_rows[...]
    act_pieces = group_copies(0, apiece, agrp)
    send_pieces(act_pieces, act, apiece, agrp)
    for r in range(1, NZ):
        take(row_zs[NZ - r])
    tsend[...] = dot(chosen, alast[...].reshape(CAP, CH)).astype(BF16).reshape(NX, 32, CH)
    t_copies = x_copies(5, lambda r: tsend.at[lax.rem(x + r, NX)], lambda r: tgt.at[r])
    for r in (2, 1, 3):
        go(t_copies[r])
    tgt[0] = tsend[x]
    column_weight[...] = jnp.broadcast_to(aw_ref[...], (ROWS, ROWS)).T
    for r in range(NX):
        if r:
            take(pc_copies[r])
        if r == 2:
            for copy in act_pieces:
                take(copy)
            act_copies = x_copies(4, lambda r: agrp.at[x], lambda r: agrp.at[x])
            for r2 in (2, 1, 3):
                go(act_copies[r2])
        second[r] = dot(act, pfull[r])
    for r in (1, 2, 3):
        take(t_copies[NX - r])
    inner = square_z = square_f = 0.0
    for r in range(NX):
        tf = tgt[r].astype(F32)
        inner = inner + jnp.sum(second[r] * tf, axis=1, keepdims=True)
        square_z = square_z + jnp.sum(second[r] * second[r], axis=1, keepdims=True)
        square_f = square_f + jnp.sum(tf * tf, axis=1, keepdims=True)
    norm_z = jnp.sqrt(square_z + 1e-6)
    norm_f = jnp.sqrt(square_f + 1e-6)
    aligned = inner / (norm_z * norm_f)
    weight = column_weight[pl.ds(pl.multiple_of(x * 32, 32), 32), 0:1]
    by_target = -weight / (norm_z * norm_f)
    by_second = weight * aligned / (norm_z * norm_z)
    b_copies = x_copies(6, lambda r: bsend.at[r], lambda r: bgrp.at[sec, y, x])
    for r in (2, 1, 3, 0):
        bsend[r] = (by_target * tgt[r].astype(F32) + by_second * second[r]).astype(BF16)
        if r:
            go(b_copies[r])
    bgrp[sec, y, x] = bsend[0]
    alall[x] = jnp.broadcast_to(aligned, (32, HD))
    l_copies = x_copies(7, lambda r: alall.at[x], lambda r: alall.at[x])
    for r in (2, 1, 3):
        go(l_copies[r])
    upstream = dot(bsend[0], pfull[0], 1, 1)
    for r in (1, 2, 3):
        upstream = upstream + dot(bsend[r], pfull[r], 1, 1)
    value = first[...]
    sig = jax.nn.sigmoid(value)
    dfirst = (upstream * sig * (1.0 + value * (1.0 - sig))).astype(BF16)
    d_pieces = group_copies(1, dpiece, dgrp)
    send_pieces(d_pieces, dfirst, dpiece, dgrp)
    for r in (1, 2, 3):
        take(b_copies[NX - r])
    back_copies = y_copies(1, lambda: bgrp.at[sec, y])
    for r in (2, 1, 3):
        go(back_copies[r])
    for r in (1, 2, 3):
        take(h_copies[NY - r])
    hidden_core = core_copy(0, hgrp.at[sec])
    go(hidden_core)
    for copy in d_pieces:
        take(copy)
    d_copies = x_copies(8, lambda r: dgrp.at[x], lambda r: dgrp.at[x])
    for r in (2, 1, 3):
        go(d_copies[r])
    for r in (1, 2, 3):
        take(l_copies[NX - r])
    al_ref[...] = alall[...].reshape(ROWS, HD).T[0:1]
    for r in (1, 2, 3):
        take(back_copies[NY - r])
    back_core = core_copy(1, bgrp.at[sec])
    go(back_core)
    for r in (1, 2, 3):
        take(act_copies[NX - r])
    take(back_core)

    def z_copies(n):
        copies = {}
        for r in range(1, NZ):
            peer = lax.rem(z + r, NZ)
            copies[r] = rcopy(gz.at[n, peer], gz_in.at[n, NZ - r], gz_s.at[n, r - 1], gz_r.at[n, NZ - r - 1],
                              {"seq": y * NZ + peer})
        return copies

    z_all = [z_copies(n) for n in range(3)]

    def product(n, left, right_of):
        value = 0.0
        for b in range(NX):
            rows = left[b].reshape(CAP, CAP)
            value = value + dot(rows, right_of(b).reshape(CAP, CH), 0, 0)
        gz[n] = value.astype(BF16).reshape(NZ, 32, CH)
        for r in (4, 3, 5, 2, 6, 1, 7):
            go(z_all[n][r])

    def finish(n):
        for r in range(1, NZ):
            take(z_all[n][NZ - r])
        value = gz[n, z].astype(F32)
        for r in range(1, NZ):
            value = value + gz_in[n, r].astype(F32)
        return value

    product(0, agrp, lambda b: bgrp[:, :, b])
    take(hidden_core)
    for r in (1, 2, 3):
        take(d_copies[NX - r])
    for n in range(2):
        product(1 + n, dgrp, lambda b: hgrp[:, :, b * 32:(b + 1) * 32, n * CH:(n + 1) * CH])
    go_ref[...] = finish(0)
    for n in range(2):
        gi_ref[:, n * CH:(n + 1) * CH] = finish(1 + n)

    for copy in pending:
        copy.wait_send()


def body(
    queries, keys, values, residual, segment_ids, enc_counts, enc_hidden, enc_down, enc_resid,
    layer_scale, norm_gain, norm_bias, proj_in, proj_out, align_weight,
):
    anywhere = pl.BlockSpec(memory_space=pl.ANY)
    vmem = pl.BlockSpec(memory_space=pltpu.VMEM)
    V, D = pltpu.VMEM, pltpu.SemaphoreType.DMA
    scratch = [
        V((NZ, ROWS, WIDTH), BF16), V((NY, ROWS, WIDTH), BF16), V((NY, ROWS, WIDTH), BF16),
        V((WIDTH, NY * ROWS), BF16), V((NY, ROWS, HD), BF16), V((ROWS, WIDTH), BF16),
        V((CAP, FF), BF16), V((FF, ENC_D), BF16), V((CAP, CH), BF16),
        V((WIDTH, PROJ), BF16), V((NX, PROJ, CH), BF16),
        V((NZ, 2, HALF, HD), BF16), V((NZ, 2, 8, HD), F32),
        V((2, 4, 2, HALF, HD), BF16), V((2, 4, 2, 8, HD), F32),
        V((NX, CAP, CH), BF16), V((NX, CAP, CH), BF16), V((CAP, CH), F32),
        V((8, CAP), F32), V((NX, 8, CAP), F32),
        V((NY, NZ, 8, CH), F32), V((NY, NZ, 8, CH), F32), V((NZ, 32, CH), BF16), V((NZ, 32, CH), BF16),
        V((NX, 32, CH), BF16), V((NX, 32, CH), BF16),
        V((2, NY, ROWS, WIDTH), BF16), V((NX, 32, PROJ), BF16), V((NX, 32, PROJ), BF16), V((32, PROJ), F32),
        V((32, PROJ), BF16), V((NX, 32, CH), F32), V((NX, 32, CH), BF16), V((2, NY, NX, 32, CH), BF16),
        V((NX, 32, HD), F32), V((ROWS, ROWS), F32),
        V((2, NY, 32, 256), BF16), V((NX, 2, NY, 32, 256), BF16),
        V((2, NY, 32, 256), BF16), V((NX, 2, NY, 32, 256), BF16),
        V((3, NZ, 32, CH), BF16), V((3, NZ, 32, CH), BF16),
        V((2, HD, HD), F32),
    ]
    scratch += [
        D((9,)), D((2, 4, 2)), D((2, 4, 2)), D((6,)), D((6,)),
        D((2, 4, 2)), D((2, 4, 2)), D((2, 4, 2)), D((2, 4, 2)),
        D((10, 3)), D((10, 3)), D((3,)), D((3,)), D((2,)), D((2,)), D((3,)), D((3,)), D((7,)), D((7,)),
        D((2,)), D((2,)), D((2, 3)), D((2, 3)), D((3, 7)), D((3, 7)), D((2, 8)), D((2, 8)),
    ]
    aligned, grad_in_t, grad_out = pl.pallas_call(
        kernel,
        out_shape=(
            jax.ShapeDtypeStruct((1, ROWS), F32),
            jax.ShapeDtypeStruct((32, WIDTH), F32),
            jax.ShapeDtypeStruct((32, CH), F32),
        ),
        in_specs=[anywhere] * 4 + [vmem] * 2 + [anywhere] * 3 + [vmem] * 3 + [anywhere] * 2 + [vmem],
        out_specs=(vmem, vmem, vmem),
        scratch_shapes=scratch,
        compiler_params=pltpu.CompilerParams(
            collective_id=0, has_side_effects=True, vmem_limit_bytes=56 * 1024 * 1024
        ),
        name="align",
    )(
        queries, keys, values, residual, segment_ids, enc_counts, enc_hidden, enc_down, enc_resid,
        layer_scale.reshape(-1, HD), norm_gain.reshape(-1, HD), norm_bias.reshape(-1, HD),
        proj_in, proj_out, align_weight.reshape(1, -1),
    )

    def hand_on(a, b, c, a_out, b_out, c_out):
        a_out[...] = a[...]
        b_out[...] = b[...]
        c_out[...] = c[...]

    aligned, grad_in_t, grad_out = pl.pallas_call(
        hand_on,
        out_shape=tuple(jax.ShapeDtypeStruct(v.shape, F32) for v in (aligned, grad_in_t, grad_out)),
        in_specs=[vmem] * 3,
        out_specs=(vmem, vmem, vmem),
        name="hand_on",
    )(aligned, grad_in_t, grad_out)
    return aligned.reshape(-1), grad_in_t, grad_out


def solution(mesh):
    return jax.shard_map(
        body,
        mesh=mesh,
        in_specs=(
            P(("section", "seq"), "mp"),
            P(("section", "seq"), "mp"),
            P(("section", "seq"), "mp"),
            P(("section", "seq"), "mp"),
            P("section", None),
            P("section", None),
            P(("section", "seq"), "mp"),
            P("mp", None),
            P(("section", "seq"), "mp"),
            P(),
            P(),
            P(),
            P("mp", None),
            P(None, "mp"),
            P(("section", "seq")),
        ),
        out_specs=(P(("section", "seq")), P(("section", "seq"), "mp"), P(("section", "seq"), "mp")),
        check_vma=False,
    )
```

```python
import math

import jax
import jax.numpy as jnp
from jax import lax
from jax.experimental import pallas as pl
from jax.experimental.pallas import tpu as pltpu
from jax.sharding import PartitionSpec as P

MESH = pl.DeviceIdType.MESH
F32, BF16, I32 = jnp.float32, jnp.bfloat16, jnp.int32
HD = 128
ENC_D = 1536
NX, NY, NZ = 4, 4, 8
NSEQ = NY * NZ
ROWS = 128
CAP = 256
WIDTH = 768
HEADS = 6
HALF = 384
CH = 384
FF = 1024
PROJ = 2048
PART = 512
SAME = 8192.0
EXP_SCALE = math.log2(math.e) * HD ** (-0.5)


def rcopy(src, dst, send, recv, dev):
    return pltpu.make_async_remote_copy(
        src_ref=src, dst_ref=dst, send_sem=send, recv_sem=recv, device_id=dev, device_id_type=MESH
    )


def iota(shape, dim):
    return lax.broadcasted_iota(I32, shape, dim)


def dot(a, b, ca=1, cb=0):
    return lax.dot_general(a, b, (((ca,), (cb,)), ((), ())), preferred_element_type=F32)


def kernel(
    q_hbm, k_hbm, v_hbm, res_hbm, seg_ref, cnt_ref, eh_hbm, ed_hbm, er_hbm, ls_ref, gain_ref, bias_ref,
    pin_hbm, pout_hbm, aw_ref,
    al_ref, gi_ref, go_ref,
    qbuf, kbuf, vbuf, vt, ko, resv, ehv, edv, erv, pin, pfull,
    opart, stats, oin, sin,
    esend, erecv, share, estat, estat_in, packed, arecv, aturn, alast, tsend, tgt,
    hgrp, fpart, frecv, first, act_rows, second, bsend, bgrp, alall, column_weight,
    apiece, agrp, dpiece, dgrp, go_z, go_in, gi_z, gi_in, segrow,
    lsem, q_s, q_r, kv_s, kv_r, o_s, o_r, os_s, os_r, x_s, x_r, pc_s, pc_r, pr_s, pr_r, ay_s, ay_r, az_s, az_r,
    gx_s, gx_r, gy_s, gy_r, gz_s, gz_r, gg_s, gg_r, gi_s, gi_r,
):
    sec = lax.axis_index("section")
    seq = lax.axis_index("seq")
    x = lax.axis_index("mp")
    y = seq // NZ
    z = lax.rem(seq, NZ)
    zp = {"seq": y * NZ + lax.rem(z + 1, NZ)}
    zm = {"seq": y * NZ + lax.rem(z + NZ - 1, NZ)}
    yp = {"seq": lax.rem(y + 1, NY) * NZ + z}
    ym = {"seq": lax.rem(y + NY - 1, NY) * NZ + z}
    pending = []

    def go(copy):
        copy.start()
        pending.append(copy)
        return copy

    def take(copy):
        copy.wait_recv()

    local = []
    for n, (src, dst) in enumerate((
        (q_hbm, qbuf.at[0]), (k_hbm, kbuf.at[0]), (v_hbm, vbuf.at[0]), (eh_hbm, ehv), (ed_hbm, edv),
        (er_hbm, erv), (res_hbm, resv), (pin_hbm, pin), (pout_hbm, pfull.at[:, pl.ds(0, CH)]),
    )):
        copy = pltpu.make_async_copy(src, dst, lsem.at[n])
        local.append(copy)

    def fetch(first, last):
        for n in range(first, last):
            local[n].start()

    fetch(0, 3)

    barrier = pltpu.get_barrier_semaphore()

    greeted = [{"seq": y * NZ + lax.rem(z + r, NZ)} for r in range(1, NZ)]
    greeted += [{"seq": lax.rem(y + r, NY) * NZ + z} for r in range(1, NY)]
    greeted += [{"mp": lax.rem(x + r, NX)} for r in range(1, NX)]
    greeted += [{"section": 1 - sec, "seq": lax.rem(y + r, NY) * NZ + z} for r in range(NY)]
    for device in greeted:
        pl.semaphore_signal(barrier, inc=1, device_id=device, device_id_type=MESH)
    pl.semaphore_wait(barrier, len(greeted))

    def q_copy(d, t, half):
        cols = pl.ds(half * HALF, HALF)
        src = qbuf.at[(8 - t) % 8 if d == 0 else t, :, cols]
        dst = qbuf.at[7 - t if d == 0 else t + 1, :, cols]
        return rcopy(src, dst, q_s.at[d, t, half], q_r.at[d, t, half], zp if d == 0 else zm)

    def kv_copy(n):
        src, dst, dev = (
            (kbuf.at[0], kbuf.at[3], yp), (kbuf.at[0], kbuf.at[1], ym),
            (vbuf.at[0], vbuf.at[3], yp), (vbuf.at[0], vbuf.at[1], ym),
            (kbuf.at[3], kbuf.at[2], yp), (vbuf.at[1], vbuf.at[2], ym),
        )[n]
        return rcopy(src, dst, kv_s.at[n], kv_r.at[n], dev)

    q_copies = [[{h: q_copy(d, t, h) for h in ((0, 1) if t < 3 else (d,))} for t in range(4)] for d in range(2)]
    kv_copies = [kv_copy(n) for n in range(6)]
    for n in range(3):
        local[n].wait()
    fetch(3, 9)
    for half in range(2):
        for d in range(2):
            go(q_copies[d][0][half])
    go(kv_copies[0])
    go(kv_copies[1])
    go(kv_copies[2])
    go(kv_copies[3])

    def x_copies(phase, src_of, dst_of, which=(1, 2, 3)):
        return {
            r: rcopy(src_of(r), dst_of(NX - r), x_s.at[phase, r - 1], x_r.at[phase, NX - r - 1],
                     {"mp": lax.rem(x + r, NX)})
            for r in which
        }

    def y_copies(n, ref_of):
        return {
            r: rcopy(ref_of(), ref_of(), gy_s.at[n, r - 1], gy_r.at[n, NY - r - 1],
                     {"seq": lax.rem(y + r, NY) * NZ + z})
            for r in (1, 2, 3)
        }

    def core_copy(n, ref):
        return rcopy(ref, ref, gx_s.at[n], gx_r.at[n], {"section": 1 - sec})

    def group_copies(n, piece_of, slot):
        copies = []
        for ds in range(2):
            for r in range(NY):
                if ds or r:
                    to_sec, to_y = lax.rem(sec + ds, 2), lax.rem(y + r, NY)
                    copies.append(rcopy(
                        piece_of(to_sec, to_y), slot,
                        gg_s.at[n, ds * NY + r], gg_r.at[n, ds * NY + (NY - r) % NY],
                        {"section": to_sec, "seq": to_y * NZ + z}))
        return copies

    local[3].wait()
    local[4].wait()
    enc_copies = x_copies(0, lambda r: esend.at[r], lambda r: erecv.at[r])
    for r in (2, 1, 3, 0):
        cols = pl.ds(pl.multiple_of(lax.rem(x + r, NX) * CH, CH), CH)
        esend[r] = dot(ehv[...], edv[:, cols]).astype(BF16)
        if r:
            go(enc_copies[r])

    core_rows = pl.ds(pl.multiple_of(sec * (PROJ // 2), PROJ // 2), PROJ // 2)
    def out_block(rows, r):
        return pfull.at[rows, pl.ds(r * CH, CH)]

    p_copies = x_copies(9, lambda r: out_block(core_rows, 0), lambda r: out_block(core_rows, r), (1, 3))

    def relay(n):
        part = pl.ds(pl.multiple_of(sec * (PROJ // 2) + n * PART, PART), PART)
        return rcopy(out_block(part, (3, 1)[n]), out_block(part, 2), pr_s.at[n], pr_r.at[n],
                     {"mp": lax.rem(x + (1, 3)[n], NX)})

    relays = [relay(0), relay(1)]
    pc_copies = {r: rcopy(out_block(core_rows, r), out_block(core_rows, r), pc_s.at[r - 1], pc_r.at[r - 1],
                          {"section": 1 - sec}) for r in (1, 2, 3)}
    ids = iota((16, NSEQ * ROWS), 0)
    seg = seg_ref[...]
    below = jnp.sum(jnp.where(seg < ids, 1.0, 0.0), axis=1, keepdims=True)
    upto = jnp.sum(jnp.where(seg <= ids, 1.0, 0.0), axis=1, keepdims=True)
    lane = iota((16, HD), 1)
    tail = jnp.full((HD - 16, HD), 1e9, F32)
    segrow[0] = jnp.concatenate([jnp.broadcast_to(below, lane.shape), tail], axis=0).T
    segrow[1] = jnp.concatenate([jnp.broadcast_to(upto, lane.shape), tail], axis=0).T

    def image_columns(device):
        place = (iota((ROWS, HD), 0) * NSEQ + device).astype(F32)
        return (place >= segrow[0]) & (place < segrow[1])

    for r in range(NY):
        device = lax.rem(y + r, NY) * NZ + z
        ko[r] = jnp.where(image_columns(device), SAME, 0.0).astype(BF16)

    def forward_q(t, half):
        for d in range(2):
            if half in q_copies[d][t]:
                take(q_copies[d][t][half])
            if t < 3 and half in q_copies[d][t + 1]:
                go(q_copies[d][t + 1][half])

    def own(ref):
        return jnp.concatenate([ref[pl.ds(3 * x + i, 1), :] for i in range(3)], axis=1)

    stat_copies = x_copies(1, lambda r: estat, lambda r: estat_in.at[r])
    pad = jnp.zeros((HD - 8, HD), F32)
    row8 = iota((8, HD), 0)
    counts = cnt_ref[...].astype(F32)

    def row_y(r):
        peer = lax.rem(y + r, NY)
        return rcopy(packed.at[peer], arecv.at[y], ay_s.at[r - 1], ay_r.at[NY - r - 1], {"seq": peer * NZ + z})

    def row_z(r):
        peer = lax.rem(z + r, NZ)
        return rcopy(aturn.at[peer], alast.at[z], az_s.at[r - 1], az_r.at[NZ - r - 1], {"seq": y * NZ + peer})

    row_ys = {r: row_y(r) for r in range(1, NY)}
    row_zs = {r: row_z(r) for r in range(1, NZ)}
    def sum_encoder():
        local[5].wait()
        for r in (1, 2, 3):
            take(enc_copies[NX - r])
        enc = esend[0].astype(F32)
        for r in (1, 2, 3):
            enc = enc + erecv[r].astype(F32)
        enc = erv[...].astype(F32) + own(ls_ref) * enc
        share[...] = enc
        lane = iota((CAP, HD), 1)
        total = jnp.sum(enc, axis=1, keepdims=True)
        square = jnp.sum(enc * enc, axis=1, keepdims=True)
        packed_stat = jnp.where(lane == 0, total, jnp.where(lane == 1, square, 0.0))
        for b in range(2):
            estat[:, b * HD:(b + 1) * HD] = packed_stat[b * HD:(b + 1) * HD].T[0:8]
        for r in (2, 1, 3):
            go(stat_copies[r])

    def gather_out():
        local[8].wait()
        for r in (1, 3):
            go(p_copies[r])

    def relay_out():
        for n in range(2):
            take(p_copies[(1, 3)[n]])
            go(relays[n])
            go(pc_copies[(3, 1)[n]])


    def send_rows():
        for r in (1, 2, 3):
            take(stat_copies[NX - r])
        both = estat[...]
        for r in (1, 2, 3):
            both = both + estat_in[r]
        mean = both[0:1] * (1.0 / ENC_D)
        scale = lax.rsqrt(both[1:2] * (1.0 / ENC_D) - mean * mean + 1e-6)
        gain = own(gain_ref)
        bias = own(bias_ref)
        parts = []
        for b in range(2):
            cut = slice(b * HD, (b + 1) * HD)
            rows = jnp.where(row8 == 0, mean[:, cut], jnp.where(row8 == 1, scale[:, cut], 0.0))
            cols = jnp.concatenate([rows, pad], axis=0).T
            parts.append((((share[cut] - cols[:, 0:1]) * cols[:, 1:2]) * gain + bias).astype(BF16))
        feature = jnp.concatenate(parts, axis=0)
        before = jnp.sum(jnp.where(iota((1, NSEQ), 1) < seq, counts, 0.0), axis=1, keepdims=True).astype(I32)
        row = iota((CAP, CAP), 0)
        wanted = (row & 7) * NSEQ + (((row >> 3) - before) & (NSEQ - 1))
        permutation = jnp.where(iota((CAP, CAP), 1) == wanted, 1.0, 0.0).astype(BF16)
        packed[...] = dot(permutation, feature).reshape(NY, NZ, 8, CH)

        for r in (2, 1, 3):
            go(row_ys[r])
        arecv[pl.ds(y, 1)] = packed[pl.ds(y, 1)]

    def attend(pair):
        keys_image = ko[...].reshape(NY * ROWS, HD)
        image = jnp.concatenate(
            [jnp.where(image_columns(y * NZ + lax.rem(z + r, NZ)), 1.0, 0.0).astype(BF16) for r in pair], axis=0)
        scores, probs = {}, {}
        for step in range(HEADS + 2):
            if step < HEADS:
                cols = slice(step * HD, (step + 1) * HD)
                keys = jnp.concatenate([kbuf[:, :, cols].reshape(NY * ROWS, HD), keys_image], axis=1)
                rows = jnp.concatenate([qbuf[r, :, cols] for r in pair], axis=0)
                scores[step] = dot(keys, jnp.concatenate([rows, image], axis=1), 1, 1)
            if 1 <= step <= HEADS:
                h = step - 1
                score = scores.pop(h)
                best = jnp.max(score, axis=0, keepdims=True)
                prob = jnp.exp2((score - best) * EXP_SCALE)
                total = jnp.sum(prob, axis=0, keepdims=True)
                half, i = h // 3, h % 3
                for n, r in enumerate(pair):
                    cut = slice(n * ROWS, (n + 1) * ROWS)
                    stats[r, half, i:i + 1] = best[:, cut] * EXP_SCALE
                    stats[r, half, 3 + i:4 + i] = total[:, cut]
                probs[h] = prob.astype(BF16)
            if step >= 2:
                h = step - 2
                half, i = h // 3, h % 3
                mixed = dot(vt[h * HD:(h + 1) * HD], probs.pop(h)).astype(BF16)
                for n, r in enumerate(pair):
                    opart[r, half, i * HD:(i + 1) * HD] = mixed[:, n * ROWS:(n + 1) * ROWS]

    def turn_values(r):
        vt[:, r * ROWS:(r + 1) * ROWS] = vbuf[r].T

    def o_copy(d, t, half):
        r = 4 - t if d == 0 else 4 + t
        dev = zp if d == 0 else zm
        return (rcopy(opart.at[r, half], oin.at[d, t, half], o_s.at[d, t, half], o_r.at[d, t, half], dev),
                rcopy(stats.at[r, half], sin.at[d, t, half], os_s.at[d, t, half], os_r.at[d, t, half], dev))

    o_copies = [[{h: o_copy(d, t, h) for h in ((0, 1) if t else (d,))} for t in range(4)] for d in range(2)]

    def go_o(d, t, half):
        for copy in o_copies[d][t][half]:
            go(copy)

    def take_o(d, t, half):
        for copy in o_copies[d][t][half]:
            take(copy)

    forward_q(0, 0)
    forward_q(0, 1)
    forward_q(1, 0)
    take(kv_copies[0])
    go(kv_copies[4])
    forward_q(1, 1)
    take(kv_copies[3])
    go(kv_copies[5])
    take(kv_copies[1])
    take(kv_copies[2])
    for r in (0, 1, 3):
        turn_values(r)
    forward_q(2, 0)
    sum_encoder()
    gather_out()
    forward_q(2, 1)
    for n in (4, 5):
        take(kv_copies[n])
    turn_values(2)
    attend((5, 3))
    forward_q(3, 0)
    forward_q(3, 1)
    attend((4, 0))
    for d in range(2):
        go_o(d, 0, d)
    for d in range(2):
        go_o(d, 1, 1 - d)
    send_rows()
    attend((6, 2))

    def merge(r, d, t, half):
        mine, other = stats[r, half], sin[d, t, half]
        for i in range(3):
            m0, m1 = mine[i:i + 1], other[i:i + 1]
            best = jnp.maximum(m0, m1)
            f0, f1 = jnp.exp2(m0 - best), jnp.exp2(m1 - best)
            rows = slice(i * HD, (i + 1) * HD)
            mixed = opart[r, half, rows].astype(F32) * f0 + oin[d, t, half, rows].astype(F32) * f1
            opart[r, half, rows] = mixed.astype(BF16)
            stats[r, half, i:i + 1] = best
            stats[r, half, 3 + i:4 + i] = mine[3 + i:4 + i] * f0 + other[3 + i:4 + i] * f1

    for t in (1, 2, 3):
        if t == 2:
            attend((7, 1))
        for turn in range(2):
            for d in range(2):
                half = d if turn else 1 - d
                if t == 1 and not turn:
                    continue
                take_o(d, t - 1, half)
                merge(4 - t if d == 0 else 4 + t, d, t - 1, half)
                go_o(d, t, half)
        if t == 2:
            relay_out()
    for r in (1, 2, 3):
        take(row_ys[NY - r])
    for n in range(NZ):
        aturn[n] = arecv[:, n].reshape(NY * 8, CH).astype(BF16)
    alast[pl.ds(z, 1)] = aturn[pl.ds(z, 1)]
    for r in (4, 3, 5, 2, 6, 1, 7):
        go(row_zs[r])
    for half in range(2):
        for d in range(2):
            take_o(d, 3, half)
            merge(0, d, 3, half)
    for n in range(2):
        take(relays[n])
    go(pc_copies[2])
    local[6].wait()
    for h in range(HEADS):
        half, i = h // 3, h % 3
        cols = slice(h * HD, (h + 1) * HD)
        attn = opart[0, half, i * HD:(i + 1) * HD].astype(F32) / stats[0, half, 3 + i:4 + i]
        attn = attn.T.astype(BF16).astype(F32)
        hgrp[sec, y, :, cols] = (resv[:, cols].astype(F32) + attn).astype(BF16)

    local[7].wait()
    hidden = hgrp[sec, y]
    f_copies = []
    for c in range(2):
        cols = slice(c * 1024, (c + 1) * 1024)
        fpart[:, :, cols] = dot(hidden, pin[:, cols]).astype(BF16).reshape(NX, 32, 1024)
        f_copies.append(x_copies(
            2 + c, lambda r: fpart.at[lax.rem(x + r, NX), :, cols], lambda r: frecv.at[r, :, cols]))
        for r in (2, 1, 3):
            go(f_copies[c][r])
    column = iota((NSEQ, CAP), 1)
    e_of = ((column >> 3) & (NY - 1)) * NZ + (column >> 5)
    device = iota((NSEQ, CAP), 0)
    counts8 = jnp.broadcast_to(counts, (8, NSEQ)).astype(BF16)
    start = dot(counts8, jnp.where(device < e_of, 1.0, 0.0).astype(BF16))[0:1]
    count = dot(counts8, jnp.where(device == e_of, 1.0, 0.0).astype(BF16))[0:1]
    low = start + ((iota((1, CAP), 1) & 7) * NSEQ).astype(F32)
    high = jnp.minimum(low + float(NSEQ), start + count)
    place = (iota((ROWS, CAP), 0) * NSEQ + seq).astype(F32)
    chosen = jnp.where((place >= low) & (place < high), 1.0, 0.0).astype(BF16)

    for c in range(2):
        cols = slice(c * 1024, (c + 1) * 1024)
        for r in (1, 2, 3):
            take(f_copies[c][NX - r])
        value = fpart[x, :, cols].astype(F32)
        for r in (1, 2, 3):
            value = value + frecv[r, :, cols].astype(F32)
        first[:, cols] = value
        act_rows[:, cols] = (value * jax.nn.sigmoid(value)).astype(BF16)
    act = act_rows[...]
    act_pieces = group_copies(0, lambda a, b: apiece.at[a, b], agrp.at[x, sec, y])
    for a in range(2):
        for b in range(NY):
            apiece[a, b] = act[:, (a * NY + b) * 256:(a * NY + b + 1) * 256]
    for copy in act_pieces:
        go(copy)
    agrp[x, sec, y] = apiece[sec, y]
    h_copies = y_copies(0, lambda: hgrp.at[sec, y])
    for r in (2, 1, 3):
        go(h_copies[r])
    for r in range(1, NZ):
        take(row_zs[NZ - r])
    tsend[...] = dot(chosen, alast[...].reshape(CAP, CH)).astype(BF16).reshape(NX, 32, CH)
    t_copies = x_copies(5, lambda r: tsend.at[lax.rem(x + r, NX)], lambda r: tgt.at[r])
    for r in (2, 1, 3):
        go(t_copies[r])
    tgt[0] = tsend[x]
    column_weight[...] = jnp.broadcast_to(aw_ref[...], (ROWS, ROWS)).T
    take(pc_copies[1])
    wide = 2 * CH
    second[:, 0:wide] = dot(act, pfull[:, 0:wide])
    for copy in act_pieces:
        take(copy)
    act_copies = x_copies(4, lambda r: agrp.at[x], lambda r: agrp.at[x])
    for r in (2, 1, 3):
        go(act_copies[r])
    take(pc_copies[3])
    take(pc_copies[2])
    second[:, wide:ENC_D] = dot(act, pfull[:, wide:ENC_D])
    for r in (1, 2, 3):
        take(t_copies[NX - r])
    inner = square_z = square_f = 0.0
    for r in range(NX):
        tf = tgt[r].astype(F32)
        value = second[:, r * CH:(r + 1) * CH]
        inner = inner + jnp.sum(value * tf, axis=1, keepdims=True)
        square_z = square_z + jnp.sum(value * value, axis=1, keepdims=True)
        square_f = square_f + jnp.sum(tf * tf, axis=1, keepdims=True)
    norm_z = jnp.sqrt(square_z + 1e-6)
    norm_f = jnp.sqrt(square_f + 1e-6)
    aligned = inner / (norm_z * norm_f)
    weight = column_weight[pl.ds(pl.multiple_of(x * 32, 32), 32), 0:1]
    by_target = -weight / (norm_z * norm_f)
    by_second = weight * aligned / (norm_z * norm_z)
    b_copies = x_copies(6, lambda r: bsend.at[r], lambda r: bgrp.at[sec, y, x])
    for r in (2, 1, 3, 0):
        bsend[r] = (by_target * tgt[r].astype(F32) + by_second * second[:, r * CH:(r + 1) * CH]).astype(BF16)
        if r:
            go(b_copies[r])
    bgrp[sec, y, x] = bsend[0]
    alall[x] = jnp.broadcast_to(aligned, (32, HD))
    l_copies = x_copies(7, lambda r: alall.at[x], lambda r: alall.at[x])
    for r in (2, 1, 3):
        go(l_copies[r])
    upstream = dot(jnp.concatenate([bsend[r] for r in range(NX)], axis=1), pfull[...], 1, 1)
    value = first[...]
    sig = jax.nn.sigmoid(value)
    dfirst = (upstream * sig * (1.0 + value * (1.0 - sig))).astype(BF16)
    d_pieces = group_copies(1, lambda a, b: dpiece.at[:, a, b], dgrp.at[:, x, sec, y])
    place = iota((CAP, CAP), 1)
    origin = ((2 * ((place >> 5) & 3) + (place >> 7)) << 5) + (place & 31)
    order = jnp.where(iota((CAP, CAP), 0) == origin, 1.0, 0.0).astype(BF16)
    for a in range(2):
        for b in range(NY):
            columns = dot(dfirst[:, (a * NY + b) * CAP:(a * NY + b + 1) * CAP], order).astype(BF16)
            for half in range(2):
                dpiece[half, a, b] = columns[:, half * HD:(half + 1) * HD]
    for copy in d_pieces:
        go(copy)
    for half in range(2):
        dgrp[half, x, sec, y] = dpiece[half, sec, y]
    for copy in d_pieces:
        take(copy)
    d_copies = []
    for half in range(2):
        d_copies.append(x_copies(8 + 2 * half, lambda r: dgrp.at[half, x], lambda r: dgrp.at[half, x]))
        for r in (2, 1, 3):
            go(d_copies[half][r])
    for r in (1, 2, 3):
        take(b_copies[NX - r])
    back_copies = y_copies(1, lambda: bgrp.at[sec, y])
    for r in (2, 1, 3):
        go(back_copies[r])
    for r in (1, 2, 3):
        take(h_copies[NY - r])
    hidden_core = core_copy(0, hgrp.at[sec])
    go(hidden_core)
    for r in (1, 2, 3):
        take(l_copies[NX - r])
    al_ref[...] = alall[...].reshape(ROWS, HD).T[0:1]
    for r in (1, 2, 3):
        take(back_copies[NY - r])
    back_core = core_copy(1, bgrp.at[sec])
    go(back_core)
    for r in (1, 2, 3):
        take(act_copies[NX - r])
    take(back_core)

    def go_copy(r):
        peer = lax.rem(z + r, NZ)
        return rcopy(go_z.at[peer], go_in.at[NZ - r], gz_s.at[r - 1], gz_r.at[NZ - r - 1], {"seq": y * NZ + peer})

    go_copies = {r: go_copy(r) for r in range(1, NZ)}
    value = 0.0
    for b in range(NX):
        value = value + dot(agrp[b].reshape(CAP, CAP), bgrp[:, :, b].reshape(CAP, CH), 0, 0)
    go_z[...] = value.astype(BF16).reshape(NZ, 32, CH)
    for r in (4, 3, 5, 2, 6, 1, 7):
        go(go_copies[r])
    take(hidden_core)

    def gi_copy(peer, mine):
        return rcopy(gi_z.at[lax.rem(peer, 2), peer // 2], gi_in.at[mine], gi_s.at[peer], gi_r.at[mine],
                     {"seq": y * NZ + peer})

    for half in range(2):
        for r in (1, 2, 3):
            take(d_copies[half][NX - r])
        value = 0.0
        for b in range(NX):
            rows = hgrp[:, :, b * 32:(b + 1) * 32].reshape(CAP, WIDTH)
            value = value + dot(dgrp[half, b].reshape(CAP, HD), rows, 0, 0)
        gi_z[half] = value.astype(BF16).reshape(4, 32, WIDTH)
        odd = lax.rem(z + half, 2)
        for m in (2, 1, 3):
            gi_copy(lax.rem(z + odd + 2 * m, NZ), z).start()

        @pl.when(odd == 1)
        def _():
            gi_copy(lax.rem(z + 1, NZ), z).start()

    for r in range(1, NZ):
        take(go_copies[NZ - r])
    value = go_z[z].astype(F32)
    for r in range(1, NZ):
        value = value + go_in[r].astype(F32)
    go_ref[...] = value
    value = gi_z[lax.rem(z, 2), z // 2].astype(F32)
    for r in range(1, NZ):
        peer = lax.rem(z + r, NZ)
        gi_copy(z, peer).wait_recv()
        value = value + gi_in[peer].astype(F32)
    gi_ref[...] = value
    for r in range(1, NZ):
        gi_copy(lax.rem(z + r, NZ), z).wait_send()

    for copy in pending:
        copy.wait_send()


def body(
    queries, keys, values, residual, segment_ids, enc_counts, enc_hidden, enc_down, enc_resid,
    layer_scale, norm_gain, norm_bias, proj_in, proj_out, align_weight,
):
    anywhere = pl.BlockSpec(memory_space=pl.ANY)
    vmem = pl.BlockSpec(memory_space=pltpu.VMEM)
    V, D = pltpu.VMEM, pltpu.SemaphoreType.DMA
    scratch = [
        V((NZ, ROWS, WIDTH), BF16), V((NY, ROWS, WIDTH), BF16), V((NY, ROWS, WIDTH), BF16),
        V((WIDTH, NY * ROWS), BF16), V((NY, ROWS, HD), BF16), V((ROWS, WIDTH), BF16),
        V((CAP, FF), BF16), V((FF, ENC_D), BF16), V((CAP, CH), BF16),
        V((WIDTH, PROJ), BF16), V((PROJ, ENC_D), BF16),
        V((NZ, 2, HALF, HD), BF16), V((NZ, 2, 8, HD), F32),
        V((2, 4, 2, HALF, HD), BF16), V((2, 4, 2, 8, HD), F32),
        V((NX, CAP, CH), BF16), V((NX, CAP, CH), BF16), V((CAP, CH), F32),
        V((8, CAP), F32), V((NX, 8, CAP), F32),
        V((NY, NZ, 8, CH), F32), V((NY, NZ, 8, CH), F32), V((NZ, 32, CH), BF16), V((NZ, 32, CH), BF16),
        V((NX, 32, CH), BF16), V((NX, 32, CH), BF16),
        V((2, NY, ROWS, WIDTH), BF16), V((NX, 32, PROJ), BF16), V((NX, 32, PROJ), BF16), V((32, PROJ), F32),
        V((32, PROJ), BF16), V((32, ENC_D), F32), V((NX, 32, CH), BF16), V((2, NY, NX, 32, CH), BF16),
        V((NX, 32, HD), F32), V((ROWS, ROWS), F32),
        V((2, NY, 32, 256), BF16), V((NX, 2, NY, 32, 256), BF16),
        V((2, 2, NY, 32, HD), BF16), V((2, NX, 2, NY, 32, HD), BF16),
        V((NZ, 32, CH), BF16), V((NZ, 32, CH), BF16), V((2, 4, 32, WIDTH), BF16), V((NZ, 32, WIDTH), BF16),
        V((2, HD, HD), F32),
    ]
    scratch += [
        D((9,)), D((2, 4, 2)), D((2, 4, 2)), D((6,)), D((6,)),
        D((2, 4, 2)), D((2, 4, 2)), D((2, 4, 2)), D((2, 4, 2)),
        D((11, 3)), D((11, 3)), D((3,)), D((3,)), D((2,)), D((2,)), D((3,)), D((3,)), D((7,)), D((7,)),
        D((2,)), D((2,)), D((2, 3)), D((2, 3)), D((7,)), D((7,)), D((2, 8)), D((2, 8)), D((8,)), D((8,)),
    ]
    aligned, grad_in_t, grad_out = pl.pallas_call(
        kernel,
        out_shape=(
            jax.ShapeDtypeStruct((1, ROWS), F32),
            jax.ShapeDtypeStruct((32, WIDTH), F32),
            jax.ShapeDtypeStruct((32, CH), F32),
        ),
        in_specs=[anywhere] * 4 + [vmem] * 2 + [anywhere] * 3 + [vmem] * 3 + [anywhere] * 2 + [vmem],
        out_specs=(vmem, vmem, vmem),
        scratch_shapes=scratch,
        compiler_params=pltpu.CompilerParams(
            collective_id=0, has_side_effects=True, vmem_limit_bytes=56 * 1024 * 1024
        ),
        name="align",
    )(
        queries, keys, values, residual, segment_ids, enc_counts, enc_hidden, enc_down, enc_resid,
        layer_scale.reshape(-1, HD), norm_gain.reshape(-1, HD), norm_bias.reshape(-1, HD),
        proj_in, proj_out, align_weight.reshape(1, -1),
    )

    def hand_on(a, b, c, a_out, b_out, c_out):
        a_out[...] = a[...]
        b_out[...] = b[...]
        c_out[...] = c[...]

    aligned, grad_in_t, grad_out = pl.pallas_call(
        hand_on,
        out_shape=tuple(jax.ShapeDtypeStruct(v.shape, F32) for v in (aligned, grad_in_t, grad_out)),
        in_specs=[vmem] * 3,
        out_specs=(vmem, vmem, vmem),
        name="hand_on",
    )(aligned, grad_in_t, grad_out)
    return aligned.reshape(-1), grad_in_t, grad_out


def solution(mesh):
    return jax.shard_map(
        body,
        mesh=mesh,
        in_specs=(
            P(("section", "seq"), "mp"),
            P(("section", "seq"), "mp"),
            P(("section", "seq"), "mp"),
            P(("section", "seq"), "mp"),
            P("section", None),
            P("section", None),
            P(("section", "seq"), "mp"),
            P("mp", None),
            P(("section", "seq"), "mp"),
            P(),
            P(),
            P(),
            P("mp", None),
            P(None, "mp"),
            P(("section", "seq")),
        ),
        out_specs=(P(("section", "seq")), P(("section", "seq"), "mp"), P(("section", "seq"), "mp")),
        check_vma=False,
    )
```

```python
import math

import jax
import jax.numpy as jnp
from jax import lax
from jax.experimental import pallas as pl
from jax.experimental.pallas import tpu as pltpu
from jax.sharding import PartitionSpec as P

MESH = pl.DeviceIdType.MESH
F32, BF16, I32 = jnp.float32, jnp.bfloat16, jnp.int32
HD = 128
ENC_D = 1536
NX, NY, NZ = 4, 4, 8
NSEQ = NY * NZ
ROWS = 128
CAP = 256
WIDTH = 768
HEADS = 6
HALF = 384
CH = 384
FF = 1024
PROJ = 2048
PART = 512
SAME = 8192.0
EXP_SCALE = math.log2(math.e) * HD ** (-0.5)


def rcopy(src, dst, send, recv, dev):
    return pltpu.make_async_remote_copy(
        src_ref=src, dst_ref=dst, send_sem=send, recv_sem=recv, device_id=dev, device_id_type=MESH
    )


def iota(shape, dim):
    return lax.broadcasted_iota(I32, shape, dim)


def dot(a, b, ca=1, cb=0):
    return lax.dot_general(a, b, (((ca,), (cb,)), ((), ())), preferred_element_type=F32)


def kernel(
    q_hbm, k_hbm, v_hbm, res_hbm, seg_ref, cnt_ref, eh_hbm, ed_hbm, er_hbm, ls_ref, gain_ref, bias_ref,
    pin_hbm, pout_hbm, aw_ref,
    al_ref, gi_ref, go_ref,
    qbuf, kbuf, vbuf, vt, ko, resv, ehv, edv, erv, pin, pfull,
    opart, stats, oin, sin,
    esend, erecv, share, estat, estat_in, packed, arecv, aturn, alast, tsend, tgt,
    hgrp, fpart, frecv, first, act_rows, second, bsend, bgrp, alall, column_weight,
    apiece, agrp, dpiece, dgrp, go_z, go_in, gi_z, gi_in, segrow,
    lsem, q_s, q_r, kv_s, kv_r, o_s, o_r, os_s, os_r, x_s, x_r, pc_s, pc_r, pr_s, pr_r, ay_s, ay_r, az_s, az_r,
    gx_s, gx_r, gy_s, gy_r, gz_s, gz_r, gg_s, gg_r, gi_s, gi_r,
):
    sec = lax.axis_index("section")
    seq = lax.axis_index("seq")
    x = lax.axis_index("mp")
    y = seq // NZ
    z = lax.rem(seq, NZ)
    zp = {"seq": y * NZ + lax.rem(z + 1, NZ)}
    zm = {"seq": y * NZ + lax.rem(z + NZ - 1, NZ)}
    yp = {"seq": lax.rem(y + 1, NY) * NZ + z}
    ym = {"seq": lax.rem(y + NY - 1, NY) * NZ + z}
    pending = []

    def go(copy):
        copy.start()
        pending.append(copy)
        return copy

    def take(copy):
        copy.wait_recv()

    local = []
    for n, (src, dst) in enumerate((
        (q_hbm, qbuf.at[0]), (k_hbm, kbuf.at[0]), (v_hbm, vbuf.at[0]), (eh_hbm, ehv), (ed_hbm, edv),
        (er_hbm, erv), (res_hbm, resv), (pin_hbm, pin), (pout_hbm, pfull.at[:, pl.ds(0, CH)]),
    )):
        copy = pltpu.make_async_copy(src, dst, lsem.at[n])
        local.append(copy)

    def fetch(first, last):
        for n in range(first, last):
            local[n].start()

    fetch(0, 3)

    barrier = pltpu.get_barrier_semaphore()

    greeted = [{"seq": y * NZ + lax.rem(z + r, NZ)} for r in range(1, NZ)]
    greeted += [{"seq": lax.rem(y + r, NY) * NZ + z} for r in range(1, NY)]
    greeted += [{"mp": lax.rem(x + r, NX)} for r in range(1, NX)]
    greeted += [{"section": 1 - sec, "seq": lax.rem(y + r, NY) * NZ + z} for r in range(NY)]
    for device in greeted:
        pl.semaphore_signal(barrier, inc=1, device_id=device, device_id_type=MESH)
    pl.semaphore_wait(barrier, len(greeted))

    def q_copy(d, t, half):
        cols = pl.ds(half * HALF, HALF)
        src = qbuf.at[(8 - t) % 8 if d == 0 else t, :, cols]
        dst = qbuf.at[7 - t if d == 0 else t + 1, :, cols]
        return rcopy(src, dst, q_s.at[d, t, half], q_r.at[d, t, half], zp if d == 0 else zm)

    def kv_copy(n):
        src, dst, dev = (
            (kbuf.at[0], kbuf.at[3], yp), (kbuf.at[0], kbuf.at[1], ym),
            (vbuf.at[0], vbuf.at[3], yp), (vbuf.at[0], vbuf.at[1], ym),
            (kbuf.at[3], kbuf.at[2], yp), (vbuf.at[1], vbuf.at[2], ym),
        )[n]
        return rcopy(src, dst, kv_s.at[n], kv_r.at[n], dev)

    q_copies = [[{h: q_copy(d, t, h) for h in ((0, 1) if t < 3 else (d,))} for t in range(4)] for d in range(2)]
    kv_copies = [kv_copy(n) for n in range(6)]
    for n in range(3):
        local[n].wait()
    fetch(3, 5)
    for half in range(2):
        for d in range(2):
            go(q_copies[d][0][half])
    go(kv_copies[0])
    go(kv_copies[1])
    go(kv_copies[2])
    go(kv_copies[3])

    def x_copies(phase, src_of, dst_of, which=(1, 2, 3)):
        return {
            r: rcopy(src_of(r), dst_of(NX - r), x_s.at[phase, r - 1], x_r.at[phase, NX - r - 1],
                     {"mp": lax.rem(x + r, NX)})
            for r in which
        }

    def y_copies(n, ref_of):
        return {
            r: rcopy(ref_of(), ref_of(), gy_s.at[n, r - 1], gy_r.at[n, NY - r - 1],
                     {"seq": lax.rem(y + r, NY) * NZ + z})
            for r in (1, 2, 3)
        }

    def core_copy(n, ref):
        return rcopy(ref, ref, gx_s.at[n], gx_r.at[n], {"section": 1 - sec})

    def group_copies(n, piece_of, slot):
        copies = []
        for ds in range(2):
            for r in range(NY):
                if ds or r:
                    to_sec, to_y = lax.rem(sec + ds, 2), lax.rem(y + r, NY)
                    copies.append(rcopy(
                        piece_of(to_sec, to_y), slot,
                        gg_s.at[n, ds * NY + r], gg_r.at[n, ds * NY + (NY - r) % NY],
                        {"section": to_sec, "seq": to_y * NZ + z}))
        return copies

    local[3].wait()
    local[4].wait()
    enc_copies = x_copies(0, lambda r: esend.at[r], lambda r: erecv.at[r])
    for r in (2, 1, 3, 0):
        cols = pl.ds(pl.multiple_of(lax.rem(x + r, NX) * CH, CH), CH)
        esend[r] = dot(ehv[...], edv[:, cols]).astype(BF16)
        if r:
            go(enc_copies[r])

    fetch(5, 9)
    core_rows = pl.ds(pl.multiple_of(sec * (PROJ // 2), PROJ // 2), PROJ // 2)
    def out_block(rows, r):
        return pfull.at[rows, pl.ds(r * CH, CH)]

    p_copies = x_copies(9, lambda r: out_block(core_rows, 0), lambda r: out_block(core_rows, r), (1, 3))

    def relay(n):
        part = pl.ds(pl.multiple_of(sec * (PROJ // 2) + n * PART, PART), PART)
        return rcopy(out_block(part, (3, 1)[n]), out_block(part, 2), pr_s.at[n], pr_r.at[n],
                     {"mp": lax.rem(x + (1, 3)[n], NX)})

    relays = [relay(0), relay(1)]
    pc_copies = {r: rcopy(out_block(core_rows, r), out_block(core_rows, r), pc_s.at[r - 1], pc_r.at[r - 1],
                          {"section": 1 - sec}) for r in (1, 2, 3)}
    ids = iota((16, NSEQ * ROWS), 0)
    seg = seg_ref[...]
    below = jnp.sum(jnp.where(seg < ids, 1.0, 0.0), axis=1, keepdims=True)
    upto = jnp.sum(jnp.where(seg <= ids, 1.0, 0.0), axis=1, keepdims=True)
    lane = iota((16, HD), 1)
    tail = jnp.full((HD - 16, HD), 1e9, F32)
    segrow[0] = jnp.concatenate([jnp.broadcast_to(below, lane.shape), tail], axis=0).T
    segrow[1] = jnp.concatenate([jnp.broadcast_to(upto, lane.shape), tail], axis=0).T

    def image_columns(device):
        place = (iota((ROWS, HD), 0) * NSEQ + device).astype(F32)
        return (place >= segrow[0]) & (place < segrow[1])

    for r in range(NY):
        device = lax.rem(y + r, NY) * NZ + z
        ko[r] = jnp.where(image_columns(device), SAME, 0.0).astype(BF16)

    def forward_q(t, half):
        for d in range(2):
            if half in q_copies[d][t]:
                take(q_copies[d][t][half])
            if t < 3 and half in q_copies[d][t + 1]:
                go(q_copies[d][t + 1][half])

    def own(ref):
        return jnp.concatenate([ref[pl.ds(3 * x + i, 1), :] for i in range(3)], axis=1)

    stat_copies = x_copies(1, lambda r: estat, lambda r: estat_in.at[r])
    pad = jnp.zeros((HD - 8, HD), F32)
    row8 = iota((8, HD), 0)
    counts = cnt_ref[...].astype(F32)

    def row_y(r):
        peer = lax.rem(y + r, NY)
        return rcopy(packed.at[peer], arecv.at[y], ay_s.at[r - 1], ay_r.at[NY - r - 1], {"seq": peer * NZ + z})

    def row_z(r):
        peer = lax.rem(z + r, NZ)
        return rcopy(aturn.at[peer], alast.at[z], az_s.at[r - 1], az_r.at[NZ - r - 1], {"seq": y * NZ + peer})

    row_ys = {r: row_y(r) for r in range(1, NY)}
    row_zs = {r: row_z(r) for r in range(1, NZ)}
    def sum_encoder():
        local[5].wait()
        for r in (1, 2, 3):
            take(enc_copies[NX - r])
        enc = esend[0].astype(F32)
        for r in (1, 2, 3):
            enc = enc + erecv[r].astype(F32)
        enc = erv[...].astype(F32) + own(ls_ref) * enc
        share[...] = enc
        lane = iota((CAP, HD), 1)
        total = jnp.sum(enc, axis=1, keepdims=True)
        square = jnp.sum(enc * enc, axis=1, keepdims=True)
        packed_stat = jnp.where(lane == 0, total, jnp.where(lane == 1, square, 0.0))
        for b in range(2):
            estat[:, b * HD:(b + 1) * HD] = packed_stat[b * HD:(b + 1) * HD].T[0:8]
        for r in (2, 1, 3):
            go(stat_copies[r])

    def gather_out():
        local[8].wait()
        for r in (1, 3):
            go(p_copies[r])

    def relay_out():
        for n in range(2):
            take(p_copies[(1, 3)[n]])
            go(relays[n])
            go(pc_copies[(3, 1)[n]])


    def send_rows():
        for r in (1, 2, 3):
            take(stat_copies[NX - r])
        both = estat[...]
        for r in (1, 2, 3):
            both = both + estat_in[r]
        mean = both[0:1] * (1.0 / ENC_D)
        scale = lax.rsqrt(both[1:2] * (1.0 / ENC_D) - mean * mean + 1e-6)
        gain = own(gain_ref)
        bias = own(bias_ref)
        parts = []
        for b in range(2):
            cut = slice(b * HD, (b + 1) * HD)
            rows = jnp.where(row8 == 0, mean[:, cut], jnp.where(row8 == 1, scale[:, cut], 0.0))
            cols = jnp.concatenate([rows, pad], axis=0).T
            parts.append((((share[cut] - cols[:, 0:1]) * cols[:, 1:2]) * gain + bias).astype(BF16))
        feature = jnp.concatenate(parts, axis=0)
        before = jnp.sum(jnp.where(iota((1, NSEQ), 1) < seq, counts, 0.0), axis=1, keepdims=True).astype(I32)
        row = iota((CAP, CAP), 0)
        wanted = (row & 7) * NSEQ + (((row >> 3) - before) & (NSEQ - 1))
        permutation = jnp.where(iota((CAP, CAP), 1) == wanted, 1.0, 0.0).astype(BF16)
        packed[...] = dot(permutation, feature).reshape(NY, NZ, 8, CH)

        for r in (2, 1, 3):
            go(row_ys[r])
        arecv[pl.ds(y, 1)] = packed[pl.ds(y, 1)]

    def attend(pair):
        keys_image = ko[...].reshape(NY * ROWS, HD)
        image = jnp.concatenate(
            [jnp.where(image_columns(y * NZ + lax.rem(z + r, NZ)), 1.0, 0.0).astype(BF16) for r in pair], axis=0)
        scores, probs = {}, {}
        for step in range(HEADS + 2):
            if step < HEADS:
                cols = slice(step * HD, (step + 1) * HD)
                keys = jnp.concatenate([kbuf[:, :, cols].reshape(NY * ROWS, HD), keys_image], axis=1)
                rows = jnp.concatenate([qbuf[r, :, cols] for r in pair], axis=0)
                scores[step] = dot(keys, jnp.concatenate([rows, image], axis=1), 1, 1)
            if 1 <= step <= HEADS:
                h = step - 1
                score = scores.pop(h)
                best = jnp.max(score, axis=0, keepdims=True)
                prob = jnp.exp2((score - best) * EXP_SCALE)
                total = jnp.sum(prob, axis=0, keepdims=True)
                half, i = h // 3, h % 3
                for n, r in enumerate(pair):
                    cut = slice(n * ROWS, (n + 1) * ROWS)
                    stats[r, half, i:i + 1] = best[:, cut] * EXP_SCALE
                    stats[r, half, 3 + i:4 + i] = total[:, cut]
                probs[h] = prob.astype(BF16)
            if step >= 2:
                h = step - 2
                half, i = h // 3, h % 3
                mixed = dot(vt[h * HD:(h + 1) * HD], probs.pop(h)).astype(BF16)
                for n, r in enumerate(pair):
                    opart[r, half, i * HD:(i + 1) * HD] = mixed[:, n * ROWS:(n + 1) * ROWS]

    def turn_values(r):
        vt[:, r * ROWS:(r + 1) * ROWS] = vbuf[r].T

    def o_copy(d, t, half):
        r = 4 - t if d == 0 else 4 + t
        dev = zp if d == 0 else zm
        return (rcopy(opart.at[r, half], oin.at[d, t, half], o_s.at[d, t, half], o_r.at[d, t, half], dev),
                rcopy(stats.at[r, half], sin.at[d, t, half], os_s.at[d, t, half], os_r.at[d, t, half], dev))

    o_copies = [[{h: o_copy(d, t, h) for h in ((0, 1) if t else (d,))} for t in range(4)] for d in range(2)]

    def go_o(d, t, half):
        for copy in o_copies[d][t][half]:
            go(copy)

    def take_o(d, t, half):
        for copy in o_copies[d][t][half]:
            take(copy)

    forward_q(0, 0)
    forward_q(0, 1)
    forward_q(1, 0)
    take(kv_copies[0])
    go(kv_copies[4])
    forward_q(1, 1)
    take(kv_copies[3])
    go(kv_copies[5])
    take(kv_copies[1])
    take(kv_copies[2])
    for r in (0, 1, 3):
        turn_values(r)
    sum_encoder()
    gather_out()
    forward_q(2, 0)
    forward_q(2, 1)
    for n in (4, 5):
        take(kv_copies[n])
    turn_values(2)
    attend((5, 3))
    forward_q(3, 0)
    forward_q(3, 1)
    attend((4, 0))
    for d in range(2):
        go_o(d, 0, d)
    for d in range(2):
        go_o(d, 1, 1 - d)
    send_rows()
    attend((6, 2))

    def merge(r, d, t, half):
        mine, other = stats[r, half], sin[d, t, half]
        for i in range(3):
            m0, m1 = mine[i:i + 1], other[i:i + 1]
            best = jnp.maximum(m0, m1)
            f0, f1 = jnp.exp2(m0 - best), jnp.exp2(m1 - best)
            rows = slice(i * HD, (i + 1) * HD)
            mixed = opart[r, half, rows].astype(F32) * f0 + oin[d, t, half, rows].astype(F32) * f1
            opart[r, half, rows] = mixed.astype(BF16)
            stats[r, half, i:i + 1] = best
            stats[r, half, 3 + i:4 + i] = mine[3 + i:4 + i] * f0 + other[3 + i:4 + i] * f1

    for t in (1, 2, 3):
        if t == 2:
            attend((7, 1))
        for turn in range(2):
            for d in range(2):
                half = d if turn else 1 - d
                if t == 1 and not turn:
                    continue
                take_o(d, t - 1, half)
                merge(4 - t if d == 0 else 4 + t, d, t - 1, half)
                go_o(d, t, half)
        if t == 1:
            relay_out()
    for r in (1, 2, 3):
        take(row_ys[NY - r])
    for n in range(NZ):
        aturn[n] = arecv[:, n].reshape(NY * 8, CH).astype(BF16)
    alast[pl.ds(z, 1)] = aturn[pl.ds(z, 1)]
    for r in (4, 3, 5, 2, 6, 1, 7):
        go(row_zs[r])
    for half in range(2):
        for d in range(2):
            take_o(d, 3, half)
            merge(0, d, 3, half)
    local[6].wait()
    for h in range(HEADS):
        half, i = h // 3, h % 3
        cols = slice(h * HD, (h + 1) * HD)
        attn = opart[0, half, i * HD:(i + 1) * HD].astype(F32) / stats[0, half, 3 + i:4 + i]
        attn = attn.T.astype(BF16).astype(F32)
        hgrp[sec, y, :, cols] = (resv[:, cols].astype(F32) + attn).astype(BF16)

    local[7].wait()
    hidden = hgrp[sec, y]
    f_copies = []
    for c in range(2):
        cols = slice(c * 1024, (c + 1) * 1024)
        fpart[:, :, cols] = dot(hidden, pin[:, cols]).astype(BF16).reshape(NX, 32, 1024)
        f_copies.append(x_copies(
            2 + c, lambda r: fpart.at[lax.rem(x + r, NX), :, cols], lambda r: frecv.at[r, :, cols]))
        for r in (2, 1, 3):
            go(f_copies[c][r])
    for n in range(2):
        take(relays[n])
    go(pc_copies[2])
    column = iota((NSEQ, CAP), 1)
    e_of = ((column >> 3) & (NY - 1)) * NZ + (column >> 5)
    device = iota((NSEQ, CAP), 0)
    counts8 = jnp.broadcast_to(counts, (8, NSEQ)).astype(BF16)
    start = dot(counts8, jnp.where(device < e_of, 1.0, 0.0).astype(BF16))[0:1]
    count = dot(counts8, jnp.where(device == e_of, 1.0, 0.0).astype(BF16))[0:1]
    low = start + ((iota((1, CAP), 1) & 7) * NSEQ).astype(F32)
    high = jnp.minimum(low + float(NSEQ), start + count)
    place = (iota((ROWS, CAP), 0) * NSEQ + seq).astype(F32)
    chosen = jnp.where((place >= low) & (place < high), 1.0, 0.0).astype(BF16)

    for c in range(2):
        cols = slice(c * 1024, (c + 1) * 1024)
        for r in (1, 2, 3):
            take(f_copies[c][NX - r])
        value = fpart[x, :, cols].astype(F32)
        for r in (1, 2, 3):
            value = value + frecv[r, :, cols].astype(F32)
        first[:, cols] = value
        act_rows[:, cols] = (value * jax.nn.sigmoid(value)).astype(BF16)
    act = act_rows[...]
    act_pieces = group_copies(0, lambda a, b: apiece.at[a, b], agrp.at[x, sec, y])
    for a in range(2):
        for b in range(NY):
            apiece[a, b] = act[:, (a * NY + b) * 256:(a * NY + b + 1) * 256]
    for copy in act_pieces:
        go(copy)
    agrp[x, sec, y] = apiece[sec, y]
    h_copies = y_copies(0, lambda: hgrp.at[sec, y])
    for r in (2, 1, 3):
        go(h_copies[r])
    for r in range(1, NZ):
        take(row_zs[NZ - r])
    tsend[...] = dot(chosen, alast[...].reshape(CAP, CH)).astype(BF16).reshape(NX, 32, CH)
    t_copies = x_copies(5, lambda r: tsend.at[lax.rem(x + r, NX)], lambda r: tgt.at[r])
    for r in (2, 1, 3):
        go(t_copies[r])
    tgt[0] = tsend[x]
    column_weight[...] = jnp.broadcast_to(aw_ref[...], (ROWS, ROWS)).T
    take(pc_copies[1])
    wide = 2 * CH
    second[:, 0:wide] = dot(act, pfull[:, 0:wide])
    for copy in act_pieces:
        take(copy)
    act_copies = x_copies(4, lambda r: agrp.at[x], lambda r: agrp.at[x])
    for r in (2, 1, 3):
        go(act_copies[r])
    take(pc_copies[3])
    take(pc_copies[2])
    second[:, wide:ENC_D] = dot(act, pfull[:, wide:ENC_D])
    for r in (1, 2, 3):
        take(t_copies[NX - r])
    inner = square_z = square_f = 0.0
    for r in range(NX):
        tf = tgt[r].astype(F32)
        value = second[:, r * CH:(r + 1) * CH]
        inner = inner + jnp.sum(value * tf, axis=1, keepdims=True)
        square_z = square_z + jnp.sum(value * value, axis=1, keepdims=True)
        square_f = square_f + jnp.sum(tf * tf, axis=1, keepdims=True)
    norm_z = jnp.sqrt(square_z + 1e-6)
    norm_f = jnp.sqrt(square_f + 1e-6)
    aligned = inner / (norm_z * norm_f)
    weight = column_weight[pl.ds(pl.multiple_of(x * 32, 32), 32), 0:1]
    by_target = -weight / (norm_z * norm_f)
    by_second = weight * aligned / (norm_z * norm_z)
    b_copies = x_copies(6, lambda r: bsend.at[r], lambda r: bgrp.at[sec, y, x])
    for r in (2, 1, 3, 0):
        bsend[r] = (by_target * tgt[r].astype(F32) + by_second * second[:, r * CH:(r + 1) * CH]).astype(BF16)
        if r:
            go(b_copies[r])
    bgrp[sec, y, x] = bsend[0]
    alall[x] = jnp.broadcast_to(aligned, (32, HD))
    l_copies = x_copies(7, lambda r: alall.at[x], lambda r: alall.at[x])
    for r in (2, 1, 3):
        go(l_copies[r])
    upstream = dot(jnp.concatenate([bsend[r] for r in range(NX)], axis=1), pfull[...], 1, 1)
    value = first[...]
    sig = jax.nn.sigmoid(value)
    dfirst = (upstream * sig * (1.0 + value * (1.0 - sig))).astype(BF16)
    d_pieces = group_copies(1, lambda a, b: dpiece.at[:, a, b], dgrp.at[:, x, sec, y])
    place = iota((CAP, CAP), 1)
    origin = ((2 * ((place >> 5) & 3) + (place >> 7)) << 5) + (place & 31)
    order = jnp.where(iota((CAP, CAP), 0) == origin, 1.0, 0.0).astype(BF16)
    for a in range(2):
        for b in range(NY):
            columns = dot(dfirst[:, (a * NY + b) * CAP:(a * NY + b + 1) * CAP], order).astype(BF16)
            for half in range(2):
                dpiece[half, a, b] = columns[:, half * HD:(half + 1) * HD]
    for copy in d_pieces:
        go(copy)
    for half in range(2):
        dgrp[half, x, sec, y] = dpiece[half, sec, y]
    for copy in d_pieces:
        take(copy)
    d_copies = []
    for half in range(2):
        d_copies.append(x_copies(8 + 2 * half, lambda r: dgrp.at[half, x], lambda r: dgrp.at[half, x]))
        for r in (2, 1, 3):
            go(d_copies[half][r])
    for r in (1, 2, 3):
        take(b_copies[NX - r])
    back_copies = y_copies(1, lambda: bgrp.at[sec, y])
    for r in (2, 1, 3):
        go(back_copies[r])
    for r in (1, 2, 3):
        take(h_copies[NY - r])
    hidden_core = core_copy(0, hgrp.at[sec])
    go(hidden_core)
    for r in (1, 2, 3):
        take(l_copies[NX - r])
    al_ref[...] = alall[...].reshape(ROWS, HD).T[0:1]
    for r in (1, 2, 3):
        take(back_copies[NY - r])
    back_core = core_copy(1, bgrp.at[sec])
    go(back_core)
    for r in (1, 2, 3):
        take(act_copies[NX - r])
    take(back_core)

    def go_copy(r):
        peer = lax.rem(z + r, NZ)
        return rcopy(go_z.at[peer], go_in.at[NZ - r], gz_s.at[r - 1], gz_r.at[NZ - r - 1], {"seq": y * NZ + peer})

    go_copies = {r: go_copy(r) for r in range(1, NZ)}
    value = 0.0
    for b in range(NX):
        value = value + dot(agrp[b].reshape(CAP, CAP), bgrp[:, :, b].reshape(CAP, CH), 0, 0)
    go_z[...] = value.astype(BF16).reshape(NZ, 32, CH)
    for r in (4, 3, 5, 2, 6, 1, 7):
        go(go_copies[r])
    take(hidden_core)

    def gi_copy(peer, mine):
        return rcopy(gi_z.at[lax.rem(peer, 2), peer // 2], gi_in.at[mine], gi_s.at[peer], gi_r.at[mine],
                     {"seq": y * NZ + peer})

    for half in range(2):
        for r in (1, 2, 3):
            take(d_copies[half][NX - r])
        value = 0.0
        for b in range(NX):
            rows = hgrp[:, :, b * 32:(b + 1) * 32].reshape(CAP, WIDTH)
            value = value + dot(dgrp[half, b].reshape(CAP, HD), rows, 0, 0)
        gi_z[half] = value.astype(BF16).reshape(4, 32, WIDTH)
        odd = lax.rem(z + half, 2)
        for m in (2, 1, 3):
            gi_copy(lax.rem(z + odd + 2 * m, NZ), z).start()

        @pl.when(odd == 1)
        def _():
            gi_copy(lax.rem(z + 1, NZ), z).start()

    for r in range(1, NZ):
        take(go_copies[NZ - r])
    value = go_z[z].astype(F32)
    for r in range(1, NZ):
        value = value + go_in[r].astype(F32)
    go_ref[...] = value
    value = gi_z[lax.rem(z, 2), z // 2].astype(F32)
    for r in range(1, NZ):
        peer = lax.rem(z + r, NZ)
        gi_copy(z, peer).wait_recv()
        value = value + gi_in[peer].astype(F32)
    gi_ref[...] = value
    for r in range(1, NZ):
        gi_copy(lax.rem(z + r, NZ), z).wait_send()

    for copy in pending:
        copy.wait_send()


def body(
    queries, keys, values, residual, segment_ids, enc_counts, enc_hidden, enc_down, enc_resid,
    layer_scale, norm_gain, norm_bias, proj_in, proj_out, align_weight,
):
    anywhere = pl.BlockSpec(memory_space=pl.ANY)
    vmem = pl.BlockSpec(memory_space=pltpu.VMEM)
    V, D = pltpu.VMEM, pltpu.SemaphoreType.DMA
    scratch = [
        V((NZ, ROWS, WIDTH), BF16), V((NY, ROWS, WIDTH), BF16), V((NY, ROWS, WIDTH), BF16),
        V((WIDTH, NY * ROWS), BF16), V((NY, ROWS, HD), BF16), V((ROWS, WIDTH), BF16),
        V((CAP, FF), BF16), V((FF, ENC_D), BF16), V((CAP, CH), BF16),
        V((WIDTH, PROJ), BF16), V((PROJ, ENC_D), BF16),
        V((NZ, 2, HALF, HD), BF16), V((NZ, 2, 8, HD), F32),
        V((2, 4, 2, HALF, HD), BF16), V((2, 4, 2, 8, HD), F32),
        V((NX, CAP, CH), BF16), V((NX, CAP, CH), BF16), V((CAP, CH), F32),
        V((8, CAP), F32), V((NX, 8, CAP), F32),
        V((NY, NZ, 8, CH), F32), V((NY, NZ, 8, CH), F32), V((NZ, 32, CH), BF16), V((NZ, 32, CH), BF16),
        V((NX, 32, CH), BF16), V((NX, 32, CH), BF16),
        V((2, NY, ROWS, WIDTH), BF16), V((NX, 32, PROJ), BF16), V((NX, 32, PROJ), BF16), V((32, PROJ), F32),
        V((32, PROJ), BF16), V((32, ENC_D), F32), V((NX, 32, CH), BF16), V((2, NY, NX, 32, CH), BF16),
        V((NX, 32, HD), F32), V((ROWS, ROWS), F32),
        V((2, NY, 32, 256), BF16), V((NX, 2, NY, 32, 256), BF16),
        V((2, 2, NY, 32, HD), BF16), V((2, NX, 2, NY, 32, HD), BF16),
        V((NZ, 32, CH), BF16), V((NZ, 32, CH), BF16), V((2, 4, 32, WIDTH), BF16), V((NZ, 32, WIDTH), BF16),
        V((2, HD, HD), F32),
    ]
    scratch += [
        D((9,)), D((2, 4, 2)), D((2, 4, 2)), D((6,)), D((6,)),
        D((2, 4, 2)), D((2, 4, 2)), D((2, 4, 2)), D((2, 4, 2)),
        D((11, 3)), D((11, 3)), D((3,)), D((3,)), D((2,)), D((2,)), D((3,)), D((3,)), D((7,)), D((7,)),
        D((2,)), D((2,)), D((2, 3)), D((2, 3)), D((7,)), D((7,)), D((2, 8)), D((2, 8)), D((8,)), D((8,)),
    ]
    aligned, grad_in_t, grad_out = pl.pallas_call(
        kernel,
        out_shape=(
            jax.ShapeDtypeStruct((1, ROWS), F32),
            jax.ShapeDtypeStruct((32, WIDTH), F32),
            jax.ShapeDtypeStruct((32, CH), F32),
        ),
        in_specs=[anywhere] * 4 + [vmem] * 2 + [anywhere] * 3 + [vmem] * 3 + [anywhere] * 2 + [vmem],
        out_specs=(vmem, vmem, vmem),
        scratch_shapes=scratch,
        compiler_params=pltpu.CompilerParams(
            collective_id=0, has_side_effects=True, vmem_limit_bytes=56 * 1024 * 1024
        ),
        name="align",
    )(
        queries, keys, values, residual, segment_ids, enc_counts, enc_hidden, enc_down, enc_resid,
        layer_scale.reshape(-1, HD), norm_gain.reshape(-1, HD), norm_bias.reshape(-1, HD),
        proj_in, proj_out, align_weight.reshape(1, -1),
    )

    def hand_on(a, b, c, a_out, b_out, c_out):
        a_out[...] = a[...]
        b_out[...] = b[...]
        c_out[...] = c[...]

    aligned, grad_in_t, grad_out = pl.pallas_call(
        hand_on,
        out_shape=tuple(jax.ShapeDtypeStruct(v.shape, F32) for v in (aligned, grad_in_t, grad_out)),
        in_specs=[vmem] * 3,
        out_specs=(vmem, vmem, vmem),
        name="hand_on",
    )(aligned, grad_in_t, grad_out)
    return aligned.reshape(-1), grad_in_t, grad_out


def solution(mesh):
    return jax.shard_map(
        body,
        mesh=mesh,
        in_specs=(
            P(("section", "seq"), "mp"),
            P(("section", "seq"), "mp"),
            P(("section", "seq"), "mp"),
            P(("section", "seq"), "mp"),
            P("section", None),
            P("section", None),
            P(("section", "seq"), "mp"),
            P("mp", None),
            P(("section", "seq"), "mp"),
            P(),
            P(),
            P(),
            P("mp", None),
            P(None, "mp"),
            P(("section", "seq")),
        ),
        out_specs=(P(("section", "seq")), P(("section", "seq"), "mp"), P(("section", "seq"), "mp")),
        check_vma=False,
    )
```

```python
import math

import jax
import jax.numpy as jnp
from jax import lax
from jax.experimental import pallas as pl
from jax.experimental.pallas import tpu as pltpu
from jax.sharding import PartitionSpec as P

MESH = pl.DeviceIdType.MESH
F32, BF16, I32 = jnp.float32, jnp.bfloat16, jnp.int32
HD = 128
ENC_D = 1536
NX, NY, NZ = 4, 4, 8
NSEQ = NY * NZ
ROWS = 128
CAP = 256
WIDTH = 768
HEADS = 6
HALF = 384
CH = 384
FF = 1024
PROJ = 2048
PART = 512
SAME = 8192.0
EXP_SCALE = math.log2(math.e) * HD ** (-0.5)


def rcopy(src, dst, send, recv, dev):
    return pltpu.make_async_remote_copy(
        src_ref=src, dst_ref=dst, send_sem=send, recv_sem=recv, device_id=dev, device_id_type=MESH
    )


def iota(shape, dim):
    return lax.broadcasted_iota(I32, shape, dim)


def dot(a, b, ca=1, cb=0):
    return lax.dot_general(a, b, (((ca,), (cb,)), ((), ())), preferred_element_type=F32)


def kernel(
    q_hbm, k_hbm, v_hbm, res_hbm, seg_ref, cnt_ref, eh_hbm, ed_hbm, er_hbm, ls_ref, gain_ref, bias_ref,
    pin_hbm, pout_hbm, aw_ref,
    al_ref, gi_ref, go_ref,
    qbuf, kbuf, vbuf, vt, ko, resv, ehv, edv, erv, pin, pfull,
    opart, stats, oin, sin,
    esend, erecv, share, estat, estat_in, packed, arecv, aturn, alast, tsend, tgt,
    hgrp, fpart, frecv, first, act_rows, second, bsend, bgrp, alall, column_weight,
    apiece, agrp, dpiece, dgrp, go_z, go_in, gi_z, gi_in, segrow,
    lsem, q_s, q_r, kv_s, kv_r, o_s, o_r, os_s, os_r, x_s, x_r, pc_s, pc_r, pr_s, pr_r, ay_s, ay_r, az_s, az_r,
    gx_s, gx_r, gy_s, gy_r, gz_s, gz_r, gg_s, gg_r, gi_s, gi_r,
):
    sec = lax.axis_index("section")
    seq = lax.axis_index("seq")
    x = lax.axis_index("mp")
    y = seq // NZ
    z = lax.rem(seq, NZ)
    zp = {"seq": y * NZ + lax.rem(z + 1, NZ)}
    zm = {"seq": y * NZ + lax.rem(z + NZ - 1, NZ)}
    yp = {"seq": lax.rem(y + 1, NY) * NZ + z}
    ym = {"seq": lax.rem(y + NY - 1, NY) * NZ + z}
    pending = []

    def go(copy):
        copy.start()
        pending.append(copy)
        return copy

    def take(copy):
        copy.wait_recv()

    local = []
    for n, (src, dst) in enumerate((
        (q_hbm, qbuf.at[0]), (k_hbm, kbuf.at[0]), (v_hbm, vbuf.at[0]), (eh_hbm, ehv), (ed_hbm, edv),
        (er_hbm, erv), (res_hbm, resv), (pin_hbm, pin), (pout_hbm, pfull.at[:, pl.ds(0, CH)]),
    )):
        copy = pltpu.make_async_copy(src, dst, lsem.at[n])
        local.append(copy)

    def fetch(first, last):
        for n in range(first, last):
            local[n].start()

    fetch(0, 3)

    barrier = pltpu.get_barrier_semaphore()

    greeted = [{"seq": y * NZ + lax.rem(z + r, NZ)} for r in range(1, NZ)]
    greeted += [{"seq": lax.rem(y + r, NY) * NZ + z} for r in range(1, NY)]
    greeted += [{"mp": lax.rem(x + r, NX)} for r in range(1, NX)]
    greeted += [{"section": 1 - sec, "seq": lax.rem(y + r, NY) * NZ + z} for r in range(NY)]
    for device in greeted:
        pl.semaphore_signal(barrier, inc=1, device_id=device, device_id_type=MESH)
    pl.semaphore_wait(barrier, len(greeted))

    def q_copy(d, t, half):
        cols = pl.ds(half * HALF, HALF)
        src = qbuf.at[(8 - t) % 8 if d == 0 else t, :, cols]
        dst = qbuf.at[7 - t if d == 0 else t + 1, :, cols]
        return rcopy(src, dst, q_s.at[d, t, half], q_r.at[d, t, half], zp if d == 0 else zm)

    def kv_copy(n):
        src, dst, dev = (
            (kbuf.at[0], kbuf.at[3], yp), (kbuf.at[0], kbuf.at[1], ym),
            (vbuf.at[0], vbuf.at[3], yp), (vbuf.at[0], vbuf.at[1], ym),
            (kbuf.at[3], kbuf.at[2], yp), (vbuf.at[1], vbuf.at[2], ym),
        )[n]
        return rcopy(src, dst, kv_s.at[n], kv_r.at[n], dev)

    q_copies = [[{h: q_copy(d, t, h) for h in ((0, 1) if t < 3 else (d,))} for t in range(4)] for d in range(2)]
    kv_copies = [kv_copy(n) for n in range(6)]
    for n in range(3):
        local[n].wait()
    fetch(3, 5)
    for half in range(2):
        for d in range(2):
            go(q_copies[d][0][half])
    go(kv_copies[0])
    go(kv_copies[1])
    go(kv_copies[2])
    go(kv_copies[3])

    def x_copies(phase, src_of, dst_of, which=(1, 2, 3)):
        return {
            r: rcopy(src_of(r), dst_of(NX - r), x_s.at[phase, r - 1], x_r.at[phase, NX - r - 1],
                     {"mp": lax.rem(x + r, NX)})
            for r in which
        }

    def y_copies(n, ref_of):
        return {
            r: rcopy(ref_of(), ref_of(), gy_s.at[n, r - 1], gy_r.at[n, NY - r - 1],
                     {"seq": lax.rem(y + r, NY) * NZ + z})
            for r in (1, 2, 3)
        }

    def core_copy(n, ref):
        return rcopy(ref, ref, gx_s.at[n], gx_r.at[n], {"section": 1 - sec})

    def group_copies(n, piece_of, slot):
        copies = []
        for ds in range(2):
            for r in range(NY):
                if ds or r:
                    to_sec, to_y = lax.rem(sec + ds, 2), lax.rem(y + r, NY)
                    copies.append(rcopy(
                        piece_of(to_sec, to_y), slot,
                        gg_s.at[n, ds * NY + r], gg_r.at[n, ds * NY + (NY - r) % NY],
                        {"section": to_sec, "seq": to_y * NZ + z}))
        return copies

    local[3].wait()
    local[4].wait()
    enc_copies = x_copies(0, lambda r: esend.at[r], lambda r: erecv.at[r])
    for r in (2, 1, 3, 0):
        cols = pl.ds(pl.multiple_of(lax.rem(x + r, NX) * CH, CH), CH)
        esend[r] = dot(ehv[...], edv[:, cols]).astype(BF16)
        if r:
            go(enc_copies[r])

    fetch(5, 9)
    core_rows = pl.ds(pl.multiple_of(sec * (PROJ // 2), PROJ // 2), PROJ // 2)
    def out_block(rows, r):
        return pfull.at[rows, pl.ds(r * CH, CH)]

    p_copies = x_copies(9, lambda r: out_block(core_rows, 0), lambda r: out_block(core_rows, r), (1, 3))

    def relay(n):
        part = pl.ds(pl.multiple_of(sec * (PROJ // 2) + n * PART, PART), PART)
        return rcopy(out_block(part, (3, 1)[n]), out_block(part, 2), pr_s.at[n], pr_r.at[n],
                     {"mp": lax.rem(x + (1, 3)[n], NX)})

    relays = [relay(0), relay(1)]
    pc_copies = {r: rcopy(out_block(core_rows, r), out_block(core_rows, r), pc_s.at[r - 1], pc_r.at[r - 1],
                          {"section": 1 - sec}) for r in (1, 2, 3)}
    ids = iota((16, NSEQ * ROWS), 0)
    seg = seg_ref[...]
    below = jnp.sum(jnp.where(seg < ids, 1.0, 0.0), axis=1, keepdims=True)
    upto = jnp.sum(jnp.where(seg <= ids, 1.0, 0.0), axis=1, keepdims=True)
    lane = iota((16, HD), 1)
    tail = jnp.full((HD - 16, HD), 1e9, F32)
    segrow[0] = jnp.concatenate([jnp.broadcast_to(below, lane.shape), tail], axis=0).T
    segrow[1] = jnp.concatenate([jnp.broadcast_to(upto, lane.shape), tail], axis=0).T

    def image_columns(device):
        place = (iota((ROWS, HD), 0) * NSEQ + device).astype(F32)
        return (place >= segrow[0]) & (place < segrow[1])

    for r in range(NY):
        device = lax.rem(y + r, NY) * NZ + z
        ko[r] = jnp.where(image_columns(device), SAME, 0.0).astype(BF16)

    def forward_q(t, half):
        for d in range(2):
            if half in q_copies[d][t]:
                take(q_copies[d][t][half])
            if t < 3 and half in q_copies[d][t + 1]:
                go(q_copies[d][t + 1][half])

    def own(ref):
        return jnp.concatenate([ref[pl.ds(3 * x + i, 1), :] for i in range(3)], axis=1)

    stat_copies = x_copies(1, lambda r: estat, lambda r: estat_in.at[r])
    pad = jnp.zeros((HD - 8, HD), F32)
    row8 = iota((8, HD), 0)
    counts = cnt_ref[...].astype(F32)

    def row_y(r):
        peer = lax.rem(y + r, NY)
        return rcopy(packed.at[peer], arecv.at[y], ay_s.at[r - 1], ay_r.at[NY - r - 1], {"seq": peer * NZ + z})

    def row_z(r):
        peer = lax.rem(z + r, NZ)
        return rcopy(aturn.at[peer], alast.at[z], az_s.at[r - 1], az_r.at[NZ - r - 1], {"seq": y * NZ + peer})

    row_ys = {r: row_y(r) for r in range(1, NY)}
    row_zs = {r: row_z(r) for r in range(1, NZ)}
    def sum_encoder():
        local[5].wait()
        for r in (1, 2, 3):
            take(enc_copies[NX - r])
        enc = esend[0].astype(F32)
        for r in (1, 2, 3):
            enc = enc + erecv[r].astype(F32)
        enc = erv[...].astype(F32) + own(ls_ref) * enc
        share[...] = enc
        lane = iota((CAP, HD), 1)
        total = jnp.sum(enc, axis=1, keepdims=True)
        square = jnp.sum(enc * enc, axis=1, keepdims=True)
        packed_stat = jnp.where(lane == 0, total, jnp.where(lane == 1, square, 0.0))
        for b in range(2):
            estat[:, b * HD:(b + 1) * HD] = packed_stat[b * HD:(b + 1) * HD].T[0:8]
        for r in (2, 1, 3):
            go(stat_copies[r])

    def gather_out():
        local[8].wait()
        for r in (1, 3):
            go(p_copies[r])

    def relay_out():
        for n in range(2):
            take(p_copies[(1, 3)[n]])
            go(relays[n])
            go(pc_copies[(3, 1)[n]])


    def send_rows():
        for r in (1, 2, 3):
            take(stat_copies[NX - r])
        both = estat[...]
        for r in (1, 2, 3):
            both = both + estat_in[r]
        mean = both[0:1] * (1.0 / ENC_D)
        scale = lax.rsqrt(both[1:2] * (1.0 / ENC_D) - mean * mean + 1e-6)
        gain = own(gain_ref)
        bias = own(bias_ref)
        parts = []
        for b in range(2):
            cut = slice(b * HD, (b + 1) * HD)
            rows = jnp.where(row8 == 0, mean[:, cut], jnp.where(row8 == 1, scale[:, cut], 0.0))
            cols = jnp.concatenate([rows, pad], axis=0).T
            parts.append((((share[cut] - cols[:, 0:1]) * cols[:, 1:2]) * gain + bias).astype(BF16))
        feature = jnp.concatenate(parts, axis=0)
        before = jnp.sum(jnp.where(iota((1, NSEQ), 1) < seq, counts, 0.0), axis=1, keepdims=True).astype(I32)
        row = iota((CAP, CAP), 0)
        wanted = (row & 7) * NSEQ + (((row >> 3) - before) & (NSEQ - 1))
        permutation = jnp.where(iota((CAP, CAP), 1) == wanted, 1.0, 0.0).astype(BF16)
        packed[...] = dot(permutation, feature).reshape(NY, NZ, 8, CH)

        for r in (2, 1, 3):
            go(row_ys[r])
        arecv[pl.ds(y, 1)] = packed[pl.ds(y, 1)]

    def attend(pair):
        keys_image = ko[...].reshape(NY * ROWS, HD)
        image = jnp.concatenate(
            [jnp.where(image_columns(y * NZ + lax.rem(z + r, NZ)), 1.0, 0.0).astype(BF16) for r in pair], axis=0)
        scores, probs = {}, {}
        for step in range(HEADS + 2):
            if step < HEADS:
                cols = slice(step * HD, (step + 1) * HD)
                keys = jnp.concatenate([kbuf[:, :, cols].reshape(NY * ROWS, HD), keys_image], axis=1)
                rows = jnp.concatenate([qbuf[r, :, cols] for r in pair], axis=0)
                scores[step] = dot(keys, jnp.concatenate([rows, image], axis=1), 1, 1)
            if 1 <= step <= HEADS:
                h = step - 1
                score = scores.pop(h)
                best = jnp.max(score, axis=0, keepdims=True)
                prob = jnp.exp2((score - best) * EXP_SCALE)
                total = jnp.sum(prob, axis=0, keepdims=True)
                half, i = h // 3, h % 3
                for n, r in enumerate(pair):
                    cut = slice(n * ROWS, (n + 1) * ROWS)
                    stats[r, half, i:i + 1] = best[:, cut] * EXP_SCALE
                    stats[r, half, 3 + i:4 + i] = total[:, cut]
                probs[h] = prob.astype(BF16)
            if step >= 2:
                h = step - 2
                half, i = h // 3, h % 3
                mixed = dot(vt[h * HD:(h + 1) * HD], probs.pop(h)).astype(BF16)
                for n, r in enumerate(pair):
                    opart[r, half, i * HD:(i + 1) * HD] = mixed[:, n * ROWS:(n + 1) * ROWS]

    def turn_values(r):
        vt[:, r * ROWS:(r + 1) * ROWS] = vbuf[r].T

    def o_copy(d, t, half):
        r = 4 - t if d == 0 else 4 + t
        dev = zp if d == 0 else zm
        return (rcopy(opart.at[r, half], oin.at[d, t, half], o_s.at[d, t, half], o_r.at[d, t, half], dev),
                rcopy(stats.at[r, half], sin.at[d, t, half], os_s.at[d, t, half], os_r.at[d, t, half], dev))

    o_copies = [[{h: o_copy(d, t, h) for h in ((0, 1) if t else (d,))} for t in range(4)] for d in range(2)]

    def go_o(d, t, half):
        for copy in o_copies[d][t][half]:
            go(copy)

    def take_o(d, t, half):
        for copy in o_copies[d][t][half]:
            take(copy)

    forward_q(0, 0)
    forward_q(0, 1)
    forward_q(1, 0)
    take(kv_copies[0])
    go(kv_copies[4])
    forward_q(1, 1)
    take(kv_copies[3])
    go(kv_copies[5])
    take(kv_copies[1])
    take(kv_copies[2])
    for r in (0, 1, 3):
        turn_values(r)
    forward_q(2, 0)
    sum_encoder()
    gather_out()
    forward_q(2, 1)
    for n in (4, 5):
        take(kv_copies[n])
    turn_values(2)
    attend((5, 3))
    forward_q(3, 0)
    forward_q(3, 1)
    attend((4, 0))
    for d in range(2):
        go_o(d, 0, d)
    for d in range(2):
        go_o(d, 1, 1 - d)
    send_rows()
    attend((6, 2))

    def merge(r, d, t, half):
        mine, other = stats[r, half], sin[d, t, half]
        for i in range(3):
            m0, m1 = mine[i:i + 1], other[i:i + 1]
            best = jnp.maximum(m0, m1)
            f0, f1 = jnp.exp2(m0 - best), jnp.exp2(m1 - best)
            rows = slice(i * HD, (i + 1) * HD)
            mixed = opart[r, half, rows].astype(F32) * f0 + oin[d, t, half, rows].astype(F32) * f1
            opart[r, half, rows] = mixed.astype(BF16)
            stats[r, half, i:i + 1] = best
            stats[r, half, 3 + i:4 + i] = mine[3 + i:4 + i] * f0 + other[3 + i:4 + i] * f1

    for t in (1, 2, 3):
        if t == 2:
            attend((7, 1))
        for turn in range(2):
            for d in range(2):
                half = d if turn else 1 - d
                if t == 1 and not turn:
                    continue
                take_o(d, t - 1, half)
                merge(4 - t if d == 0 else 4 + t, d, t - 1, half)
                go_o(d, t, half)
        if t == 3:
            relay_out()
    for r in (1, 2, 3):
        take(row_ys[NY - r])
    for n in range(NZ):
        aturn[n] = arecv[:, n].reshape(NY * 8, CH).astype(BF16)
    alast[pl.ds(z, 1)] = aturn[pl.ds(z, 1)]
    for r in (4, 3, 5, 2, 6, 1, 7):
        go(row_zs[r])
    for half in range(2):
        for d in range(2):
            take_o(d, 3, half)
            merge(0, d, 3, half)
    local[6].wait()
    for h in range(HEADS):
        half, i = h // 3, h % 3
        cols = slice(h * HD, (h + 1) * HD)
        attn = opart[0, half, i * HD:(i + 1) * HD].astype(F32) / stats[0, half, 3 + i:4 + i]
        attn = attn.T.astype(BF16).astype(F32)
        hgrp[sec, y, :, cols] = (resv[:, cols].astype(F32) + attn).astype(BF16)

    local[7].wait()
    hidden = hgrp[sec, y]
    f_copies = []
    for c in range(2):
        cols = slice(c * 1024, (c + 1) * 1024)
        fpart[:, :, cols] = dot(hidden, pin[:, cols]).astype(BF16).reshape(NX, 32, 1024)
        f_copies.append(x_copies(
            2 + c, lambda r: fpart.at[lax.rem(x + r, NX), :, cols], lambda r: frecv.at[r, :, cols]))
        for r in (2, 1, 3):
            go(f_copies[c][r])
    for n in range(2):
        take(relays[n])
    go(pc_copies[2])
    column = iota((NSEQ, CAP), 1)
    e_of = ((column >> 3) & (NY - 1)) * NZ + (column >> 5)
    device = iota((NSEQ, CAP), 0)
    counts8 = jnp.broadcast_to(counts, (8, NSEQ)).astype(BF16)
    start = dot(counts8, jnp.where(device < e_of, 1.0, 0.0).astype(BF16))[0:1]
    count = dot(counts8, jnp.where(device == e_of, 1.0, 0.0).astype(BF16))[0:1]
    low = start + ((iota((1, CAP), 1) & 7) * NSEQ).astype(F32)
    high = jnp.minimum(low + float(NSEQ), start + count)
    place = (iota((ROWS, CAP), 0) * NSEQ + seq).astype(F32)
    chosen = jnp.where((place >= low) & (place < high), 1.0, 0.0).astype(BF16)

    for c in range(2):
        cols = slice(c * 1024, (c + 1) * 1024)
        for r in (1, 2, 3):
            take(f_copies[c][NX - r])
        value = fpart[x, :, cols].astype(F32)
        for r in (1, 2, 3):
            value = value + frecv[r, :, cols].astype(F32)
        first[:, cols] = value
        act_rows[:, cols] = (value * jax.nn.sigmoid(value)).astype(BF16)
    act = act_rows[...]
    act_pieces = group_copies(0, lambda a, b: apiece.at[a, b], agrp.at[x, sec, y])
    for a in range(2):
        for b in range(NY):
            apiece[a, b] = act[:, (a * NY + b) * 256:(a * NY + b + 1) * 256]
    for copy in act_pieces:
        go(copy)
    agrp[x, sec, y] = apiece[sec, y]
    h_copies = y_copies(0, lambda: hgrp.at[sec, y])
    for r in (2, 1, 3):
        go(h_copies[r])
    for r in range(1, NZ):
        take(row_zs[NZ - r])
    tsend[...] = dot(chosen, alast[...].reshape(CAP, CH)).astype(BF16).reshape(NX, 32, CH)
    t_copies = x_copies(5, lambda r: tsend.at[lax.rem(x + r, NX)], lambda r: tgt.at[r])
    for r in (2, 1, 3):
        go(t_copies[r])
    tgt[0] = tsend[x]
    column_weight[...] = jnp.broadcast_to(aw_ref[...], (ROWS, ROWS)).T
    take(pc_copies[1])
    wide = 2 * CH
    second[:, 0:wide] = dot(act, pfull[:, 0:wide])
    for copy in act_pieces:
        take(copy)
    act_copies = x_copies(4, lambda r: agrp.at[x], lambda r: agrp.at[x])
    for r in (2, 1, 3):
        go(act_copies[r])
    take(pc_copies[3])
    take(pc_copies[2])
    second[:, wide:ENC_D] = dot(act, pfull[:, wide:ENC_D])
    for r in (1, 2, 3):
        take(t_copies[NX - r])
    inner = square_z = square_f = 0.0
    for r in range(NX):
        tf = tgt[r].astype(F32)
        value = second[:, r * CH:(r + 1) * CH]
        inner = inner + jnp.sum(value * tf, axis=1, keepdims=True)
        square_z = square_z + jnp.sum(value * value, axis=1, keepdims=True)
        square_f = square_f + jnp.sum(tf * tf, axis=1, keepdims=True)
    norm_z = jnp.sqrt(square_z + 1e-6)
    norm_f = jnp.sqrt(square_f + 1e-6)
    aligned = inner / (norm_z * norm_f)
    weight = column_weight[pl.ds(pl.multiple_of(x * 32, 32), 32), 0:1]
    by_target = -weight / (norm_z * norm_f)
    by_second = weight * aligned / (norm_z * norm_z)
    b_copies = x_copies(6, lambda r: bsend.at[r], lambda r: bgrp.at[sec, y, x])
    for r in (2, 1, 3, 0):
        bsend[r] = (by_target * tgt[r].astype(F32) + by_second * second[:, r * CH:(r + 1) * CH]).astype(BF16)
        if r:
            go(b_copies[r])
    bgrp[sec, y, x] = bsend[0]
    alall[x] = jnp.broadcast_to(aligned, (32, HD))
    l_copies = x_copies(7, lambda r: alall.at[x], lambda r: alall.at[x])
    for r in (2, 1, 3):
        go(l_copies[r])
    upstream = dot(jnp.concatenate([bsend[r] for r in range(NX)], axis=1), pfull[...], 1, 1)
    value = first[...]
    sig = jax.nn.sigmoid(value)
    dfirst = (upstream * sig * (1.0 + value * (1.0 - sig))).astype(BF16)
    d_pieces = group_copies(1, lambda a, b: dpiece.at[:, a, b], dgrp.at[:, x, sec, y])
    place = iota((CAP, CAP), 1)
    origin = ((2 * ((place >> 5) & 3) + (place >> 7)) << 5) + (place & 31)
    order = jnp.where(iota((CAP, CAP), 0) == origin, 1.0, 0.0).astype(BF16)
    for a in range(2):
        for b in range(NY):
            columns = dot(dfirst[:, (a * NY + b) * CAP:(a * NY + b + 1) * CAP], order).astype(BF16)
            for half in range(2):
                dpiece[half, a, b] = columns[:, half * HD:(half + 1) * HD]
    for copy in d_pieces:
        go(copy)
    for half in range(2):
        dgrp[half, x, sec, y] = dpiece[half, sec, y]
    for copy in d_pieces:
        take(copy)
    d_copies = []
    for half in range(2):
        d_copies.append(x_copies(8 + 2 * half, lambda r: dgrp.at[half, x], lambda r: dgrp.at[half, x]))
        for r in (2, 1, 3):
            go(d_copies[half][r])
    for r in (1, 2, 3):
        take(b_copies[NX - r])
    back_copies = y_copies(1, lambda: bgrp.at[sec, y])
    for r in (2, 1, 3):
        go(back_copies[r])
    for r in (1, 2, 3):
        take(h_copies[NY - r])
    hidden_core = core_copy(0, hgrp.at[sec])
    go(hidden_core)
    for r in (1, 2, 3):
        take(l_copies[NX - r])
    al_ref[...] = alall[...].reshape(ROWS, HD).T[0:1]
    for r in (1, 2, 3):
        take(back_copies[NY - r])
    back_core = core_copy(1, bgrp.at[sec])
    go(back_core)
    for r in (1, 2, 3):
        take(act_copies[NX - r])
    take(back_core)

    def go_copy(r):
        peer = lax.rem(z + r, NZ)
        return rcopy(go_z.at[peer], go_in.at[NZ - r], gz_s.at[r - 1], gz_r.at[NZ - r - 1], {"seq": y * NZ + peer})

    go_copies = {r: go_copy(r) for r in range(1, NZ)}
    value = 0.0
    for b in range(NX):
        value = value + dot(agrp[b].reshape(CAP, CAP), bgrp[:, :, b].reshape(CAP, CH), 0, 0)
    go_z[...] = value.astype(BF16).reshape(NZ, 32, CH)
    for r in (4, 3, 5, 2, 6, 1, 7):
        go(go_copies[r])
    take(hidden_core)

    def gi_copy(peer, mine):
        return rcopy(gi_z.at[lax.rem(peer, 2), peer // 2], gi_in.at[mine], gi_s.at[peer], gi_r.at[mine],
                     {"seq": y * NZ + peer})

    for half in range(2):
        for r in (1, 2, 3):
            take(d_copies[half][NX - r])
        value = 0.0
        for b in range(NX):
            rows = hgrp[:, :, b * 32:(b + 1) * 32].reshape(CAP, WIDTH)
            value = value + dot(dgrp[half, b].reshape(CAP, HD), rows, 0, 0)
        gi_z[half] = value.astype(BF16).reshape(4, 32, WIDTH)
        odd = lax.rem(z + half, 2)
        for m in (2, 1, 3):
            gi_copy(lax.rem(z + odd + 2 * m, NZ), z).start()

        @pl.when(odd == 1)
        def _():
            gi_copy(lax.rem(z + 1, NZ), z).start()

    for r in range(1, NZ):
        take(go_copies[NZ - r])
    value = go_z[z].astype(F32)
    for r in range(1, NZ):
        value = value + go_in[r].astype(F32)
    go_ref[...] = value
    value = gi_z[lax.rem(z, 2), z // 2].astype(F32)
    for r in range(1, NZ):
        peer = lax.rem(z + r, NZ)
        gi_copy(z, peer).wait_recv()
        value = value + gi_in[peer].astype(F32)
    gi_ref[...] = value
    for r in range(1, NZ):
        gi_copy(lax.rem(z + r, NZ), z).wait_send()

    for copy in pending:
        copy.wait_send()


def body(
    queries, keys, values, residual, segment_ids, enc_counts, enc_hidden, enc_down, enc_resid,
    layer_scale, norm_gain, norm_bias, proj_in, proj_out, align_weight,
):
    anywhere = pl.BlockSpec(memory_space=pl.ANY)
    vmem = pl.BlockSpec(memory_space=pltpu.VMEM)
    V, D = pltpu.VMEM, pltpu.SemaphoreType.DMA
    scratch = [
        V((NZ, ROWS, WIDTH), BF16), V((NY, ROWS, WIDTH), BF16), V((NY, ROWS, WIDTH), BF16),
        V((WIDTH, NY * ROWS), BF16), V((NY, ROWS, HD), BF16), V((ROWS, WIDTH), BF16),
        V((CAP, FF), BF16), V((FF, ENC_D), BF16), V((CAP, CH), BF16),
        V((WIDTH, PROJ), BF16), V((PROJ, ENC_D), BF16),
        V((NZ, 2, HALF, HD), BF16), V((NZ, 2, 8, HD), F32),
        V((2, 4, 2, HALF, HD), BF16), V((2, 4, 2, 8, HD), F32),
        V((NX, CAP, CH), BF16), V((NX, CAP, CH), BF16), V((CAP, CH), F32),
        V((8, CAP), F32), V((NX, 8, CAP), F32),
        V((NY, NZ, 8, CH), F32), V((NY, NZ, 8, CH), F32), V((NZ, 32, CH), BF16), V((NZ, 32, CH), BF16),
        V((NX, 32, CH), BF16), V((NX, 32, CH), BF16),
        V((2, NY, ROWS, WIDTH), BF16), V((NX, 32, PROJ), BF16), V((NX, 32, PROJ), BF16), V((32, PROJ), F32),
        V((32, PROJ), BF16), V((32, ENC_D), F32), V((NX, 32, CH), BF16), V((2, NY, NX, 32, CH), BF16),
        V((NX, 32, HD), F32), V((ROWS, ROWS), F32),
        V((2, NY, 32, 256), BF16), V((NX, 2, NY, 32, 256), BF16),
        V((2, 2, NY, 32, HD), BF16), V((2, NX, 2, NY, 32, HD), BF16),
        V((NZ, 32, CH), BF16), V((NZ, 32, CH), BF16), V((2, 4, 32, WIDTH), BF16), V((NZ, 32, WIDTH), BF16),
        V((2, HD, HD), F32),
    ]
    scratch += [
        D((9,)), D((2, 4, 2)), D((2, 4, 2)), D((6,)), D((6,)),
        D((2, 4, 2)), D((2, 4, 2)), D((2, 4, 2)), D((2, 4, 2)),
        D((11, 3)), D((11, 3)), D((3,)), D((3,)), D((2,)), D((2,)), D((3,)), D((3,)), D((7,)), D((7,)),
        D((2,)), D((2,)), D((2, 3)), D((2, 3)), D((7,)), D((7,)), D((2, 8)), D((2, 8)), D((8,)), D((8,)),
    ]
    aligned, grad_in_t, grad_out = pl.pallas_call(
        kernel,
        out_shape=(
            jax.ShapeDtypeStruct((1, ROWS), F32),
            jax.ShapeDtypeStruct((32, WIDTH), F32),
            jax.ShapeDtypeStruct((32, CH), F32),
        ),
        in_specs=[anywhere] * 4 + [vmem] * 2 + [anywhere] * 3 + [vmem] * 3 + [anywhere] * 2 + [vmem],
        out_specs=(vmem, vmem, vmem),
        scratch_shapes=scratch,
        compiler_params=pltpu.CompilerParams(
            collective_id=0, has_side_effects=True, vmem_limit_bytes=56 * 1024 * 1024
        ),
        name="align",
    )(
        queries, keys, values, residual, segment_ids, enc_counts, enc_hidden, enc_down, enc_resid,
        layer_scale.reshape(-1, HD), norm_gain.reshape(-1, HD), norm_bias.reshape(-1, HD),
        proj_in, proj_out, align_weight.reshape(1, -1),
    )

    def hand_on(a, b, c, a_out, b_out, c_out):
        a_out[...] = a[...]
        b_out[...] = b[...]
        c_out[...] = c[...]

    aligned, grad_in_t, grad_out = pl.pallas_call(
        hand_on,
        out_shape=tuple(jax.ShapeDtypeStruct(v.shape, F32) for v in (aligned, grad_in_t, grad_out)),
        in_specs=[vmem] * 3,
        out_specs=(vmem, vmem, vmem),
        name="hand_on",
    )(aligned, grad_in_t, grad_out)
    return aligned.reshape(-1), grad_in_t, grad_out


def solution(mesh):
    return jax.shard_map(
        body,
        mesh=mesh,
        in_specs=(
            P(("section", "seq"), "mp"),
            P(("section", "seq"), "mp"),
            P(("section", "seq"), "mp"),
            P(("section", "seq"), "mp"),
            P("section", None),
            P("section", None),
            P(("section", "seq"), "mp"),
            P("mp", None),
            P(("section", "seq"), "mp"),
            P(),
            P(),
            P(),
            P("mp", None),
            P(None, "mp"),
            P(("section", "seq")),
        ),
        out_specs=(P(("section", "seq")), P(("section", "seq"), "mp"), P(("section", "seq"), "mp")),
        check_vma=False,
    )
```
